128 devices in a mesh: seq: 32 (over y, z, core), head: 4 (over x).
Axes of the slice: x: 4, y: 4, z: 4, core: 2. Of those that a mesh axis runs over, the one named last changes fastest.
Arguments:
- queries: bfloat16 [16384, 32, 128], P('seq', 'head'), may hold values from -6 to 6
- key_vectors: bfloat16 [16384, 32, 128], P('seq', 'head'), may hold values from -6 to 6
- value_vectors: bfloat16 [16384, 32, 128], P('seq', 'head'), may hold values from -6 to 6
- doc_ids: int32 [16384], P('seq'), may hold values from 0 to 7, never falling along the last dimension, each value on 1 to 8192 neighbouring positions
- out_weight: bfloat16 [4096, 3072], P('head'), may hold values from -0.09375 to 0.09375
- grad_out: bfloat16 [16384, 3072], P('seq', 'head'), may hold values from -6 to 6
Outputs:
- layer_out: bfloat16 [16384, 3072], P('seq', 'head')
- grad_queries: bfloat16 [16384, 32, 128], P('seq', 'head')
- grad_keys: bfloat16 [16384, 32, 128], P('seq', 'head')
- grad_values: bfloat16 [16384, 32, 128], P('seq', 'head')
- grad_weight: float32 [4096, 3072], P('head', 'seq')
The draws below stay inside these ranges and needn't reach their ends.
Inputs may be any that keep to these rules, and one draw needn't show every extreme that they name: doc_ids never falls; each of the 8 documents has 1 to 8192 tokens and one has exactly 8192.
All inputs are finite; a program needn't handle non-finite values.
Results may differ from the reference program's by a relative error of at most 0.0063.
Values may be sent and summed in bfloat16 or wider, within the bound.
No kernel may reach another device: no remote copies, remote signals or barrier semaphores. Data moves between devices by JAX's collectives and lax.ppermute only.
A program may use at most 128 MiB of HBM per device.

```python
import math
import jax
import jax.numpy as jnp
import numpy as np
from jax import lax

DH = 128
HEADS = 32
DM = 3072
TOK_DEV = 512
TOKENS = 16384
HD = 4096
DOCS = 8
DOC_MOST = 8192


def steps_of(key, shape, shards, smallest, high):
    def one(position, blocks):
        heights = jax.random.uniform(jax.random.fold_in(jax.random.fold_in(key, 6), position), (blocks,), jnp.float32, smallest / len(shards), high / len(shards))
        return jnp.repeat(jnp.exp(heights), shape[position] // blocks).reshape((-1,) + (1,) * (len(shape) - position - 1))

    level = one(*shards[0])
    for cut in shards[1:]:
        level = level * one(*cut)
    return level


def length_profile(count, total, bound, slope):
    loads = [(1 << 20) // math.isqrt(grade ** slope) + 1 for grade in range(2, count + 1)]
    rest, counts = total - bound - (count - 1), [1] * (count - 1)
    while rest > 0:
        candidates = [i for i in range(count - 1) if counts[i] < bound]
        pool, left = sum([loads[i] for i in candidates]), rest
        for i in candidates:
            addition = min(bound - counts[i], max(1, left * loads[i] // pool), rest)
            counts[i] = counts[i] + addition
            rest = rest - addition
    return np.array([bound] + counts)


def ragged(stream_key, count, total, bound, lean):
    if count == 2:
        one = jax.random.randint(stream_key, (), max(1, total - bound), min(bound, total - 1) + 1)
        return jnp.stack([one, total - one])
    lengths = jnp.asarray(length_profile(count, total, bound, lean), jnp.int32)
    couples = (count - 1) // 2
    source_of, taker = lengths[1:1 + 2 * couples:2], lengths[2:2 + 2 * couples:2]
    margin = jnp.minimum(source_of - 1, bound - taker)
    shifted = jax.random.randint(jax.random.fold_in(stream_key, 1), (couples,), 0, 1 << 20) % (margin + 1)
    lengths = lengths.at[1:1 + 2 * couples:2].set(source_of - shifted).at[2:2 + 2 * couples:2].set(taker + shifted)
    return lengths[jax.random.permutation(jax.random.fold_in(stream_key, 2), count)]


def scatter_about(own_key, extent, scale, most, shards=(), held_as=jnp.bfloat16):
    entries = scale * jax.random.normal(own_key, extent, jnp.float32)
    if shards:
        entries = entries * steps_of(own_key, extent, shards, -0.22, 0.18)
    return jnp.clip(entries, -most, most).astype(held_as)


def setup_inputs(seed: int = 0) -> dict:
    seeds = jax.random.split(jax.random.key(seed), 7)
    queries = scatter_about(seeds[0], (TOKENS, HEADS, DH), 1.0, 6.0, ((0, 32), (1, 4)))
    key_vectors = scatter_about(seeds[1], (TOKENS, HEADS, DH), 1.0, 6.0, ((0, 32), (1, 4)))
    value_vectors = scatter_about(seeds[2], (TOKENS, HEADS, DH), 1.0, 6.0, ((0, 32), (1, 4)))
    doc_ids = jnp.searchsorted(jnp.cumsum(ragged(seeds[3], DOCS, TOKENS, DOC_MOST, 0)), jnp.arange(TOKENS), side="right").astype(jnp.int32)
    out_weight = scatter_about(seeds[4], (HD, DM), HD ** -0.5, 0.09375, ((0, 4),))
    grad_out = scatter_about(seeds[5], (TOKENS, DM), 1.0, 6.0, ((0, 32), (1, 4)))
    return {"queries": queries, "key_vectors": key_vectors, "value_vectors": value_vectors, "doc_ids": doc_ids, "out_weight": out_weight, "grad_out": grad_out}


def combine(earlier, later):
    same = (earlier[0] == later[0]).astype(jnp.float32)
    return (later[0], later[1] + same[0] * earlier[1])

def reference(queries, key_vectors, value_vectors, doc_ids, out_weight, grad_out):
    blocks = TOKENS // TOK_DEV
    query_blocks = queries.reshape(blocks, TOK_DEV, HEADS, DH)
    key_blocks = key_vectors.reshape(blocks, TOK_DEV, HEADS, DH)
    value_blocks = value_vectors.reshape(blocks, TOK_DEV, HEADS, DH)
    doc_blocks = doc_ids.astype(jnp.float32).reshape(blocks, TOK_DEV)
    causal = lax.broadcasted_iota(jnp.int32, (TOK_DEV, TOK_DEV), 0) >= lax.broadcasted_iota(jnp.int32, (TOK_DEV, TOK_DEV), 1)
    start = (jnp.full((1,), -1.0, jnp.float32), jnp.zeros((HEADS, DH, DH), jnp.float32))

    def scores_of(query_f, key_f, doc_row):
        pairs = causal & (doc_row[:, None] == doc_row[None, :])
        scores = jnp.einsum('thd,shd->hts', query_f, key_f)
        return (jnp.where(pairs[None], scores, 0.0).astype(jnp.bfloat16), pairs)

    def forward_step(carry, inputs):
        query_blk, key_blk, value_blk, doc_row = inputs
        query_f = query_blk.astype(jnp.float32)
        key_f = key_blk.astype(jnp.float32)
        value_f = value_blk.astype(jnp.float32)
        state_low = carry[1].astype(jnp.bfloat16).astype(jnp.float32)
        reads = (doc_row == carry[0][0]).astype(jnp.float32)
        scores_low, pairs = scores_of(query_f, key_f, doc_row)
        attn = jnp.einsum('hts,she->the', scores_low.astype(jnp.float32), value_f)
        attn = attn + reads[:, None, None] * jnp.einsum('thd,hde->the', query_f, state_low)
        tail = (doc_row == doc_row[-1]).astype(jnp.float32)
        own_state = jnp.einsum('shd,she->hde', key_f * tail[:, None, None], value_f)
        return (combine(carry, (doc_row[-1:], own_state)), (attn, carry[1], carry[0]))
    last_carry, (attn, state_in, prev_doc) = lax.scan(forward_step, start, (query_blocks, key_blocks, value_blocks, doc_blocks))
    attn = attn.reshape(TOKENS, HEADS, DH)
    scale = lax.rsqrt(lax.optimization_barrier(jnp.mean(attn * attn, axis=-1, keepdims=True)) + 1e-05)
    normed_f = attn * scale
    normed = normed_f.astype(jnp.bfloat16).reshape(TOKENS, HD)
    layer_out = jnp.dot(normed, out_weight, preferred_element_type=jnp.float32).astype(jnp.bfloat16)
    grad_normed = lax.dot_general(grad_out, out_weight, (((1,), (1,)), ((), ())), preferred_element_type=jnp.float32).reshape(TOKENS, HEADS, DH)
    grad_attn = (scale * (grad_normed - normed_f * lax.optimization_barrier(jnp.mean(grad_normed * normed_f, axis=-1, keepdims=True)))).astype(jnp.bfloat16)
    grad_weight = lax.dot_general(normed, grad_out, (((0,), (0,)), ((), ())), preferred_element_type=jnp.float32)
    grad_blocks = grad_attn.reshape(blocks, TOK_DEV, HEADS, DH)

    def backward_step(carry, inputs):
        query_blk, key_blk, value_blk, doc_row, grad_blk, state_blk, prev_blk = inputs
        query_f = query_blk.astype(jnp.float32)
        key_f = key_blk.astype(jnp.float32)
        value_f = value_blk.astype(jnp.float32)
        grad_f = grad_blk.astype(jnp.float32)
        state_low = state_blk.astype(jnp.bfloat16).astype(jnp.float32)
        back_low = carry[1].astype(jnp.bfloat16).astype(jnp.float32)
        reads = (doc_row == prev_blk[0]).astype(jnp.float32)
        writes = (doc_row == carry[0][0]).astype(jnp.float32)
        scores_low, pairs = scores_of(query_f, key_f, doc_row)
        grad_scores = jnp.einsum('the,she->hts', grad_f, value_f)
        grad_scores = jnp.where(pairs[None], grad_scores, 0.0).astype(jnp.bfloat16).astype(jnp.float32)
        grad_q = jnp.einsum('hts,shd->thd', grad_scores, key_f) + reads[:, None, None] * jnp.einsum('the,hde->thd', grad_f, state_low)
        grad_k = jnp.einsum('hts,thd->shd', grad_scores, query_f) + writes[:, None, None] * jnp.einsum('she,hde->shd', value_f, back_low)
        grad_v = jnp.einsum('hts,the->she', scores_low.astype(jnp.float32), grad_f) + writes[:, None, None] * jnp.einsum('shd,hde->she', key_f, back_low)
        head_mask = (doc_row == doc_row[0]).astype(jnp.float32)
        own_state = jnp.einsum('thd,the->hde', query_f * head_mask[:, None, None], grad_f)
        outs = (grad_q.astype(jnp.bfloat16), grad_k.astype(jnp.bfloat16), grad_v.astype(jnp.bfloat16))
        return (combine(carry, (doc_row[:1], own_state)), outs)
    final_carry, (grad_q, grad_k, grad_v) = lax.scan(backward_step, start, (query_blocks, key_blocks, value_blocks, doc_blocks, grad_blocks, state_in, prev_doc), reverse=True)
    shape = (TOKENS, HEADS, DH)
    return (layer_out, grad_q.reshape(shape), grad_k.reshape(shape), grad_v.reshape(shape), grad_weight)
```

```python
import functools

import jax
import jax.numpy as jnp
from jax import lax
from jax.experimental import pallas as pl
from jax.experimental.pallas import tpu as pltpu
from jax.sharding import PartitionSpec as P

BF = jnp.bfloat16
F32 = jnp.float32


def seq_index(y, z, c):
    return ((y % 4) * 4 + z % 4) * 2 + c


def seq_coords(i):
    return i // 8, (i // 2) % 4, i % 2


def route(move):
    pairs = []
    for i in range(32):
        target = move(*seq_coords(i))
        if target is not None:
            pairs.append((i, seq_index(*target)))
    return pairs


SWAP = route(lambda y, z, c: (y, z, 1 - c))


def along_z(step):
    return route(lambda y, z, c: (y, z + step, c))


def along_y_open(step):
    return route(lambda y, z, c: (y + step, z, c) if 0 <= y + step < 4 else None)


def along_first(step):
    return route(lambda y, z, c: (y + step, z, c) if c == 0 else (y, z + step, c))


def along_second(step):
    return route(lambda y, z, c: (y, z + step, c) if c == 0 else (y + step, z, c))


def exchange_states(own, doc, y, z, c, forward):
    sign = 1 if forward else -1
    heads, dim, _ = own.shape
    half = heads // 2
    rows = half * dim
    halves = own.reshape(2, rows, dim)
    mine = lax.dynamic_index_in_dim(halves, c, 0, keepdims=False)
    theirs = lax.dynamic_index_in_dim(halves, 1 - c, 0, keepdims=False)
    got = lax.ppermute(
        jnp.concatenate([theirs, jnp.full((8, dim), doc, F32)], 0), "seq", SWAP
    )
    other, other_doc = got[:rows], got[rows, 0]
    far_is_mine = (c == 0) if forward else (c == 1)
    far = jnp.where(far_is_mine, mine, other)
    near = jnp.where(far_is_mine, other, mine)
    far_doc = jnp.where(far_is_mine, doc, other_doc)
    near_doc = jnp.where(far_is_mine, other_doc, doc)
    chip = near + (far_doc == near_doc).astype(F32) * far
    packed = jnp.concatenate([chip, jnp.full((16, dim), near_doc, F32)], 0).astype(BF)
    row = [packed] + [lax.ppermute(packed, "seq", along_z(sign * k)) for k in (1, 2, 3)]
    row_doc = [near_doc] + [r[rows, 0].astype(F32) for r in row[1:]]
    place = z if forward else 3 - z
    end_doc = row_doc[0]
    for k in (1, 2, 3):
        end_doc = jnp.where((place - k) % 4 == 3, row_doc[k], end_doc)
    total = sum((row_doc[k] == end_doc).astype(F32) * row[k][:rows].astype(F32) for k in range(4))
    total = jnp.concatenate([total, jnp.full((16, dim), end_doc, F32)], 0).astype(BF)
    above = [lax.ppermute(total, "seq", along_y_open(sign * k)) for k in (1, 2)]
    level = y if forward else 3 - y
    above_doc = [
        jnp.where(level >= k + 1, above[k][rows, 0].astype(F32), -1.0) for k in range(2)
    ]
    before_doc = jnp.where(place >= 1, row_doc[1], above_doc[0])
    before = sum(
        ((row_doc[k] == before_doc) & (place >= k)).astype(F32) * row[k][:rows].astype(F32)
        for k in (1, 2, 3)
    )
    for k in range(2):
        before = before + ((above_doc[k] == before_doc) & (level >= k + 1)).astype(F32) * above[k][
            :rows
        ].astype(F32)
    after = far + (before_doc == far_doc).astype(F32) * before
    keep = jnp.where(far_is_mine, before, after).astype(BF)
    give = jnp.where(far_is_mine, after, before).astype(BF)
    take = lax.ppermute(give, "seq", SWAP)
    first = jnp.where(c == 0, keep, take)
    second = jnp.where(c == 0, take, keep)
    state = jnp.concatenate([first, second], 0).reshape(heads, dim, dim)
    return state, jnp.where(far_is_mine, before_doc, far_doc)


def weight_kernel(place, normed_ref, cot_ref, out_ref, turned, slots, sems):
    y, z, c = place[0], place[1], place[2]
    slices = cot_ref.shape[1] // 768
    width = 512
    copies = [None, None]
    for k in range(slices):
        slot = k % 2
        turned[...] = cot_ref[:, k * 768 : (k + 1) * 768].T
        if copies[slot] is not None:
            for copy in copies[slot]:
                copy.wait()
        for n in range(normed_ref.shape[1] // width):
            cols = slice(n * width, (n + 1) * width)
            product = jnp.dot(turned[...], normed_ref[:, cols], preferred_element_type=F32)
            slots[slot, :, :, cols] = product.astype(BF).reshape(8, 96, width)
        copies[slot] = []
        for piece in range(8):
            zz, cc = piece // 2, piece % 2
            a, b = (k, zz) if cc == 0 else (zz, k)
            here_a, here_b = (y, z) if cc == 0 else (z, y)
            copy = pltpu.make_async_copy(
                slots.at[slot, piece],
                out_ref.at[lax.rem(c + cc, 2), lax.rem(a + 4 - here_a, 4), lax.rem(b + 4 - here_b, 4)],
                sems.at[slot, piece],
            )
            copy.start()
            copies[slot].append(copy)
    for pending in copies:
        for copy in pending:
            copy.wait()


def weight_terms(normed, cotangent, place):
    tokens, features = normed.shape
    whole = pl.BlockSpec(memory_space=pltpu.VMEM)
    return pl.pallas_call(
        weight_kernel,
        out_shape=jax.ShapeDtypeStruct((2, 4, 4, 96, features), BF),
        in_specs=[pl.BlockSpec(memory_space=pltpu.SMEM), whole, whole],
        out_specs=pl.BlockSpec(memory_space=pl.ANY),
        scratch_shapes=[
            pltpu.VMEM((768, tokens), BF),
            pltpu.VMEM((2, 8, 96, features), BF),
            pltpu.SemaphoreType.DMA((2, 8)),
        ],
        compiler_params=pltpu.CompilerParams(vmem_limit_bytes=40 * 2**20),
        cost_estimate=pl.CostEstimate(
            flops=2 * tokens * features * 3072, bytes_accessed=11 * 2**20, transcendentals=0
        ),
        name="weight_terms",
    )(place, normed, cotangent)


def ring_sum(parts, plus, minus):
    rows = parts[0].shape[0] // 2
    up = lax.ppermute(parts[2][:rows].astype(BF), "seq", plus)
    down = lax.ppermute(parts[2][rows:].astype(BF), "seq", minus)
    right = jnp.concatenate([parts[1][:rows] + up.astype(F32), parts[1][rows:]], 0)
    left = jnp.concatenate([parts[3][:rows], parts[3][rows:] + down.astype(F32)], 0)
    from_left = lax.ppermute(right.astype(BF), "seq", plus)
    from_right = lax.ppermute(left.astype(BF), "seq", minus)
    return parts[0] + from_left.astype(F32) + from_right.astype(F32)


def shards(queries, key_vectors, value_vectors, doc_ids, out_weight, grad_out):
    i = lax.axis_index("seq")
    y, z, c = seq_coords(i)
    length = queries.shape[0]
    docs = doc_ids.astype(F32)
    cotangent = lax.all_gather(grad_out, "head", axis=1, tiled=True)
    causal = lax.broadcasted_iota(jnp.int32, (length, length), 0) >= lax.broadcasted_iota(
        jnp.int32, (length, length), 1
    )
    pairs = causal & (docs[:, None] == docs[None, :])
    tail = (docs == docs[-1]).astype(BF)
    own_state = jnp.einsum(
        "shd,she->hde",
        key_vectors * tail[:, None, None],
        value_vectors,
        preferred_element_type=F32,
    )
    state_low, before_doc = exchange_states(own_state, docs[-1], y, z, c, True)
    reads = (docs == before_doc).astype(F32)
    scores = jnp.einsum("thd,shd->hts", queries, key_vectors, preferred_element_type=F32)
    scores_low = jnp.where(pairs[None], scores, 0.0).astype(BF)
    attn = jnp.einsum("hts,she->the", scores_low, value_vectors, preferred_element_type=F32)
    attn = attn + reads[:, None, None] * jnp.einsum(
        "thd,hde->the", queries, state_low, preferred_element_type=F32
    )
    scale = lax.rsqrt(jnp.mean(attn * attn, axis=-1, keepdims=True) + 1e-05)
    normed_f = attn * scale
    normed = normed_f.astype(BF).reshape(length, -1)
    partial_out = jnp.dot(normed, out_weight, preferred_element_type=F32).astype(BF)
    layer_out = lax.psum_scatter(partial_out, "head", scatter_dimension=1, tiled=True).astype(BF)

    grad_normed = lax.dot_general(
        cotangent, out_weight, (((1,), (1,)), ((), ())), preferred_element_type=F32
    ).reshape(attn.shape)
    grad_attn = (
        scale * (grad_normed - normed_f * jnp.mean(grad_normed * normed_f, axis=-1, keepdims=True))
    ).astype(BF)

    head_mask = (docs == docs[0]).astype(BF)
    own_back = jnp.einsum(
        "thd,the->hde", queries * head_mask[:, None, None], grad_attn, preferred_element_type=F32
    )
    back_low, after_doc = exchange_states(own_back, docs[0], y, z, c, False)
    writes = (docs == after_doc).astype(F32)

    place = jnp.stack([y, z, c]).astype(jnp.int32)
    terms = weight_terms(normed, cotangent, place)
    swapped = lax.ppermute(terms[1], "seq", SWAP)
    shares = terms[0].astype(F32) + swapped.astype(F32)
    shares = shares.reshape(4, 4 * 96, -1)
    shares = ring_sum([shares[r] for r in range(4)], along_first(1), along_first(-1))
    shares = shares.reshape(4, 96, -1)
    shares = ring_sum([shares[r] for r in range(4)], along_second(1), along_second(-1))
    grad_weight = shares.T

    grad_scores = jnp.einsum("the,she->hts", grad_attn, value_vectors, preferred_element_type=F32)
    grad_scores = jnp.where(pairs[None], grad_scores, 0.0).astype(BF)
    grad_queries = jnp.einsum(
        "hts,shd->thd", grad_scores, key_vectors, preferred_element_type=F32
    )
    grad_queries = grad_queries + reads[:, None, None] * jnp.einsum(
        "the,hde->thd", grad_attn, state_low, preferred_element_type=F32
    )
    grad_keys = jnp.einsum("hts,thd->shd", grad_scores, queries, preferred_element_type=F32)
    grad_keys = grad_keys + writes[:, None, None] * jnp.einsum(
        "she,hde->shd", value_vectors, back_low, preferred_element_type=F32
    )
    grad_values = jnp.einsum("hts,the->she", scores_low, grad_attn, preferred_element_type=F32)
    grad_values = grad_values + writes[:, None, None] * jnp.einsum(
        "shd,hde->she", key_vectors, back_low, preferred_element_type=F32
    )
    return (
        layer_out,
        grad_queries.astype(BF),
        grad_keys.astype(BF),
        grad_values.astype(BF),
        grad_weight,
    )


def solution(mesh):
    placed = (
        P("seq", "head", None),
        P("seq", "head", None),
        P("seq", "head", None),
        P("seq"),
        P("head", None),
        P("seq", "head"),
    )
    return jax.shard_map(
        shards,
        mesh=mesh,
        in_specs=placed,
        out_specs=(
            P("seq", "head"),
            P("seq", "head", None),
            P("seq", "head", None),
            P("seq", "head", None),
            P("head", "seq"),
        ),
        check_vma=False,
    )
```

```python
import jax
import jax.numpy as jnp
from jax import lax
from jax.experimental import pallas as pl
from jax.experimental.pallas import tpu as pltpu
from jax.sharding import PartitionSpec as P

BF = jnp.bfloat16
F32 = jnp.float32
TOK, HEADS, DIM, FEAT, COLS = 512, 8, 128, 1024, 3072
HALF = HEADS // 2
ROWS = HALF * DIM
MIB = 2**20


def shape(dims, dtype):
    return jax.ShapeDtypeStruct(dims, dtype)


def whole():
    return pl.BlockSpec(memory_space=pltpu.VMEM)


def scalars():
    return pl.BlockSpec(memory_space=pltpu.SMEM)


def params(mib):
    return pltpu.CompilerParams(vmem_limit_bytes=mib * MIB)


def cost(flops, moved):
    return pl.CostEstimate(flops=flops, bytes_accessed=moved, transcendentals=0)


def dot(a, b, ca, cb):
    return lax.dot_general(a, b, (((ca,), (cb,)), ((), ())), preferred_element_type=F32)


def upright(docs_row, width):
    return jnp.broadcast_to(docs_row, (width, docs_row.shape[1])).T


def prepare_kernel(place, q_ref, k_ref, v_ref, docs_ref, qh_ref, kh_ref, vh_ref, keep_ref, give_ref, own):
    c = place[2]
    docs = docs_ref[...]
    last = docs[:, TOK - 1 :]
    tail = (upright(docs, DIM) == last).astype(BF)
    kh = jnp.swapaxes(k_ref[...], 0, 1)
    vh = jnp.swapaxes(v_ref[...], 0, 1)
    kh_ref[...] = kh
    vh_ref[...] = vh
    for h in range(HEADS):
        own[h // HALF, (h % HALF) * DIM : (h % HALF + 1) * DIM] = dot(kh[h] * tail, vh[h], 0, 0)
    keep_ref[:ROWS] = own[c]
    give_ref[:ROWS] = own[1 - c]
    doc_rows = jnp.broadcast_to(last, (8, DIM))
    keep_ref[ROWS:] = doc_rows
    give_ref[ROWS:] = doc_rows
    qh_ref[...] = jnp.swapaxes(q_ref[...], 0, 1)


def prepare(place, queries, keys, values, docs):
    head_major = shape((HEADS, TOK, DIM), BF)
    half = shape((ROWS + 8, DIM), F32)
    return pl.pallas_call(
        prepare_kernel,
        out_shape=(head_major, head_major, head_major, half, half),
        in_specs=[scalars()] + [whole()] * 4,
        out_specs=(whole(),) * 5,
        scratch_shapes=[pltpu.VMEM((2, ROWS, DIM), F32)],
        compiler_params=params(32),
        cost_estimate=cost(2 * HEADS * TOK * DIM * DIM, 8 * MIB),
        name="prepare",
    )(place, queries, keys, values, docs)


def chip_kernel(forward, place, keep_ref, got_ref, far_ref, chip_ref):
    c = place[2]
    far_is_mine = (c == 0) if forward else (c == 1)

    def write(far, near):
        same = (far[ROWS : ROWS + 1] == near[ROWS : ROWS + 1]).astype(F32)
        far_ref[...] = far[...]
        chip_ref[:ROWS] = (near[:ROWS] + same * far[:ROWS]).astype(BF)
        chip_ref[ROWS:] = jnp.broadcast_to(near[ROWS : ROWS + 1], (16, DIM)).astype(BF)

    @pl.when(far_is_mine)
    def _():
        write(keep_ref, got_ref)

    @pl.when(jnp.logical_not(far_is_mine))
    def _():
        write(got_ref, keep_ref)


def chip_state(place, keep, got, forward):
    def kernel(*refs):
        chip_kernel(forward, *refs)

    return pl.pallas_call(
        kernel,
        out_shape=(shape((ROWS + 8, DIM), F32), shape((ROWS + 16, DIM), BF)),
        in_specs=[scalars(), whole(), whole()],
        out_specs=(whole(), whole()),
        compiler_params=params(8),
        cost_estimate=cost(ROWS * DIM * 3, MIB),
        name="chip_state",
    )(place, keep, got)


def row_kernel(forward, place, p0, p1, p2, p3, total_ref):
    z = place[1]
    spot = z if forward else 3 - z
    parts = (p0, p1, p2, p3)
    docs = [p[ROWS : ROWS + 1].astype(F32) for p in parts]
    end = docs[0]
    for k in (1, 2, 3):
        end = jnp.where(lax.rem(spot + 4 - k, 4) == 3, docs[k], end)
    total = (docs[0] == end).astype(F32) * p0[:ROWS].astype(F32)
    for k in (1, 2, 3):
        total = total + (docs[k] == end).astype(F32) * parts[k][:ROWS].astype(F32)
    total_ref[:ROWS] = total.astype(BF)
    total_ref[ROWS:] = jnp.broadcast_to(end, (16, DIM)).astype(BF)


def row_state(place, parts, forward):
    def kernel(*refs):
        row_kernel(forward, *refs)

    return pl.pallas_call(
        kernel,
        out_shape=shape((ROWS + 16, DIM), BF),
        in_specs=[scalars()] + [whole()] * 4,
        out_specs=whole(),
        compiler_params=params(8),
        cost_estimate=cost(ROWS * DIM * 8, MIB),
        name="row_state",
    )(place, *parts)


def entry_kernel(forward, place, far_ref, p1, p2, p3, above1, above2, keep_ref, give_ref, doc_ref):
    y, z, c = place[0], place[1], place[2]
    spot = z if forward else 3 - z
    level = y if forward else 3 - y
    far_is_mine = (c == 0) if forward else (c == 1)
    parts = (p1, p2, p3)
    aboves = (above1, above2)
    docs = [p[ROWS : ROWS + 1].astype(F32) for p in parts]
    above_docs = [
        jnp.where(level >= k + 1, aboves[k][ROWS : ROWS + 1].astype(F32), -1.0) for k in range(2)
    ]
    before_doc = jnp.where(spot >= 1, docs[0], above_docs[0])
    before = jnp.zeros((ROWS, DIM), F32)
    for k in range(3):
        use = jnp.where(spot >= k + 1, (docs[k] == before_doc).astype(F32), 0.0)
        before = before + use * parts[k][:ROWS].astype(F32)
    for k in range(2):
        use = jnp.where(level >= k + 1, (above_docs[k] == before_doc).astype(F32), 0.0)
        before = before + use * aboves[k][:ROWS].astype(F32)
    far_doc = far_ref[ROWS : ROWS + 1]
    after = far_ref[:ROWS] + (before_doc == far_doc).astype(F32) * before

    @pl.when(far_is_mine)
    def _():
        keep_ref[...] = before.astype(BF)
        give_ref[...] = after.astype(BF)
        doc_ref[...] = jnp.broadcast_to(before_doc, (8, DIM))

    @pl.when(jnp.logical_not(far_is_mine))
    def _():
        keep_ref[...] = after.astype(BF)
        give_ref[...] = before.astype(BF)
        doc_ref[...] = jnp.broadcast_to(far_doc, (8, DIM))


def entry_state(place, far, parts, aboves, forward):
    def kernel(*refs):
        entry_kernel(forward, *refs)

    half = shape((ROWS, DIM), BF)
    return pl.pallas_call(
        kernel,
        out_shape=(half, half, shape((8, DIM), F32)),
        in_specs=[scalars()] + [whole()] * 6,
        out_specs=(whole(),) * 3,
        compiler_params=params(8),
        cost_estimate=cost(ROWS * DIM * 12, MIB),
        name="entry_state",
    )(place, far, *parts, *aboves)


def intra_kernel(q_ref, k_ref, v_ref, docs_ref, attn_ref, mask):
    @pl.when(pl.program_id(0) == 0)
    def _():
        row = jnp.broadcast_to(docs_ref[...], (TOK, TOK))
        t = lax.broadcasted_iota(jnp.int32, (TOK, TOK), 0)
        s = lax.broadcasted_iota(jnp.int32, (TOK, TOK), 1)
        mask[...] = ((t >= s) & (row.T == row)).astype(BF)

    q, k, v = q_ref[0], k_ref[0], v_ref[0]
    mid = TOK // 2
    for rows, width in ((slice(0, mid), mid), (slice(mid, TOK), TOK)):
        scores = dot(q[rows], k[:width], 1, 1).astype(BF) * mask[rows, :width]
        attn_ref[0, rows] = dot(scores, v[:width], 1, 0)


def intra(qh, kh, vh, docs):
    head = pl.BlockSpec((1, TOK, DIM), lambda h: (h, 0, 0))
    return pl.pallas_call(
        intra_kernel,
        grid=(HEADS,),
        out_shape=shape((HEADS, TOK, DIM), F32),
        in_specs=[head, head, head, pl.BlockSpec((1, TOK), lambda h: (0, 0))],
        out_specs=head,
        scratch_shapes=[pltpu.VMEM((TOK, TOK), BF)],
        compiler_params=params(32),
        cost_estimate=cost(4 * HEADS * TOK * TOK * DIM, 5 * MIB),
        name="intra",
    )(qh, kh, vh, docs)


def pick_state(c, keep_ref, take_ref, h):
    rows = slice((h % HALF) * DIM, (h % HALF + 1) * DIM)
    mine = c == h // HALF
    return jnp.where(mine, keep_ref[rows], take_ref[rows])


def finish_kernel(place, q_ref, intra_ref, keep_ref, take_ref, doc_ref, docs_ref, w_ref, attn_ref, normed_ref, out_ref):
    @pl.when(pl.program_id(0) == 0)
    def _():
        c = place[2]
        reads = (upright(docs_ref[...], DIM) == doc_ref[:1]).astype(F32)
        for h in range(HEADS):
            state = pick_state(c, keep_ref, take_ref, h)
            attn = intra_ref[h] + reads * dot(q_ref[h], state, 1, 0)
            attn_ref[h] = attn
            scale = lax.rsqrt(jnp.mean(attn * attn, axis=-1, keepdims=True) + 1e-05)
            normed_ref[:, h * DIM : (h + 1) * DIM] = (attn * scale).astype(BF)

    out_ref[...] = jnp.dot(normed_ref[...], w_ref[...], preferred_element_type=F32).astype(BF)


def finish(place, qh, attn_intra, keep, take, doc, docs, weight):
    steps, width = 3, COLS // 3
    fixed = lambda *dims: pl.BlockSpec(dims, lambda n: (0,) * len(dims))
    return pl.pallas_call(
        finish_kernel,
        grid=(steps,),
        out_shape=(shape((HEADS, TOK, DIM), F32), shape((TOK, FEAT), BF), shape((TOK, COLS), BF)),
        in_specs=[
            scalars(),
            fixed(HEADS, TOK, DIM),
            fixed(HEADS, TOK, DIM),
            fixed(ROWS, DIM),
            fixed(ROWS, DIM),
            fixed(8, DIM),
            fixed(1, TOK),
            pl.BlockSpec((FEAT, width), lambda n: (0, n)),
        ],
        out_specs=(
            fixed(HEADS, TOK, DIM),
            fixed(TOK, FEAT),
            pl.BlockSpec((TOK, width), lambda n: (0, n)),
        ),
        compiler_params=params(40),
        cost_estimate=cost(2 * TOK * FEAT * COLS + 2 * HEADS * TOK * DIM * DIM, 15 * MIB),
        name="finish",
    )(place, qh, attn_intra, keep, take, doc, docs, weight)


def back_kernel(place, cot_ref, w_ref, attn_ref, q_ref, docs_ref, grad_ref, keep_ref, give_ref, own):
    n = pl.program_id(0)
    docs = docs_ref[...]
    first = docs[:, :1]
    lead = (upright(docs, DIM) == first).astype(BF)
    grad_normed = dot(cot_ref[...], w_ref[...], 1, 1)
    for j in range(2):
        attn = attn_ref[j]
        scale = lax.rsqrt(jnp.mean(attn * attn, axis=-1, keepdims=True) + 1e-05)
        normed = attn * scale
        grad = grad_normed[:, j * DIM : (j + 1) * DIM]
        grad = scale * (grad - normed * jnp.mean(grad * normed, axis=-1, keepdims=True))
        grad = grad.astype(BF)
        grad_ref[j] = grad
        spot = pl.multiple_of(lax.rem(n, 2) * 2 * DIM + j * DIM, DIM)
        own[n // 2, pl.ds(spot, DIM)] = dot(q_ref[j] * lead, grad, 0, 0)

    @pl.when(n == pl.num_programs(0) - 1)
    def _():
        c = place[2]
        keep_ref[:ROWS] = own[c]
        give_ref[:ROWS] = own[1 - c]
        doc_rows = jnp.broadcast_to(first, (8, DIM))
        keep_ref[ROWS:] = doc_rows
        give_ref[ROWS:] = doc_rows


def back(place, cotangent, weight, attn, qh, docs):
    fixed = lambda *dims: pl.BlockSpec(dims, lambda n: (0,) * len(dims))
    pair = pl.BlockSpec((2, TOK, DIM), lambda n: (n, 0, 0))
    half = shape((ROWS + 8, DIM), F32)
    return pl.pallas_call(
        back_kernel,
        grid=(HEADS // 2,),
        out_shape=(shape((HEADS, TOK, DIM), BF), half, half),
        in_specs=[
            scalars(),
            fixed(TOK, COLS),
            pl.BlockSpec((2 * DIM, COLS), lambda n: (n, 0)),
            pair,
            pair,
            fixed(1, TOK),
        ],
        out_specs=(pair, fixed(ROWS + 8, DIM), fixed(ROWS + 8, DIM)),
        scratch_shapes=[pltpu.VMEM((2, ROWS, DIM), F32)],
        compiler_params=params(40),
        cost_estimate=cost(2 * TOK * FEAT * COLS + 2 * HEADS * TOK * DIM * DIM, 15 * MIB),
        name="back",
    )(place, cotangent, weight, attn, qh, docs)


def terms_kernel(place, cot_ref, cot2_ref, normed_ref, normed2_ref, out_ref, up_ref, down_ref, turned, sums):
    y, z, c = place[0], place[1], place[2]
    n = pl.program_id(0)
    turned[:, :TOK] = cot_ref[...].T
    turned[:, TOK:] = cot2_ref[...].T
    base = pl.multiple_of(c * 96, 32)
    left = jnp.concatenate([turned[pl.ds(base + 192 * b, 96)] for b in range(4)], 0)
    product = dot(left[:, :TOK], normed_ref[...], 1, 0) + dot(left[:, TOK:], normed2_ref[...], 1, 0)
    for b in range(4):
        first = jnp.where(c == 0, lax.rem(n + 4 - y, 4), lax.rem(b + 4 - z, 4))
        second = jnp.where(c == 0, lax.rem(b + 4 - z, 4), lax.rem(n + 4 - y, 4))
        block = product[b * 96 : (b + 1) * 96]
        out_ref[first, second] = block

    @pl.when(n == 3)
    def _():
        up_ref[...] = out_ref[2, :2].reshape(192, FEAT).astype(BF)
        down_ref[...] = out_ref[2, 2:].reshape(192, FEAT).astype(BF)


def weight_terms(place, cotangent, cotangent2, normed, normed2):
    fixed = lambda *dims: pl.BlockSpec(dims, lambda n: (0,) * len(dims))
    slab = pl.BlockSpec((TOK, 768), lambda n: (0, n))
    return pl.pallas_call(
        terms_kernel,
        grid=(4,),
        out_shape=(shape((4, 4, 96, FEAT), F32), shape((192, FEAT), BF), shape((192, FEAT), BF)),
        in_specs=[scalars(), slab, slab, fixed(TOK, FEAT), fixed(TOK, FEAT)],
        out_specs=(fixed(4, 4, 96, FEAT), fixed(192, FEAT), fixed(192, FEAT)),
        scratch_shapes=[pltpu.VMEM((768, 2 * TOK), BF), pltpu.SMEM((1,), jnp.int32)],
        compiler_params=params(48),
        cost_estimate=cost(2 * TOK * FEAT * COLS, 15 * MIB),
        name="weight_terms",
    )(place, cotangent, cotangent2, normed, normed2)


def inner_kernel(place, q_ref, k_ref, v_ref, grad_ref, keep_ref, take_ref, doc_ref, docs_ref, gq_ref, gk_ref, gv_ref, mask, turned, held):
    n = pl.program_id(0)

    @pl.when(n == 0)
    def _():
        row = jnp.broadcast_to(docs_ref[...], (TOK, TOK))
        same = row.T == row
        t = lax.broadcasted_iota(jnp.int32, (TOK, TOK), 0)
        s = lax.broadcasted_iota(jnp.int32, (TOK, TOK), 1)
        mask[...] = ((t >= s) & same).astype(BF)
        turned[...] = ((s >= t) & same).astype(BF)

    c = place[2]
    q, k, v, grad = q_ref[0], k_ref[0], v_ref[0], grad_ref[0]
    spot = pl.multiple_of(lax.rem(n, HALF) * DIM, DIM)
    state = jnp.where(c == n // HALF, keep_ref[pl.ds(spot, DIM)], take_ref[pl.ds(spot, DIM)])
    reads = (upright(docs_ref[...], DIM) == doc_ref[:1]).astype(F32)
    across = reads * dot(grad, state, 1, 1)
    mid = TOK // 2
    for rows, width in ((slice(0, mid), mid), (slice(mid, TOK), TOK)):
        scores = dot(grad[rows], v[:width], 1, 1).astype(BF) * mask[rows, :width]
        held[n, rows] = (dot(scores, k[:width], 1, 0) + across[rows]).astype(BF)
    for rows, start in ((slice(0, mid), 0), (slice(mid, TOK), mid)):
        scores = dot(v[rows], grad[start:], 1, 1).astype(BF) * turned[rows, start:]
        gk_ref[0, rows] = dot(scores, q[start:], 1, 0)
        scores = dot(k[rows], q[start:], 1, 1).astype(BF) * turned[rows, start:]
        gv_ref[0, rows] = dot(scores, grad[start:], 1, 0)

    @pl.when(n == HEADS - 1)
    def _():
        gq_ref[...] = jnp.swapaxes(held[...], 0, 1)


def inner(place, qh, kh, vh, grad, keep, take, doc, docs):
    head = pl.BlockSpec((1, TOK, DIM), lambda h: (h, 0, 0))
    fixed = lambda *dims: pl.BlockSpec(dims, lambda n: (0,) * len(dims))
    return pl.pallas_call(
        inner_kernel,
        grid=(HEADS,),
        out_shape=(shape((TOK, HEADS, DIM), BF),) + (shape((HEADS, TOK, DIM), F32),) * 2,
        in_specs=[scalars()] + [head] * 4 + [fixed(ROWS, DIM)] * 2 + [fixed(8, DIM), fixed(1, TOK)],
        out_specs=(fixed(TOK, HEADS, DIM), head, head),
        scratch_shapes=[
            pltpu.VMEM((TOK, TOK), BF),
            pltpu.VMEM((TOK, TOK), BF),
            pltpu.VMEM((HEADS, TOK, DIM), BF),
        ],
        compiler_params=params(32),
        cost_estimate=cost(10 * HEADS * TOK * TOK * DIM, 9 * MIB),
        name="inner",
    )(place, qh, kh, vh, grad, keep, take, doc, docs)


def last_kernel(place, k_ref, v_ref, gk_ref, gv_ref, keep_ref, take_ref, doc_ref, docs_ref, out_k, out_v, held_k, held_v):
    c = place[2]
    writes = (upright(docs_ref[...], DIM) == doc_ref[:1]).astype(F32)
    for h in range(HEADS):
        state = pick_state(c, keep_ref, take_ref, h)
        held_k[h] = (gk_ref[h] + writes * dot(v_ref[h], state, 1, 1)).astype(BF)
        held_v[h] = (gv_ref[h] + writes * dot(k_ref[h], state, 1, 0)).astype(BF)
    out_k[...] = jnp.swapaxes(held_k[...], 0, 1)
    out_v[...] = jnp.swapaxes(held_v[...], 0, 1)


def last(place, kh, vh, gk, gv, keep, take, doc, docs):
    out = shape((TOK, HEADS, DIM), BF)
    return pl.pallas_call(
        last_kernel,
        out_shape=(out, out),
        in_specs=[scalars()] + [whole()] * 8,
        out_specs=(whole(), whole()),
        scratch_shapes=[pltpu.VMEM((HEADS, TOK, DIM), BF)] * 2,
        compiler_params=params(32),
        cost_estimate=cost(4 * HEADS * TOK * DIM * DIM, 9 * MIB),
        name="last",
    )(place, kh, vh, gk, gv, keep, take, doc, docs)


def pass_kernel(right_ref, left_ref, up_ref, down_ref, out_right, out_left):
    rows = up_ref.shape[0]
    right = right_ref[...].reshape(2 * rows, FEAT)
    left = left_ref[...].reshape(2 * rows, FEAT)
    out_right[:rows] = (right[:rows] + up_ref[...].astype(F32)).astype(BF)
    out_right[rows:] = right[rows:].astype(BF)
    out_left[:rows] = left[:rows].astype(BF)
    out_left[rows:] = (left[rows:] + down_ref[...].astype(F32)).astype(BF)


def pass_on(terms, up, down):
    part = terms.shape[1:]
    pick = lambda r: pl.BlockSpec((pl.squeezed,) + part, lambda n: (r,) + (0,) * len(part))
    rows = up.shape[0]
    fixed = lambda r: pl.BlockSpec((r, FEAT), lambda n: (0, 0))
    out = shape((2 * rows, FEAT), BF)
    return pl.pallas_call(
        pass_kernel,
        grid=(1,),
        out_shape=(out, out),
        in_specs=[pick(1), pick(3), fixed(rows), fixed(rows)],
        out_specs=(fixed(2 * rows), fixed(2 * rows)),
        compiler_params=params(32),
        cost_estimate=cost(rows * FEAT * 4, 24 * rows * FEAT),
        name="pass_on",
    )(terms, terms, up, down)


def middle_kernel(own_ref, left_ref, right_ref, terms_ref, up_ref, down_ref):
    total = own_ref[...].reshape(384, FEAT) + left_ref[...].astype(F32) + right_ref[...].astype(F32)
    terms_ref[...] = total.reshape(4, 96, FEAT)
    up_ref[...] = total[192:240].astype(BF)
    down_ref[...] = total[240:288].astype(BF)


def middle(terms, from_left, from_right):
    part = (4, 96, FEAT)
    fixed = lambda *dims: pl.BlockSpec(dims, lambda n: (0,) * len(dims))
    small = shape((48, FEAT), BF)
    return pl.pallas_call(
        middle_kernel,
        grid=(1,),
        out_shape=(shape(part, F32), small, small),
        in_specs=[
            pl.BlockSpec((pl.squeezed,) + part, lambda n: (0, 0, 0, 0)),
            fixed(384, FEAT),
            fixed(384, FEAT),
        ],
        out_specs=(fixed(*part), fixed(48, FEAT), fixed(48, FEAT)),
        compiler_params=params(32),
        cost_estimate=cost(384 * FEAT * 2, 5 * MIB),
        name="middle",
    )(terms, from_left, from_right)


def end_kernel(own_ref, left_ref, right_ref, out_ref):
    total = own_ref[...] + left_ref[...].astype(F32) + right_ref[...].astype(F32)
    out_ref[...] = total.T


def end(terms, from_left, from_right):
    fixed = lambda *dims: pl.BlockSpec(dims, lambda n: (0,) * len(dims))
    return pl.pallas_call(
        end_kernel,
        grid=(1,),
        out_shape=shape((FEAT, 96), F32),
        in_specs=[
            pl.BlockSpec((pl.squeezed, 96, FEAT), lambda n: (0, 0, 0)),
            fixed(96, FEAT),
            fixed(96, FEAT),
        ],
        out_specs=fixed(FEAT, 96),
        compiler_params=params(16),
        cost_estimate=cost(96 * FEAT * 2, MIB),
        name="end",
    )(terms, from_left, from_right)


def route(move):
    pairs = []
    for i in range(32):
        target = move(i // 8, (i // 2) % 4, i % 2)
        if target is not None:
            y, z, c = target
            pairs.append((i, ((y % 4) * 4 + z % 4) * 2 + c))
    return pairs


SWAP = route(lambda y, z, c: (y, z, 1 - c))


def along_z(step):
    return route(lambda y, z, c: (y, z + step, c))


def along_y_open(step):
    return route(lambda y, z, c: (y + step, z, c) if 0 <= y + step < 4 else None)


def along_first(step):
    return route(lambda y, z, c: (y + step, z, c) if c == 0 else (y, z + step, c))


def along_second(step):
    return route(lambda y, z, c: (y, z + step, c) if c == 0 else (y + step, z, c))


def send(array, pairs):
    return lax.ppermute(array, "seq", pairs)


def exchange(place, keep, give, forward):
    sign = 1 if forward else -1
    got = send(give, SWAP)
    far, chip = chip_state(place, keep, got, forward)
    parts = [send(chip, along_z(sign * k)) for k in (1, 2, 3)]
    total = row_state(place, [chip] + parts, forward)
    aboves = [send(total, along_y_open(sign * k)) for k in (1, 2)]
    mine, theirs, doc = entry_state(place, far, parts, aboves, forward)
    return mine, send(theirs, SWAP), doc


def shards(queries, key_vectors, value_vectors, doc_ids, out_weight, grad_out):
    i = lax.axis_index("seq")
    place = jnp.stack([i // 8, (i // 2) % 4, i % 2]).astype(jnp.int32)
    docs = doc_ids.astype(F32).reshape(1, TOK)
    cotangent = lax.all_gather(grad_out, "head", axis=1, tiled=True)
    qh, kh, vh, keep, give = prepare(place, queries, key_vectors, value_vectors, docs)
    mine, taken, doc = exchange(place, keep, give, True)
    attn_intra = intra(qh, kh, vh, docs)
    attn, normed, partial_out = finish(place, qh, attn_intra, mine, taken, doc, docs, out_weight)
    layer_out = lax.psum_scatter(partial_out, "head", scatter_dimension=1, tiled=True)
    normed2 = send(normed, SWAP)
    cotangent2 = send(cotangent, SWAP)
    grad, keep, give = back(place, cotangent, out_weight, attn, qh, docs)
    back_mine, back_taken, back_doc = exchange(place, keep, give, False)
    terms, up, down = weight_terms(place, cotangent, cotangent2, normed, normed2)
    up, down = send(up, along_first(1)), send(down, along_first(-1))
    right, left = pass_on(terms, up, down)
    terms, up, down = middle(terms, send(right, along_first(1)), send(left, along_first(-1)))
    up, down = send(up, along_second(1)), send(down, along_second(-1))
    right, left = pass_on(terms, up, down)
    grad_weight = end(terms, send(right, along_second(1)), send(left, along_second(-1)))
    grad_queries, gk, gv = inner(place, qh, kh, vh, grad, mine, taken, doc, docs)
    grad_keys, grad_values = last(place, kh, vh, gk, gv, back_mine, back_taken, back_doc, docs)
    return layer_out, grad_queries, grad_keys, grad_values, grad_weight


def solution(mesh):
    placed = (
        P("seq", "head", None),
        P("seq", "head", None),
        P("seq", "head", None),
        P("seq"),
        P("head", None),
        P("seq", "head"),
    )
    return jax.shard_map(
        shards,
        mesh=mesh,
        in_specs=placed,
        out_specs=(
            P("seq", "head"),
            P("seq", "head", None),
            P("seq", "head", None),
            P("seq", "head", None),
            P("head", "seq"),
        ),
        check_vma=False,
    )
```

```python
import jax
import jax.numpy as jnp
from jax import lax
from jax.experimental import pallas as pl
from jax.experimental.pallas import tpu as pltpu
from jax.sharding import PartitionSpec as P

BF = jnp.bfloat16
F32 = jnp.float32
TOK, HEADS, DIM, FEAT, COLS = 512, 8, 128, 1024, 3072
HALF = HEADS // 2
ROWS = HALF * DIM
MIB = 2**20


def shape(dims, dtype):
    return jax.ShapeDtypeStruct(dims, dtype)


def whole():
    return pl.BlockSpec(memory_space=pltpu.VMEM)


def scalars():
    return pl.BlockSpec(memory_space=pltpu.SMEM)


def params(mib):
    return pltpu.CompilerParams(vmem_limit_bytes=mib * MIB)


def cost(flops, moved):
    return pl.CostEstimate(flops=flops, bytes_accessed=moved, transcendentals=0)


def dot(a, b, ca, cb):
    return lax.dot_general(a, b, (((ca,), (cb,)), ((), ())), preferred_element_type=F32)


def fixed(*dims):
    return pl.BlockSpec(dims, lambda n: (0,) * len(dims))


def anywhere():
    return pl.BlockSpec(memory_space=pl.ANY)


def upright(docs_row, width):
    return jnp.broadcast_to(docs_row, (width, docs_row.shape[1])).T


def prepare_kernel(place, k_ref, v_ref, docs_ref, kh_ref, vh_ref, keep_ref, give_ref, own):
    c = place[2]
    n = pl.program_id(0)
    last = docs_ref[:, TOK - 1 :]
    rows = k_ref.shape[0]
    spot = pl.multiple_of(n * rows, rows)
    tail = (upright(docs_ref[:, pl.ds(spot, rows)], DIM) == last).astype(BF)
    kh = jnp.swapaxes(k_ref[...], 0, 1)
    vh = jnp.swapaxes(v_ref[...], 0, 1)
    kh_ref[...] = kh
    vh_ref[...] = vh

    @pl.when(n == 0)
    def _():
        own[...] = jnp.zeros_like(own)

    for h in range(HEADS):
        own[h // HALF, (h % HALF) * DIM : (h % HALF + 1) * DIM] += dot(kh[h] * tail, vh[h], 0, 0)

    @pl.when(n == pl.num_programs(0) - 1)
    def _():
        keep_ref[:ROWS] = own[c]
        give_ref[:ROWS] = own[1 - c]
        doc_rows = jnp.broadcast_to(last, (8, DIM))
        keep_ref[ROWS:] = doc_rows
        give_ref[ROWS:] = doc_rows


def prepare(place, keys, values, docs):
    steps = 2
    rows = TOK // steps
    head_major = shape((HEADS, TOK, DIM), BF)
    half = shape((ROWS + 8, DIM), F32)
    some = pl.BlockSpec((rows, HEADS, DIM), lambda n: (n, 0, 0))
    turned = pl.BlockSpec((HEADS, rows, DIM), lambda n: (0, n, 0))
    return pl.pallas_call(
        prepare_kernel,
        grid=(steps,),
        out_shape=(head_major, head_major, half, half),
        in_specs=[scalars(), some, some, fixed(1, TOK)],
        out_specs=(turned, turned, fixed(ROWS + 8, DIM), fixed(ROWS + 8, DIM)),
        scratch_shapes=[pltpu.VMEM((2, ROWS, DIM), F32)],
        compiler_params=params(12),
        cost_estimate=cost(2 * HEADS * TOK * DIM * DIM, 5 * MIB),
        name="prepare",
    )(place, keys, values, docs)


def chip_kernel(forward, place, keep_ref, got_ref, earlier, far_ref, chip_ref):
    c = place[2]
    far_is_mine = (c == 0) if forward else (c == 1)

    def write(far, near):
        same = (far[ROWS : ROWS + 1] == near[ROWS : ROWS + 1]).astype(F32)
        far_ref[...] = far[...]
        chip_ref[:ROWS] = (near[:ROWS] + same * far[:ROWS]).astype(BF)
        chip_ref[ROWS:] = jnp.broadcast_to(near[ROWS : ROWS + 1], (16, DIM)).astype(BF)

    @pl.when(far_is_mine)
    def _():
        write(keep_ref, got_ref)

    @pl.when(jnp.logical_not(far_is_mine))
    def _():
        write(got_ref, keep_ref)


def chip_state(place, keep, got, forward, earlier):
    def kernel(*refs):
        chip_kernel(forward, *refs)

    return pl.pallas_call(
        kernel,
        out_shape=(shape((ROWS + 8, DIM), F32), shape((ROWS + 16, DIM), BF)),
        in_specs=[scalars(), whole(), whole(), anywhere()],
        out_specs=(whole(), whole()),
        compiler_params=params(4),
        cost_estimate=cost(ROWS * DIM * 3, MIB),
        name="chip_state",
    )(place, keep, got, earlier)


def row_kernel(forward, place, p0, p1, p2, p3, earlier, total_ref):
    z = place[1]
    spot = z if forward else 3 - z
    parts = (p0, p1, p2, p3)
    docs = [p[ROWS : ROWS + 1].astype(F32) for p in parts]
    end = docs[0]
    for k in (1, 2, 3):
        end = jnp.where(lax.rem(spot + 4 - k, 4) == 3, docs[k], end)
    total = (docs[0] == end).astype(F32) * p0[:ROWS].astype(F32)
    for k in (1, 2, 3):
        total = total + (docs[k] == end).astype(F32) * parts[k][:ROWS].astype(F32)
    total_ref[:ROWS] = total.astype(BF)
    total_ref[ROWS:] = jnp.broadcast_to(end, (16, DIM)).astype(BF)


def row_state(place, parts, forward, earlier):
    def kernel(*refs):
        row_kernel(forward, *refs)

    return pl.pallas_call(
        kernel,
        out_shape=shape((ROWS + 16, DIM), BF),
        in_specs=[scalars()] + [whole()] * 4 + [anywhere()],
        out_specs=whole(),
        compiler_params=params(4),
        cost_estimate=cost(ROWS * DIM * 8, MIB),
        name="row_state",
    )(place, *parts, earlier)


def entry_kernel(forward, place, far_ref, p1, p2, p3, above1, above2, earlier, keep_ref, give_ref, doc_ref):
    y, z, c = place[0], place[1], place[2]
    spot = z if forward else 3 - z
    level = y if forward else 3 - y
    far_is_mine = (c == 0) if forward else (c == 1)
    parts = (p1, p2, p3)
    aboves = (above1, above2)
    docs = [p[ROWS : ROWS + 1].astype(F32) for p in parts]
    above_docs = [
        jnp.where(level >= k + 1, aboves[k][ROWS : ROWS + 1].astype(F32), -1.0) for k in range(2)
    ]
    before_doc = jnp.where(spot >= 1, docs[0], above_docs[0])
    before = jnp.zeros((ROWS, DIM), F32)
    for k in range(3):
        use = jnp.where(spot >= k + 1, (docs[k] == before_doc).astype(F32), 0.0)
        before = before + use * parts[k][:ROWS].astype(F32)
    for k in range(2):
        use = jnp.where(level >= k + 1, (above_docs[k] == before_doc).astype(F32), 0.0)
        before = before + use * aboves[k][:ROWS].astype(F32)
    far_doc = far_ref[ROWS : ROWS + 1]
    after = far_ref[:ROWS] + (before_doc == far_doc).astype(F32) * before

    @pl.when(far_is_mine)
    def _():
        keep_ref[...] = before.astype(BF)
        give_ref[...] = after.astype(BF)
        doc_ref[...] = jnp.broadcast_to(before_doc, (8, DIM))

    @pl.when(jnp.logical_not(far_is_mine))
    def _():
        keep_ref[...] = after.astype(BF)
        give_ref[...] = before.astype(BF)
        doc_ref[...] = jnp.broadcast_to(far_doc, (8, DIM))


def entry_state(place, far, parts, aboves, forward, earlier):
    def kernel(*refs):
        entry_kernel(forward, *refs)

    half = shape((ROWS, DIM), BF)
    return pl.pallas_call(
        kernel,
        out_shape=(half, half, shape((8, DIM), F32)),
        in_specs=[scalars()] + [whole()] * 6 + [anywhere()],
        out_specs=(whole(),) * 3,
        compiler_params=params(4),
        cost_estimate=cost(ROWS * DIM * 12, MIB),
        name="entry_state",
    )(place, far, *parts, *aboves, earlier)


def intra_kernel(q_ref, k_ref, v_ref, docs_ref, earlier, attn_ref, qh_ref, mask):
    n = pl.program_id(0)

    @pl.when(n == 0)
    def _():
        row = jnp.broadcast_to(docs_ref[...], (TOK, TOK))
        t = lax.broadcasted_iota(jnp.int32, (TOK, TOK), 0)
        s = lax.broadcasted_iota(jnp.int32, (TOK, TOK), 1)
        mask[...] = ((t >= s) & (row.T == row)).astype(BF)
        qh_ref[...] = jnp.swapaxes(q_ref[...], 0, 1)

    mid = TOK // 2
    for j in range(2):
        q, k, v = qh_ref[2 * n + j], k_ref[j], v_ref[j]
        for rows, width in ((slice(0, mid), mid), (slice(mid, TOK), TOK)):
            scores = dot(q[rows], k[:width], 1, 1).astype(BF) * mask[rows, :width]
            attn_ref[j, rows] = dot(scores, v[:width], 1, 0)


def intra(queries, kh, vh, docs, earlier):
    pair = pl.BlockSpec((2, TOK, DIM), lambda h: (h, 0, 0))
    return pl.pallas_call(
        intra_kernel,
        grid=(HEADS // 2,),
        out_shape=(shape((HEADS, TOK, DIM), F32), shape((HEADS, TOK, DIM), BF)),
        in_specs=[fixed(TOK, HEADS, DIM), pair, pair, fixed(1, TOK), anywhere()],
        out_specs=(pair, fixed(HEADS, TOK, DIM)),
        scratch_shapes=[pltpu.VMEM((TOK, TOK), BF)],
        compiler_params=params(16),
        cost_estimate=cost(4 * HEADS * TOK * TOK * DIM, 6 * MIB),
        name="intra",
    )(queries, kh, vh, docs, earlier)


def pick_state(c, keep_ref, take_ref, h):
    rows = slice((h % HALF) * DIM, (h % HALF + 1) * DIM)
    mine = c == h // HALF
    return jnp.where(mine, keep_ref[rows], take_ref[rows])


def finish_kernel(place, q_ref, intra_ref, keep_ref, take_ref, doc_ref, docs_ref, w_ref, attn_ref, normed_ref, out_ref):
    @pl.when(pl.program_id(0) == 0)
    def _():
        c = place[2]
        reads = (upright(docs_ref[...], DIM) == doc_ref[:1]).astype(F32)
        for h in range(HEADS):
            state = pick_state(c, keep_ref, take_ref, h)
            attn = intra_ref[h] + reads * dot(q_ref[h], state, 1, 0)
            attn_ref[h] = attn
            scale = lax.rsqrt(jnp.mean(attn * attn, axis=-1, keepdims=True) + 1e-05)
            normed_ref[:, h * DIM : (h + 1) * DIM] = (attn * scale).astype(BF)

    out_ref[...] = jnp.dot(normed_ref[...], w_ref[...], preferred_element_type=F32).astype(BF)


def finish(place, qh, attn_intra, keep, take, doc, docs, weight):
    steps, width = 3, COLS // 3
    return pl.pallas_call(
        finish_kernel,
        grid=(steps,),
        out_shape=(shape((HEADS, TOK, DIM), F32), shape((TOK, FEAT), BF), shape((TOK, COLS), BF)),
        in_specs=[
            scalars(),
            fixed(HEADS, TOK, DIM),
            fixed(HEADS, TOK, DIM),
            fixed(ROWS, DIM),
            fixed(ROWS, DIM),
            fixed(8, DIM),
            fixed(1, TOK),
            pl.BlockSpec((FEAT, width), lambda n: (0, n)),
        ],
        out_specs=(
            fixed(HEADS, TOK, DIM),
            fixed(TOK, FEAT),
            pl.BlockSpec((TOK, width), lambda n: (0, n)),
        ),
        compiler_params=params(28),
        cost_estimate=cost(2 * TOK * FEAT * COLS + 2 * HEADS * TOK * DIM * DIM, 15 * MIB),
        name="finish",
    )(place, qh, attn_intra, keep, take, doc, docs, weight)


def turn_kernel(place, *refs):
    c = place[2]
    halves, (keep_ref, give_ref) = refs[:8], refs[9:]
    mid = TOK // 2
    for r in range(4):
        for j in range(2):
            turned = halves[2 * r + j][...].T.reshape(4, 2, 96, mid)
            tokens = slice(j * mid, (j + 1) * mid)

            @pl.when(c == 0)
            def _():
                keep_ref[r, :, :, tokens] = turned[:, 0]
                give_ref[r, :, :, tokens] = turned[:, 1]

            @pl.when(c == 1)
            def _():
                keep_ref[r, :, :, tokens] = turned[:, 1]
                give_ref[r, :, :, tokens] = turned[:, 0]


def turn(place, halves, earlier):
    out = shape((4, 4, 96, TOK), BF)
    return pl.pallas_call(
        turn_kernel,
        out_shape=(out, out),
        in_specs=[scalars()] + [whole()] * 8 + [anywhere()],
        out_specs=(whole(), whole()),
        compiler_params=params(16),
        cost_estimate=cost(TOK * COLS, 6 * MIB),
        name="turn",
    )(place, *halves, earlier)


def back_kernel(place, *refs):
    halves, (w_ref, attn_ref, q_ref, docs_ref, earlier) = refs[:8], refs[8:13]
    grad_ref, keep_ref, give_ref, own, joined = refs[13:]
    n = pl.program_id(0)
    x = place[3]
    mid = TOK // 2

    @pl.when(n == 0)
    def _():
        for r in range(4):
            spot = pl.multiple_of(lax.rem(x + r, 4) * 768, 768)
            for j in range(2):
                joined[j * mid : (j + 1) * mid, pl.ds(spot, 768)] = halves[2 * r + j][...]

    docs = docs_ref[...]
    first = docs[:, :1]
    lead = (upright(docs, DIM) == first).astype(BF)
    grad_normed = dot(joined[...], w_ref[...], 1, 1)
    for j in range(2):
        attn = attn_ref[j]
        scale = lax.rsqrt(jnp.mean(attn * attn, axis=-1, keepdims=True) + 1e-05)
        normed = attn * scale
        grad = grad_normed[:, j * DIM : (j + 1) * DIM]
        grad = scale * (grad - normed * jnp.mean(grad * normed, axis=-1, keepdims=True))
        grad = grad.astype(BF)
        grad_ref[j] = grad
        spot = pl.multiple_of(lax.rem(n, 2) * 2 * DIM + j * DIM, DIM)
        own[n // 2, pl.ds(spot, DIM)] = dot(q_ref[j] * lead, grad, 0, 0)

    @pl.when(n == pl.num_programs(0) - 1)
    def _():
        c = place[2]
        keep_ref[:ROWS] = own[c]
        give_ref[:ROWS] = own[1 - c]
        doc_rows = jnp.broadcast_to(first, (8, DIM))
        keep_ref[ROWS:] = doc_rows
        give_ref[ROWS:] = doc_rows


def back(place, halves, weight, attn, qh, docs, earlier):
    pair = pl.BlockSpec((2, TOK, DIM), lambda n: (n, 0, 0))
    half = shape((ROWS + 8, DIM), F32)
    return pl.pallas_call(
        back_kernel,
        grid=(HEADS // 2,),
        out_shape=(shape((HEADS, TOK, DIM), BF), half, half),
        in_specs=[scalars()]
        + [fixed(TOK // 2, 768)] * 8
        + [pl.BlockSpec((2 * DIM, COLS), lambda n: (n, 0)), pair, pair, fixed(1, TOK), anywhere()],
        out_specs=(pair, fixed(ROWS + 8, DIM), fixed(ROWS + 8, DIM)),
        scratch_shapes=[pltpu.VMEM((2, ROWS, DIM), F32), pltpu.VMEM((TOK, COLS), BF)],
        compiler_params=params(28),
        cost_estimate=cost(2 * TOK * FEAT * COLS + 2 * HEADS * TOK * DIM * DIM, 15 * MIB),
        name="back",
    )(place, *halves, weight, attn, qh, docs, earlier)


def block_rows(place, keep_ref, got_ref, a):
    y, z, c, x = place[0], place[1], place[2], place[3]
    rows = []
    for b in range(4):
        to_y = lax.rem(y + jnp.where(c == 0, a, b), 4)
        to_z = lax.rem(z + jnp.where(c == 0, b, a), 4)
        r = lax.rem(to_y + 4 - x, 4)
        rows.append(jnp.concatenate([keep_ref[r, to_z], got_ref[r, to_z]], 1))
    return jnp.concatenate(rows, 0)


def far_terms_kernel(place, keep_ref, got_ref, normed_ref, normed2_ref, up_ref, down_ref):
    rows = block_rows(place, keep_ref, got_ref, 2)
    total = dot(rows[:, :TOK], normed_ref[...], 1, 0) + dot(rows[:, TOK:], normed2_ref[...], 1, 0)
    up_ref[...] = total[:192].astype(BF)
    down_ref[...] = total[192:].astype(BF)


def far_terms(place, keep, got, normed, normed2):
    out = shape((192, FEAT), BF)
    return pl.pallas_call(
        far_terms_kernel,
        out_shape=(out, out),
        in_specs=[scalars()] + [whole()] * 4,
        out_specs=(whole(), whole()),
        compiler_params=params(16),
        cost_estimate=cost(TOK * FEAT * COLS // 2, 6 * MIB),
        name="far_terms",
    )(place, keep, got, normed, normed2)


def near_terms_kernel(place, keep_ref, got_ref, normed_ref, normed2_ref, earlier, out_ref):
    n = pl.program_id(0)
    rows = block_rows(place, keep_ref, got_ref, jnp.where(n == 0, 1, jnp.where(n == 1, 3, 0)))
    out_ref[...] = dot(rows[:, :TOK], normed_ref[...], 1, 0) + dot(rows[:, TOK:], normed2_ref[...], 1, 0)


def near_terms(place, keep, got, normed, normed2, earlier):
    blocks = fixed(4, 4, 96, TOK)
    return pl.pallas_call(
        near_terms_kernel,
        grid=(3,),
        out_shape=shape((3, 384, FEAT), F32),
        in_specs=[scalars(), blocks, blocks, fixed(TOK, FEAT), fixed(TOK, FEAT), anywhere()],
        out_specs=pl.BlockSpec((pl.squeezed, 384, FEAT), lambda n: (n, 0, 0)),
        compiler_params=params(24),
        cost_estimate=cost(3 * TOK * FEAT * COLS // 2, 10 * MIB),
        name="near_terms",
    )(place, keep, got, normed, normed2, earlier)


def inner_kernel(group, place, q_ref, k_ref, v_ref, grad_ref, keep_ref, take_ref, doc_ref, docs_ref, earlier, gq_ref, gk_ref, gv_ref, mask, turned):
    n = pl.program_id(0)

    @pl.when(n == 0)
    def _():
        row = jnp.broadcast_to(docs_ref[...], (TOK, TOK))
        same = row.T == row
        t = lax.broadcasted_iota(jnp.int32, (TOK, TOK), 0)
        s = lax.broadcasted_iota(jnp.int32, (TOK, TOK), 1)
        mask[...] = ((t >= s) & same).astype(BF)
        turned[...] = ((s >= t) & same).astype(BF)

    c = place[2]
    reads = (upright(docs_ref[...], DIM) == doc_ref[:1]).astype(F32)
    mid = TOK // 2
    for j in range(2):
        q, k, v, grad = q_ref[j], k_ref[j], v_ref[j], grad_ref[j]
        spot = pl.multiple_of((n * 2 + j) * DIM, DIM)
        state = jnp.where(c == group, keep_ref[pl.ds(spot, DIM)], take_ref[pl.ds(spot, DIM)])
        across = reads * dot(grad, state, 1, 1)
        for rows, width in ((slice(0, mid), mid), (slice(mid, TOK), TOK)):
            scores = dot(grad[rows], v[:width], 1, 1).astype(BF) * mask[rows, :width]
            gq_ref[j, rows] = (dot(scores, k[:width], 1, 0) + across[rows]).astype(BF)
        for rows, start in ((slice(0, mid), 0), (slice(mid, TOK), mid)):
            scores = dot(v[rows], grad[start:], 1, 1).astype(BF) * turned[rows, start:]
            gk_ref[j, rows] = dot(scores, q[start:], 1, 0)
            scores = dot(k[rows], q[start:], 1, 1).astype(BF) * turned[rows, start:]
            gv_ref[j, rows] = dot(scores, grad[start:], 1, 0)


def inner(group, place, qh, kh, vh, grad, keep, take, doc, docs, earlier):
    def kernel(*refs):
        inner_kernel(group, *refs)

    head = pl.BlockSpec((2, TOK, DIM), lambda n: (n + group * HALF // 2, 0, 0))
    out = pl.BlockSpec((2, TOK, DIM), lambda n: (n, 0, 0))
    return pl.pallas_call(
        kernel,
        grid=(HALF // 2,),
        out_shape=(shape((HALF, TOK, DIM), BF),) + (shape((HALF, TOK, DIM), F32),) * 2,
        in_specs=[scalars()]
        + [head] * 4
        + [fixed(ROWS, DIM)] * 2
        + [fixed(8, DIM), fixed(1, TOK), anywhere()],
        out_specs=(out, out, out),
        scratch_shapes=[pltpu.VMEM((TOK, TOK), BF), pltpu.VMEM((TOK, TOK), BF)],
        compiler_params=params(20),
        cost_estimate=cost(5 * HEADS * TOK * TOK * DIM, 5 * MIB),
        name="inner",
    )(place, qh, kh, vh, grad, keep, take, doc, docs, earlier)


def last_kernel(place, k_ref, v_ref, gq0, gk0, gv0, gq1, gk1, gv1, keep_ref, take_ref, doc_ref, docs_ref, out_q, out_k, out_v, held_k, held_v):
    c = place[2]
    writes = (upright(docs_ref[...], DIM) == doc_ref[:1]).astype(F32)
    for h in range(HEADS):
        state = pick_state(c, keep_ref, take_ref, h)
        gk, gv = ((gk0, gv0), (gk1, gv1))[h // HALF]
        held_k[h] = (gk[h % HALF] + writes * dot(v_ref[h], state, 1, 1)).astype(BF)
        held_v[h] = (gv[h % HALF] + writes * dot(k_ref[h], state, 1, 0)).astype(BF)
    out_q[...] = jnp.swapaxes(jnp.concatenate([gq0[...], gq1[...]], 0), 0, 1)
    out_k[...] = jnp.swapaxes(held_k[...], 0, 1)
    out_v[...] = jnp.swapaxes(held_v[...], 0, 1)


def last(place, kh, vh, lower, upper, keep, take, doc, docs):
    out = shape((TOK, HEADS, DIM), BF)
    return pl.pallas_call(
        last_kernel,
        out_shape=(out, out, out),
        in_specs=[scalars()] + [whole()] * 12,
        out_specs=(whole(),) * 3,
        scratch_shapes=[pltpu.VMEM((HEADS, TOK, DIM), BF)] * 2,
        compiler_params=params(24),
        cost_estimate=cost(4 * HEADS * TOK * DIM * DIM, 9 * MIB),
        name="last",
    )(place, kh, vh, *lower, *upper, keep, take, doc, docs)


def pass_kernel(terms_ref, up_ref, down_ref, out_right, out_left):
    rows = up_ref.shape[0]
    out_right[:rows] = (terms_ref[0, :rows] + up_ref[...].astype(F32)).astype(BF)
    out_right[rows:] = terms_ref[0, rows:].astype(BF)
    out_left[:rows] = terms_ref[1, :rows].astype(BF)
    out_left[rows:] = (terms_ref[1, rows:] + down_ref[...].astype(F32)).astype(BF)


def pass_on(terms, up, down):
    out = shape((384, FEAT), BF)
    return pl.pallas_call(
        pass_kernel,
        grid=(1,),
        out_shape=(out, out),
        in_specs=[pl.BlockSpec((2, 384, FEAT), lambda n: (0, 0, 0)), fixed(192, FEAT), fixed(192, FEAT)],
        out_specs=(fixed(384, FEAT), fixed(384, FEAT)),
        compiler_params=params(16),
        cost_estimate=cost(384 * FEAT * 2, 5 * MIB),
        name="pass_on",
    )(terms, up, down)


def middle_kernel(own_ref, left_ref, right_ref, own_out, *outs):
    total = own_ref[...] + left_ref[...].astype(F32) + right_ref[...].astype(F32)
    own_out[...] = total[:96]
    for b in (1, 2, 3):
        outs[b - 1][...] = total[96 * b : 96 * (b + 1)].astype(BF)


def middle(terms, from_left, from_right):
    small = shape((96, FEAT), BF)
    return pl.pallas_call(
        middle_kernel,
        grid=(1,),
        out_shape=(shape((96, FEAT), F32), small, small, small),
        in_specs=[
            pl.BlockSpec((pl.squeezed, 384, FEAT), lambda n: (2, 0, 0)),
            fixed(384, FEAT),
            fixed(384, FEAT),
        ],
        out_specs=(fixed(96, FEAT),) * 4,
        compiler_params=params(16),
        cost_estimate=cost(384 * FEAT * 2, 4 * MIB),
        name="middle",
    )(terms, from_left, from_right)


def end_kernel(own_ref, p1, p2, p3, out_ref):
    out_ref[...] = own_ref[...] + p1[...].astype(F32) + p2[...].astype(F32) + p3[...].astype(F32)


def end(own, parts):
    return pl.pallas_call(
        end_kernel,
        grid=(1,),
        out_shape=shape((96, FEAT), F32),
        in_specs=[fixed(96, FEAT)] * 4,
        out_specs=fixed(96, FEAT),
        compiler_params=params(8),
        cost_estimate=cost(96 * FEAT * 3, MIB),
        name="end",
    )(own, *parts)


def route(move):
    pairs = []
    for i in range(32):
        target = move(i // 8, (i // 2) % 4, i % 2)
        if target is not None:
            y, z, c = target
            pairs.append((i, ((y % 4) * 4 + z % 4) * 2 + c))
    return pairs


SWAP = route(lambda y, z, c: (y, z, 1 - c))


def along_z(step):
    return route(lambda y, z, c: (y, z + step, c))


def along_y_open(step):
    return route(lambda y, z, c: (y + step, z, c) if 0 <= y + step < 4 else None)


def along_first(step):
    return route(lambda y, z, c: (y + step, z, c) if c == 0 else (y, z + step, c))


def along_second(step):
    return route(lambda y, z, c: (y, z + step, c) if c == 0 else (y + step, z, c))


def send(array, pairs):
    return lax.ppermute(array, "seq", pairs)


def along_head(array, step):
    return lax.ppermute(array, "head", [(i, (i + step) % 4) for i in range(4)])


def gather_halves(block):
    mid = block.shape[0] // 2
    top, bottom = block[:mid], block[mid:]
    back_top, on_bottom = along_head(top, 1), along_head(bottom, -1)
    back_bottom, on_top = along_head(bottom, 1), along_head(top, -1)
    far_top, far_bottom = along_head(back_top, 1), along_head(on_bottom, -1)
    return [top, bottom, on_top, on_bottom, far_top, far_bottom, back_top, back_bottom]


def shards(queries, key_vectors, value_vectors, doc_ids, out_weight, grad_out):
    i = lax.axis_index("seq")
    place = jnp.stack([i // 8, (i // 2) % 4, i % 2, lax.axis_index("head")]).astype(jnp.int32)
    docs = doc_ids.astype(F32).reshape(1, TOK)
    halves = gather_halves(grad_out)

    kh, vh, keep, give = prepare(place, key_vectors, value_vectors, docs)
    far, chip = chip_state(place, keep, send(give, SWAP), True, docs)
    parts = [send(chip, along_z(k)) for k in (1, 2, 3)]
    attn_intra, qh = intra(queries, kh, vh, docs, far)
    total = row_state(place, [chip] + parts, True, qh)
    aboves = [send(total, along_y_open(k)) for k in (1, 2)]
    mine, theirs, doc = entry_state(place, far, parts, aboves, True, docs)
    taken = send(theirs, SWAP)
    attn, normed, partial_out = finish(place, qh, attn_intra, mine, taken, doc, docs, out_weight)
    layer_out = lax.psum_scatter(partial_out, "head", scatter_dimension=1, tiled=True)
    normed2 = send(normed, SWAP)

    blocks, others = turn(place, halves, normed)
    blocks2 = send(others, SWAP)
    grad, keep, give = back(place, halves, out_weight, attn, qh, docs, others)
    got = send(give, SWAP)
    up, down = far_terms(place, blocks, blocks2, normed, normed2)
    up, down = send(up, along_first(1)), send(down, along_first(-1))
    far, chip = chip_state(place, keep, got, False, up)
    parts = [send(chip, along_z(-k)) for k in (1, 2, 3)]
    terms = near_terms(place, blocks, blocks2, normed, normed2, far)
    right, left = pass_on(terms, up, down)
    right, left = send(right, along_first(1)), send(left, along_first(-1))
    lower = inner(0, place, qh, kh, vh, grad, mine, taken, doc, docs, terms)
    total = row_state(place, [chip] + parts, False, terms)
    aboves = [send(total, along_y_open(-k)) for k in (1, 2)]
    upper = inner(1, place, qh, kh, vh, grad, mine, taken, doc, docs, total)
    back_mine, theirs, back_doc = entry_state(place, far, parts, aboves, False, lower[0])
    back_taken = send(theirs, SWAP)
    own, *shares = middle(terms, right, left)
    shares = [send(share, along_second(k)) for k, share in zip((1, 2, 3), shares)]
    grad_queries, grad_keys, grad_values = last(
        place, kh, vh, lower, upper, back_mine, back_taken, back_doc, docs
    )
    grad_weight = end(own, shares).T
    return layer_out, grad_queries, grad_keys, grad_values, grad_weight


def solution(mesh):
    placed = (
        P("seq", "head", None),
        P("seq", "head", None),
        P("seq", "head", None),
        P("seq"),
        P("head", None),
        P("seq", "head"),
    )
    return jax.shard_map(
        shards,
        mesh=mesh,
        in_specs=placed,
        out_specs=(
            P("seq", "head"),
            P("seq", "head", None),
            P("seq", "head", None),
            P("seq", "head", None),
            P("head", "seq"),
        ),
        check_vma=False,
    )
```

```python
import jax
import jax.numpy as jnp
from jax import lax
from jax.experimental import pallas as pl
from jax.experimental.pallas import tpu as pltpu
from jax.sharding import PartitionSpec as P

BF = jnp.bfloat16
F32 = jnp.float32
TOK, HEADS, DIM, FEAT, COLS = 512, 8, 128, 1024, 3072
HALF = HEADS // 2
ROWS = HALF * DIM
MIB = 2**20


def shape(dims, dtype):
    return jax.ShapeDtypeStruct(dims, dtype)


def whole():
    return pl.BlockSpec(memory_space=pltpu.VMEM)


def scalars():
    return pl.BlockSpec(memory_space=pltpu.SMEM)


def params(mib):
    return pltpu.CompilerParams(vmem_limit_bytes=mib * MIB)


def cost(flops, moved):
    return pl.CostEstimate(flops=flops, bytes_accessed=moved, transcendentals=0)


def dot(a, b, ca, cb):
    return lax.dot_general(a, b, (((ca,), (cb,)), ((), ())), preferred_element_type=F32)


def fixed(*dims):
    return pl.BlockSpec(dims, lambda n: (0,) * len(dims))


def in_hbm():
    return pl.BlockSpec(memory_space=pltpu.HBM)


def anywhere():
    return pl.BlockSpec(memory_space=pl.ANY)


def upright(docs_row, width):
    docs_row = docs_row.astype(F32)
    return jnp.broadcast_to(docs_row, (width, docs_row.shape[1])).T


def prepare_kernel(place, q_hbm, k_hbm, v_hbm, docs_hbm, qh_ref, kh_ref, vh_ref, keep_ref, give_ref, q_buf, k_buf, v_buf, docs_buf, own, sems, docs_sem):
    steps = k_buf.shape[0]
    rows = TOK // steps

    def fetch(n, source, target, sem):
        copy = pltpu.make_async_copy(source.at[n * rows : (n + 1) * rows], target.at[n], sem)
        copy.start()
        return copy

    docs_copy = pltpu.make_async_copy(docs_hbm, docs_buf, docs_sem)
    docs_copy.start()
    copies = []
    for n in range(steps):
        copies.append(fetch(n, k_hbm, k_buf, sems.at[0, n]))
        copies.append(fetch(n, v_hbm, v_buf, sems.at[1, n]))
    q_copies = [fetch(n, q_hbm, q_buf, sems.at[2, n]) for n in range(steps)]
    c = place[2]
    docs_copy.wait()
    docs = docs_buf[...].astype(F32)
    last = docs[:, TOK - 1 :]
    tail = (upright(docs, DIM) == last).astype(BF)
    for n in range(steps):
        span = slice(n * rows, (n + 1) * rows)
        copies[2 * n].wait()
        copies[2 * n + 1].wait()
        kh = jnp.swapaxes(k_buf[n], 0, 1)
        vh = jnp.swapaxes(v_buf[n], 0, 1)
        kh_ref[:, span] = kh
        vh_ref[:, span] = vh
        for h in range(HEADS):
            part = dot(kh[h] * tail[span], vh[h], 0, 0)
            spot = slice((h % HALF) * DIM, (h % HALF + 1) * DIM)
            if n == 0:
                own[h // HALF, spot] = part
            else:
                own[h // HALF, spot] += part
    keep_ref[:ROWS] = own[c]
    give_ref[:ROWS] = own[1 - c]
    doc_rows = jnp.broadcast_to(last, (8, DIM))
    keep_ref[ROWS:] = doc_rows
    give_ref[ROWS:] = doc_rows
    for n in range(steps):
        q_copies[n].wait()
        qh_ref[:, n * rows : (n + 1) * rows] = jnp.swapaxes(q_buf[n], 0, 1)


def prepare(place, queries, keys, values, docs):
    steps = 2
    head_major = shape((HEADS, TOK, DIM), BF)
    half = shape((ROWS + 8, DIM), F32)
    buffer = pltpu.VMEM((steps, TOK // steps, HEADS, DIM), BF)
    return pl.pallas_call(
        prepare_kernel,
        out_shape=(head_major, head_major, head_major, half, half),
        in_specs=[scalars()] + [in_hbm()] * 4,
        out_specs=(whole(),) * 5,
        scratch_shapes=[
            buffer,
            buffer,
            buffer,
            pltpu.VMEM((1, TOK), jnp.int32),
            pltpu.VMEM((2, ROWS, DIM), F32),
            pltpu.SemaphoreType.DMA((3, steps)),
            pltpu.SemaphoreType.DMA,
        ],
        compiler_params=params(12),
        cost_estimate=cost(2 * HEADS * TOK * DIM * DIM, 6 * MIB),
        name="prepare",
    )(place, *[pltpu.with_memory_space_constraint(a, pltpu.HBM) for a in (queries, keys, values, docs)])


def chip_kernel(forward, place, keep_ref, got_ref, *rest):
    far_ref, chip_ref = rest[-2:]
    c = place[2]
    far_is_mine = (c == 0) if forward else (c == 1)

    def write(far, near):
        same = (far[ROWS : ROWS + 1] == near[ROWS : ROWS + 1]).astype(F32)
        far_ref[...] = far[...]
        chip_ref[:ROWS] = (near[:ROWS] + same * far[:ROWS]).astype(BF)
        chip_ref[ROWS:] = jnp.broadcast_to(near[ROWS : ROWS + 1], (16, DIM)).astype(BF)

    @pl.when(far_is_mine)
    def _():
        write(keep_ref, got_ref)

    @pl.when(jnp.logical_not(far_is_mine))
    def _():
        write(got_ref, keep_ref)


def chip_state(place, keep, got, forward, *earlier):
    def kernel(*refs):
        chip_kernel(forward, *refs)

    return pl.pallas_call(
        kernel,
        out_shape=(shape((ROWS + 8, DIM), F32), shape((ROWS + 16, DIM), BF)),
        in_specs=[scalars(), whole(), whole()] + [anywhere()] * len(earlier),
        out_specs=(whole(), whole()),
        compiler_params=params(4),
        cost_estimate=cost(ROWS * DIM * 3, MIB),
        name="chip_state",
    )(place, keep, got, *earlier)


def spot_of(place, forward, step):
    spot = lax.rem(place[1] // step, 2)
    return spot if forward else 1 - spot


def join_kernel(forward, step, place, own_ref, other_ref, *rest):
    out_ref = rest[-1]
    first = spot_of(place, forward, step) == 0

    def write(early, late):
        doc = late[ROWS : ROWS + 1]
        same = (early[ROWS : ROWS + 1] == doc).astype(F32)
        total = late[:ROWS].astype(F32) + same * early[:ROWS].astype(F32)
        out_ref[:ROWS] = total.astype(BF)
        out_ref[ROWS:] = jnp.broadcast_to(doc, (16, DIM))

    @pl.when(first)
    def _():
        write(own_ref, other_ref)

    @pl.when(jnp.logical_not(first))
    def _():
        write(other_ref, own_ref)


def join(place, own, other, forward, step, *earlier):
    def kernel(*refs):
        join_kernel(forward, step, *refs)

    return pl.pallas_call(
        kernel,
        out_shape=shape((ROWS + 16, DIM), BF),
        in_specs=[scalars()] + [whole()] * 2 + [anywhere()] * len(earlier),
        out_specs=whole(),
        compiler_params=params(4),
        cost_estimate=cost(ROWS * DIM * 3, MIB),
        name="join",
    )(place, own, other, *earlier)


def entry_kernel(forward, place, far_ref, p1, p2, above1, above2, *rest):
    keep_ref, give_ref, doc_ref = rest[-3:]
    y, c = place[0], place[2]
    level = y if forward else 3 - y
    far_is_mine = (c == 0) if forward else (c == 1)
    parts = (p1, p2)
    inside = [spot_of(place, forward, step) == 1 for step in (1, 2)]
    aboves = (above1, above2)
    docs = [p[ROWS : ROWS + 1].astype(F32) for p in parts]
    above_docs = [
        jnp.where(level >= k + 1, aboves[k][ROWS : ROWS + 1].astype(F32), -1.0) for k in range(2)
    ]
    before_doc = jnp.where(inside[0], docs[0], jnp.where(inside[1], docs[1], above_docs[0]))
    before = jnp.zeros((ROWS, DIM), F32)
    for k in range(2):
        use = jnp.where(inside[k], (docs[k] == before_doc).astype(F32), 0.0)
        before = before + use * parts[k][:ROWS].astype(F32)
    for k in range(2):
        use = jnp.where(level >= k + 1, (above_docs[k] == before_doc).astype(F32), 0.0)
        before = before + use * aboves[k][:ROWS].astype(F32)
    far_doc = far_ref[ROWS : ROWS + 1]
    after = far_ref[:ROWS] + (before_doc == far_doc).astype(F32) * before

    @pl.when(far_is_mine)
    def _():
        keep_ref[...] = before.astype(BF)
        give_ref[...] = after.astype(BF)
        doc_ref[...] = jnp.broadcast_to(before_doc, (8, DIM))

    @pl.when(jnp.logical_not(far_is_mine))
    def _():
        keep_ref[...] = after.astype(BF)
        give_ref[...] = before.astype(BF)
        doc_ref[...] = jnp.broadcast_to(far_doc, (8, DIM))


def entry_state(place, far, parts, aboves, forward, *earlier):
    def kernel(*refs):
        entry_kernel(forward, *refs)

    half = shape((ROWS, DIM), BF)
    return pl.pallas_call(
        kernel,
        out_shape=(half, half, shape((8, DIM), F32)),
        in_specs=[scalars()] + [whole()] * 5 + [anywhere()] * len(earlier),
        out_specs=(whole(),) * 3,
        compiler_params=params(4),
        cost_estimate=cost(ROWS * DIM * 10, MIB),
        name="entry_state",
    )(place, far, *parts, *aboves, *earlier)


def causal(docs_ref):
    row = jnp.broadcast_to(docs_ref[...].astype(F32), (TOK, TOK))
    t = lax.broadcasted_iota(jnp.int32, (TOK, TOK), 0)
    s = lax.broadcasted_iota(jnp.int32, (TOK, TOK), 1)
    same = row.T == row
    return (t >= s) & same, (s >= t) & same


def intra_kernel(q_ref, k_ref, v_ref, docs_ref, *rest):
    attn_ref, mask = rest[-2:]
    mask[...] = causal(docs_ref)[0].astype(BF)
    mid = TOK // 2
    for h in range(q_ref.shape[0]):
        for rows, width in ((slice(0, mid), mid), (slice(mid, TOK), TOK)):
            scores = dot(q_ref[h, rows], k_ref[h, :width], 1, 1).astype(BF) * mask[rows, :width]
            attn_ref[h, rows] = dot(scores, v_ref[h, :width], 1, 0)


def intra(qh, kh, vh, docs, group, *earlier):
    part = pl.BlockSpec((HALF, TOK, DIM), lambda n: (group, 0, 0))
    return pl.pallas_call(
        intra_kernel,
        grid=(1,),
        out_shape=shape((HALF, TOK, DIM), F32),
        in_specs=[part, part, part, fixed(1, TOK)] + [anywhere()] * len(earlier),
        out_specs=fixed(HALF, TOK, DIM),
        scratch_shapes=[pltpu.VMEM((TOK, TOK), BF)],
        compiler_params=params(14),
        cost_estimate=cost(2 * HEADS * TOK * TOK * DIM, 3 * MIB),
        name="intra",
    )(qh, kh, vh, docs, *earlier)


def pick_state(c, keep_ref, take_ref, h):
    rows = slice((h % HALF) * DIM, (h % HALF + 1) * DIM)
    mine = c == h // HALF
    return jnp.where(mine, keep_ref[rows], take_ref[rows])


def attend_kernel(place, q_ref, intra0, intra1, keep_ref, take_ref, doc_ref, docs_ref, *rest):
    attn_ref, normed_ref = rest[-2:]
    c = place[2]
    reads = (upright(docs_ref[...], DIM) == doc_ref[:1]).astype(F32)
    for h in range(HEADS):
        state = pick_state(c, keep_ref, take_ref, h)
        attn = (intra0, intra1)[h // HALF][h % HALF] + reads * dot(q_ref[h], state, 1, 0)
        attn_ref[h] = attn
        scale = lax.rsqrt(jnp.mean(attn * attn, axis=-1, keepdims=True) + 1e-05)
        normed_ref[:, h * DIM : (h + 1) * DIM] = (attn * scale).astype(BF)


def attend(place, qh, intra0, intra1, keep, take, doc, docs, *earlier):
    return pl.pallas_call(
        attend_kernel,
        out_shape=(shape((HEADS, TOK, DIM), F32), shape((TOK, FEAT), BF)),
        in_specs=[scalars()] + [whole()] * 7 + [anywhere()] * len(earlier),
        out_specs=(whole(), whole()),
        compiler_params=params(8),
        cost_estimate=cost(2 * HEADS * TOK * DIM * DIM, 6 * MIB),
        name="attend",
    )(place, qh, intra0, intra1, keep, take, doc, docs, *earlier)


def project_kernel(place, normed_ref, w_hbm, *rest):
    top_ref, bottom_ref, right_ref, left_ref, own_ref, w_buf, sems = rest[-7:]
    x = place[3]
    mid = TOK // 2
    copies = []
    for n, r in enumerate((2, 1, 3, 0)):
        spot = pl.multiple_of(lax.rem(x + r, 4) * 768, 768)
        copies.append(pltpu.make_async_copy(w_hbm.at[:, pl.ds(spot, 768)], w_buf.at[n], sems.at[n]))
        copies[n].start()
    for n in range(4):
        copies[n].wait()
        part = jnp.dot(normed_ref[...], w_buf[n], preferred_element_type=F32)
        if n == 0:
            top_ref[...] = part[:mid].astype(BF)
            bottom_ref[...] = part[mid:].astype(BF)
        elif n < 3:
            (right_ref, left_ref)[n - 1][...] = part.astype(BF)
        else:
            own_ref[...] = part


def project(place, normed, weight, *earlier):
    part, half = shape((TOK, 768), BF), shape((TOK // 2, 768), BF)
    return pl.pallas_call(
        project_kernel,
        out_shape=(half, half, part, part, shape((TOK, 768), F32)),
        in_specs=[scalars(), whole(), in_hbm()] + [anywhere()] * len(earlier),
        out_specs=(whole(),) * 5,
        scratch_shapes=[pltpu.VMEM((4, FEAT, 768), BF), pltpu.SemaphoreType.DMA((4,))],
        compiler_params=params(14),
        cost_estimate=cost(2 * TOK * FEAT * COLS, 10 * MIB),
        name="project",
    )(place, normed, weight, *earlier)


def halves_kernel(left_ref, right_ref, *rest):
    top_ref, bottom_ref = rest[-2:]
    mid = TOK // 2
    top_ref[...] = left_ref[:mid]
    bottom_ref[...] = right_ref[mid:]


def halves(left, right, *earlier):
    out = shape((TOK // 2, 768), BF)
    return pl.pallas_call(
        halves_kernel,
        out_shape=(out, out),
        in_specs=[whole()] * 2 + [anywhere()] * len(earlier),
        out_specs=(whole(),) * 2,
        compiler_params=params(6),
        cost_estimate=cost(TOK * 768, 2 * MIB),
        name="halves",
    )(left, right, *earlier)


def out_pass_kernel(right_ref, left_ref, top_ref, bottom_ref, *rest):
    out_right, out_left = rest[-2:]
    mid = TOK // 2
    out_right[:mid] = (right_ref[:mid].astype(F32) + top_ref[...].astype(F32)).astype(BF)
    out_right[mid:] = right_ref[mid:]
    out_left[:mid] = left_ref[:mid]
    out_left[mid:] = (left_ref[mid:].astype(F32) + bottom_ref[...].astype(F32)).astype(BF)


def out_pass(right, left, top, bottom, *earlier):
    part = shape((TOK, 768), BF)
    return pl.pallas_call(
        out_pass_kernel,
        out_shape=(part, part),
        in_specs=[whole()] * 4 + [anywhere()] * len(earlier),
        out_specs=(whole(), whole()),
        compiler_params=params(6),
        cost_estimate=cost(TOK * 768, 4 * MIB),
        name="out_pass",
    )(right, left, top, bottom, *earlier)


def out_end_kernel(own_ref, left_ref, right_ref, *rest):
    total = own_ref[...] + left_ref[...].astype(F32) + right_ref[...].astype(F32)
    rest[-1][...] = total.astype(BF)


def out_end(own, from_left, from_right, *earlier):
    return pl.pallas_call(
        out_end_kernel,
        out_shape=shape((TOK, 768), BF),
        in_specs=[whole()] * 3 + [anywhere()] * len(earlier),
        out_specs=whole(),
        compiler_params=params(6),
        cost_estimate=cost(2 * TOK * 768, 4 * MIB),
        name="out_end",
    )(own, from_left, from_right, *earlier)


def turn_kernel(place, own_hbm, right_ref, top_ref, bottom_ref, left_ref, *rest):
    joined_ref, keep_ref, give_ref, sem = rest[-4:]
    c, x = place[2], place[3]
    mid = TOK // 2
    spots = [pl.multiple_of(lax.rem(x + r, 4) * 768, 768) for r in range(4)]
    copy = pltpu.make_async_copy(own_hbm, joined_ref.at[:, pl.ds(spots[0], 768)], sem)
    copy.start()

    def place_block(r, block, tokens):
        turned = block.T.reshape(4, 2, 96, block.shape[0])
        low, high = turned[:, 0], turned[:, 1]
        keep_ref[r, :, :, tokens] = jnp.where(c == 0, low, high)
        give_ref[r, :, :, tokens] = jnp.where(c == 0, high, low)

    for r, ref, tokens in (
        (1, right_ref, slice(0, TOK)),
        (3, left_ref, slice(0, TOK)),
        (2, top_ref, slice(0, mid)),
        (2, bottom_ref, slice(mid, TOK)),
    ):
        block = ref[...]
        joined_ref[tokens, pl.ds(spots[r], 768)] = block
        place_block(r, block, tokens)
    copy.wait()
    place_block(0, joined_ref[:, pl.ds(spots[0], 768)], slice(0, TOK))


def turn(place, own, right, top, bottom, left, *earlier):
    out = shape((4, 4, 96, TOK), BF)
    return pl.pallas_call(
        turn_kernel,
        out_shape=(shape((TOK, COLS), BF), out, out),
        in_specs=[scalars(), in_hbm()] + [whole()] * 4 + [anywhere()] * len(earlier),
        out_specs=(whole(),) * 3,
        scratch_shapes=[pltpu.SemaphoreType.DMA],
        compiler_params=params(8),
        cost_estimate=cost(TOK * COLS, 6 * MIB),
        name="turn",
    )(place, pltpu.with_memory_space_constraint(own, pltpu.HBM), right, top, bottom, left, *earlier)


def back_kernel(place, cot_ref, w_hbm, attn_ref, q_ref, docs_ref, *rest):
    grad_ref, keep_ref, give_ref, own, w_buf, sems = rest[-6:]
    c = place[2]
    pairs = HEADS // 2
    copies = [
        pltpu.make_async_copy(w_hbm.at[n * 2 * DIM : (n + 1) * 2 * DIM], w_buf.at[n], sems.at[n])
        for n in range(pairs)
    ]
    for copy in copies:
        copy.start()
    docs = docs_ref[...].astype(F32)
    first = docs[:, :1]
    lead = (upright(docs, DIM) == first).astype(BF)
    for n in range(pairs):
        copies[n].wait()
        grad_normed = dot(cot_ref[...], w_buf[n], 1, 1)
        for j in range(2):
            h = 2 * n + j
            attn = attn_ref[h]
            scale = lax.rsqrt(jnp.mean(attn * attn, axis=-1, keepdims=True) + 1e-05)
            normed = attn * scale
            grad = grad_normed[:, j * DIM : (j + 1) * DIM]
            grad = scale * (grad - normed * jnp.mean(grad * normed, axis=-1, keepdims=True))
            grad = grad.astype(BF)
            grad_ref[h] = grad
            spot = slice((h % HALF) * DIM, (h % HALF + 1) * DIM)
            own[h // HALF, spot] = dot(q_ref[h] * lead, grad, 0, 0)
    keep_ref[:ROWS] = own[c]
    give_ref[:ROWS] = own[1 - c]
    doc_rows = jnp.broadcast_to(first, (8, DIM))
    keep_ref[ROWS:] = doc_rows
    give_ref[ROWS:] = doc_rows


def back(place, cotangent, weight, attn, qh, docs, *earlier):
    half = shape((ROWS + 8, DIM), F32)
    return pl.pallas_call(
        back_kernel,
        out_shape=(shape((HEADS, TOK, DIM), BF), half, half),
        in_specs=[scalars(), whole(), in_hbm()] + [whole()] * 3 + [anywhere()] * len(earlier),
        out_specs=(whole(),) * 3,
        scratch_shapes=[
            pltpu.VMEM((2, ROWS, DIM), F32),
            pltpu.VMEM((HEADS // 2, 2 * DIM, COLS), BF),
            pltpu.SemaphoreType.DMA((HEADS // 2,)),
        ],
        compiler_params=params(14),
        cost_estimate=cost(2 * TOK * FEAT * COLS + 2 * HEADS * TOK * DIM * DIM, 15 * MIB),
        name="back",
    )(place, cotangent, weight, attn, qh, docs, *earlier)


def block_rows(place, keep_ref, got_ref, a):
    y, z, c, x = place[0], place[1], place[2], place[3]
    rows = []
    for b in range(4):
        to_y = lax.rem(y + jnp.where(c == 0, a, b), 4)
        to_z = lax.rem(z + jnp.where(c == 0, b, a), 4)
        r = lax.rem(to_y + 4 - x, 4)
        rows.append(jnp.concatenate([keep_ref[r, to_z], got_ref[r, to_z]], 1))
    return jnp.concatenate(rows, 0)


def far_terms_kernel(place, keep_ref, got_ref, normed_ref, normed2_ref, *rest):
    up_ref, down_ref = rest[-2:]
    rows = block_rows(place, keep_ref, got_ref, 2)
    total = dot(rows[:, :TOK], normed_ref[...], 1, 0) + dot(rows[:, TOK:], normed2_ref[...], 1, 0)
    up_ref[...] = total[:192].astype(BF)
    down_ref[...] = total[192:].astype(BF)


def far_terms(place, keep, got, normed, normed2, *earlier):
    out = shape((192, FEAT), BF)
    return pl.pallas_call(
        far_terms_kernel,
        out_shape=(out, out),
        in_specs=[scalars()] + [whole()] * 4 + [anywhere()] * len(earlier),
        out_specs=(whole(), whole()),
        compiler_params=params(10),
        cost_estimate=cost(TOK * FEAT * COLS // 2, 6 * MIB),
        name="far_terms",
    )(place, keep, got, normed, normed2, *earlier)


def near_terms_kernel(place, keep_ref, got_ref, normed_ref, normed2_ref, *rest):
    out_ref = rest[-1]
    for slot, a in ((0, 1), (1, 3), (2, 0)):
        rows = block_rows(place, keep_ref, got_ref, a)
        part = dot(rows[:, :TOK], normed_ref[...], 1, 0)
        out_ref[slot] = part + dot(rows[:, TOK:], normed2_ref[...], 1, 0)


def near_terms(place, keep, got, normed, normed2, *earlier):
    return pl.pallas_call(
        near_terms_kernel,
        out_shape=shape((3, 384, FEAT), F32),
        in_specs=[scalars()] + [whole()] * 4 + [anywhere()] * len(earlier),
        out_specs=whole(),
        compiler_params=params(12),
        cost_estimate=cost(3 * TOK * FEAT * COLS // 2, 10 * MIB),
        name="near_terms",
    )(place, keep, got, normed, normed2, *earlier)


def inner_kernel(group, place, q_ref, k_ref, v_ref, grad_ref, keep_ref, take_ref, doc_ref, docs_ref, *rest):
    gq_ref, gk_ref, gv_ref, mask, turned = rest[-5:]
    n = pl.program_id(0)

    @pl.when(n == 0)
    def _():
        before, after = causal(docs_ref)
        mask[...] = before.astype(BF)
        turned[...] = after.astype(BF)

    c = place[2]
    reads = (upright(docs_ref[...], DIM) == doc_ref[:1]).astype(F32)
    mid = TOK // 2
    for j in range(2):
        q, k, v, grad = q_ref[j], k_ref[j], v_ref[j], grad_ref[j]
        spot = pl.multiple_of((n * 2 + j) * DIM, DIM)
        state = jnp.where(c == group, keep_ref[pl.ds(spot, DIM)], take_ref[pl.ds(spot, DIM)])
        across = reads * dot(grad, state, 1, 1)
        for rows, width in ((slice(0, mid), mid), (slice(mid, TOK), TOK)):
            scores = dot(grad[rows], v[:width], 1, 1).astype(BF) * mask[rows, :width]
            gq_ref[j, rows] = (dot(scores, k[:width], 1, 0) + across[rows]).astype(BF)
        for rows, start in ((slice(0, mid), 0), (slice(mid, TOK), mid)):
            scores = dot(v[rows], grad[start:], 1, 1).astype(BF) * turned[rows, start:]
            gk_ref[j, rows] = dot(scores, q[start:], 1, 0)
            scores = dot(k[rows], q[start:], 1, 1).astype(BF) * turned[rows, start:]
            gv_ref[j, rows] = dot(scores, grad[start:], 1, 0)


def inner(group, place, qh, kh, vh, grad, keep, take, doc, docs, *earlier):
    def kernel(*refs):
        inner_kernel(group, *refs)

    head = pl.BlockSpec((2, TOK, DIM), lambda n: (n + group * HALF // 2, 0, 0))
    out = pl.BlockSpec((2, TOK, DIM), lambda n: (n, 0, 0))
    return pl.pallas_call(
        kernel,
        grid=(HALF // 2,),
        out_shape=(shape((HALF, TOK, DIM), BF),) + (shape((HALF, TOK, DIM), F32),) * 2,
        in_specs=[scalars()]
        + [head] * 4
        + [fixed(ROWS, DIM)] * 2
        + [fixed(8, DIM), fixed(1, TOK)]
        + [anywhere()] * len(earlier),
        out_specs=(out, out, out),
        scratch_shapes=[pltpu.VMEM((TOK, TOK), BF), pltpu.VMEM((TOK, TOK), BF)],
        compiler_params=params(12),
        cost_estimate=cost(5 * HEADS * TOK * TOK * DIM, 5 * MIB),
        name="inner",
    )(place, qh, kh, vh, grad, keep, take, doc, docs, *earlier)


def last_kernel(place, k_ref, v_ref, gq0, gk0, gv0, gq1, gk1, gv1, keep_ref, take_ref, doc_ref, docs_ref, *rest):
    out_q, out_k, out_v, held_k, held_v = rest[-5:]
    c = place[2]
    writes = (upright(docs_ref[...], DIM) == doc_ref[:1]).astype(F32)
    for h in range(HEADS):
        state = pick_state(c, keep_ref, take_ref, h)
        gk, gv = ((gk0, gv0), (gk1, gv1))[h // HALF]
        held_k[h] = (gk[h % HALF] + writes * dot(v_ref[h], state, 1, 1)).astype(BF)
        held_v[h] = (gv[h % HALF] + writes * dot(k_ref[h], state, 1, 0)).astype(BF)
    out_q[...] = jnp.swapaxes(jnp.concatenate([gq0[...], gq1[...]], 0), 0, 1)
    out_k[...] = jnp.swapaxes(held_k[...], 0, 1)
    out_v[...] = jnp.swapaxes(held_v[...], 0, 1)


def last(place, kh, vh, lower, upper, keep, take, doc, docs, *earlier):
    out = shape((TOK, HEADS, DIM), BF)
    return pl.pallas_call(
        last_kernel,
        out_shape=(out, out, out),
        in_specs=[scalars()] + [whole()] * 12 + [anywhere()] * len(earlier),
        out_specs=(whole(),) * 3,
        scratch_shapes=[pltpu.VMEM((HEADS, TOK, DIM), BF)] * 2,
        compiler_params=params(12),
        cost_estimate=cost(4 * HEADS * TOK * DIM * DIM, 9 * MIB),
        name="last",
    )(place, kh, vh, *lower, *upper, keep, take, doc, docs, *earlier)


def pass_kernel(terms_ref, up_ref, down_ref, out_right, out_left):
    rows = up_ref.shape[0]
    out_right[:rows] = (terms_ref[0, :rows] + up_ref[...].astype(F32)).astype(BF)
    out_right[rows:] = terms_ref[0, rows:].astype(BF)
    out_left[:rows] = terms_ref[1, :rows].astype(BF)
    out_left[rows:] = (terms_ref[1, rows:] + down_ref[...].astype(F32)).astype(BF)


def pass_on(terms, up, down):
    out = shape((384, FEAT), BF)
    return pl.pallas_call(
        pass_kernel,
        grid=(1,),
        out_shape=(out, out),
        in_specs=[pl.BlockSpec((2, 384, FEAT), lambda n: (0, 0, 0)), fixed(192, FEAT), fixed(192, FEAT)],
        out_specs=(fixed(384, FEAT), fixed(384, FEAT)),
        compiler_params=params(16),
        cost_estimate=cost(384 * FEAT * 2, 5 * MIB),
        name="pass_on",
    )(terms, up, down)


def middle_kernel(own_ref, left_ref, right_ref, own_out, *outs):
    total = own_ref[...] + left_ref[...].astype(F32) + right_ref[...].astype(F32)
    own_out[...] = total[:96]
    for b in (1, 2, 3):
        outs[b - 1][...] = total[96 * b : 96 * (b + 1)].astype(BF)


def middle(terms, from_left, from_right):
    small = shape((96, FEAT), BF)
    return pl.pallas_call(
        middle_kernel,
        grid=(1,),
        out_shape=(shape((96, FEAT), F32), small, small, small),
        in_specs=[
            pl.BlockSpec((pl.squeezed, 384, FEAT), lambda n: (2, 0, 0)),
            fixed(384, FEAT),
            fixed(384, FEAT),
        ],
        out_specs=(fixed(96, FEAT),) * 4,
        compiler_params=params(16),
        cost_estimate=cost(384 * FEAT * 2, 4 * MIB),
        name="middle",
    )(terms, from_left, from_right)


def end_kernel(own_ref, p1, p2, p3, out_ref):
    out_ref[...] = own_ref[...] + p1[...].astype(F32) + p2[...].astype(F32) + p3[...].astype(F32)


def end(own, parts):
    return pl.pallas_call(
        end_kernel,
        grid=(1,),
        out_shape=shape((96, FEAT), F32),
        in_specs=[fixed(96, FEAT)] * 4,
        out_specs=fixed(96, FEAT),
        compiler_params=params(8),
        cost_estimate=cost(96 * FEAT * 3, MIB),
        name="end",
    )(own, *parts)


def route(move):
    pairs = []
    for i in range(32):
        target = move(i // 8, (i // 2) % 4, i % 2)
        if target is not None:
            y, z, c = target
            pairs.append((i, ((y % 4) * 4 + z % 4) * 2 + c))
    return pairs


SWAP = route(lambda y, z, c: (y, z, 1 - c))


def across_z(step):
    return route(lambda y, z, c: (y, z ^ step, c))


def along_y_open(step):
    return route(lambda y, z, c: (y + step, z, c) if 0 <= y + step < 4 else None)


def along_first(step):
    return route(lambda y, z, c: (y + step, z, c) if c == 0 else (y, z + step, c))


def along_second(step):
    return route(lambda y, z, c: (y, z + step, c) if c == 0 else (y + step, z, c))


def send(array, pairs):
    return lax.ppermute(array, "seq", pairs)


def along_head(array, step):
    return lax.ppermute(array, "head", [(i, (i + step) % 4) for i in range(4)])


def shards(queries, key_vectors, value_vectors, doc_ids, out_weight, grad_out):
    i = lax.axis_index("seq")
    place = jnp.stack([i // 8, (i // 2) % 4, i % 2, lax.axis_index("head")]).astype(jnp.int32)
    docs = doc_ids.reshape(1, TOK)
    on_left, on_right = along_head(grad_out, 1), along_head(grad_out, -1)

    qh, kh, vh, keep, give = prepare(place, queries, key_vectors, value_vectors, docs)
    far, chip = chip_state(place, keep, send(give, SWAP), True)
    beside = send(chip, across_z(1))
    intra0 = intra(qh, kh, vh, docs, 0, far)
    pair = join(place, chip, beside, True, 1, intra0)
    beyond = send(pair, across_z(2))
    intra1 = intra(qh, kh, vh, docs, 1, pair)
    total = join(place, pair, beyond, True, 2, intra1)
    aboves = [send(total, along_y_open(k)) for k in (1, 2)]
    top, bottom = halves(on_left, on_right, total)
    mine, theirs, doc = entry_state(place, far, (beside, beyond), aboves, True, top)
    far_top, far_bottom = along_head(top, 1), along_head(bottom, -1)
    taken = send(theirs, SWAP)
    attn, normed = attend(place, qh, intra0, intra1, mine, taken, doc, docs)
    normed2 = send(normed, SWAP)
    cotangent, blocks, others = turn(
        place, grad_out, on_right, far_top, far_bottom, on_left, normed
    )
    blocks2 = send(others, SWAP)
    top, bottom, right, left, out_own = project(place, normed, out_weight, others)
    top, bottom = along_head(top, 1), along_head(bottom, -1)
    far_up, far_down = far_terms(place, blocks, blocks2, normed, normed2, right)
    up, down = send(far_up, along_first(1)), send(far_down, along_first(-1))
    grad, keep, give = back(place, cotangent, out_weight, attn, qh, docs, far_up)
    got = send(give, SWAP)
    right, left = out_pass(right, left, top, bottom, keep)
    right, left = along_head(right, 1), along_head(left, -1)
    far, chip = chip_state(place, keep, got, False)
    beside = send(chip, across_z(1))
    terms = near_terms(place, blocks, blocks2, normed, normed2, far)
    pair = join(place, chip, beside, False, 1, terms)
    beyond = send(pair, across_z(2))
    on, back_on = pass_on(terms, up, down)
    lower = inner(0, place, qh, kh, vh, grad, mine, taken, doc, docs, on, pair)
    on, back_on = send(on, along_first(1)), send(back_on, along_first(-1))
    total = join(place, pair, beyond, False, 2, lower[0])
    aboves = [send(total, along_y_open(-k)) for k in (1, 2)]
    upper = inner(1, place, qh, kh, vh, grad, mine, taken, doc, docs, total)
    back_mine, theirs, back_doc = entry_state(place, far, (beside, beyond), aboves, False, upper[0])
    back_taken = send(theirs, SWAP)
    own, *shares = middle(terms, on, back_on)
    shares = [send(share, along_second(k)) for k, share in zip((1, 2, 3), shares)]
    grad_queries, grad_keys, grad_values = last(
        place, kh, vh, lower, upper, back_mine, back_taken, back_doc, docs, own
    )
    layer_out = out_end(out_own, right, left, own)
    grad_weight = end(own, shares).T
    return layer_out, grad_queries, grad_keys, grad_values, grad_weight


def solution(mesh):
    placed = (
        P("seq", "head", None),
        P("seq", "head", None),
        P("seq", "head", None),
        P("seq"),
        P("head", None),
        P("seq", "head"),
    )
    return jax.shard_map(
        shards,
        mesh=mesh,
        in_specs=placed,
        out_specs=(
            P("seq", "head"),
            P("seq", "head", None),
            P("seq", "head", None),
            P("seq", "head", None),
            P("head", "seq"),
        ),
        check_vma=False,
    )
```

```python
import jax
import jax.numpy as jnp
from jax import lax
from jax.experimental import pallas as pl
from jax.experimental.pallas import tpu as pltpu
from jax.sharding import PartitionSpec as P

BF = jnp.bfloat16
F32 = jnp.float32
TOK, HEADS, DIM, FEAT, COLS = 512, 8, 128, 1024, 3072
HALF = HEADS // 2
ROWS = HALF * DIM
MIB = 2**20


def shape(dims, dtype):
    return jax.ShapeDtypeStruct(dims, dtype)


def whole():
    return pl.BlockSpec(memory_space=pltpu.VMEM)


def scalars():
    return pl.BlockSpec(memory_space=pltpu.SMEM)


def params(mib):
    return pltpu.CompilerParams(vmem_limit_bytes=mib * MIB)


def cost(flops, moved):
    return pl.CostEstimate(flops=flops, bytes_accessed=moved, transcendentals=0)


def dot(a, b, ca, cb):
    return lax.dot_general(a, b, (((ca,), (cb,)), ((), ())), preferred_element_type=F32)


def fixed(*dims):
    return pl.BlockSpec(dims, lambda n: (0,) * len(dims))


def in_hbm():
    return pl.BlockSpec(memory_space=pltpu.HBM)


def anywhere():
    return pl.BlockSpec(memory_space=pl.ANY)


def upright(docs_row, width):
    docs_row = docs_row.astype(F32)
    return jnp.broadcast_to(docs_row, (width, docs_row.shape[1])).T


def prepare_kernel(place, q_hbm, k_hbm, v_hbm, docs_hbm, cot_hbm, qh_ref, kh_ref, vh_ref, keep_ref, give_ref, cot_ref, q_buf, k_buf, v_buf, docs_buf, own, sems, docs_sem, cot_sem):
    steps = k_buf.shape[0]
    rows = TOK // steps

    def fetch(n, source, target, sem):
        copy = pltpu.make_async_copy(source.at[n * rows : (n + 1) * rows], target.at[n], sem)
        copy.start()
        return copy

    docs_copy = pltpu.make_async_copy(docs_hbm, docs_buf, docs_sem)
    docs_copy.start()
    copies = []
    for n in range(steps):
        copies.append(fetch(n, k_hbm, k_buf, sems.at[0, n]))
        copies.append(fetch(n, v_hbm, v_buf, sems.at[1, n]))
    q_copies = [fetch(n, q_hbm, q_buf, sems.at[2, n]) for n in range(steps)]
    cot_copy = pltpu.make_async_copy(cot_hbm, cot_ref, cot_sem)
    cot_copy.start()
    c = place[2]
    docs_copy.wait()
    docs = docs_buf[...].astype(F32)
    last = docs[:, TOK - 1 :]
    tail = (upright(docs, DIM) == last).astype(BF)
    for n in range(steps):
        span = slice(n * rows, (n + 1) * rows)
        copies[2 * n].wait()
        copies[2 * n + 1].wait()
        kh = jnp.swapaxes(k_buf[n], 0, 1)
        vh = jnp.swapaxes(v_buf[n], 0, 1)
        kh_ref[:, span] = kh
        vh_ref[:, span] = vh
        for h in range(HEADS):
            part = dot(kh[h] * tail[span], vh[h], 0, 0)
            spot = slice((h % HALF) * DIM, (h % HALF + 1) * DIM)
            if n == 0:
                own[h // HALF, spot] = part
            else:
                own[h // HALF, spot] += part
    keep_ref[:ROWS] = own[c]
    give_ref[:ROWS] = own[1 - c]
    doc_rows = jnp.broadcast_to(last, (8, DIM))
    keep_ref[ROWS:] = doc_rows
    give_ref[ROWS:] = doc_rows
    for n in range(steps):
        q_copies[n].wait()
        qh_ref[:, n * rows : (n + 1) * rows] = jnp.swapaxes(q_buf[n], 0, 1)
    cot_copy.wait()


def prepare(place, queries, keys, values, docs, cotangent):
    steps = 2
    head_major = shape((HEADS, TOK, DIM), BF)
    half = shape((ROWS + 8, DIM), F32)
    buffer = pltpu.VMEM((steps, TOK // steps, HEADS, DIM), BF)
    return pl.pallas_call(
        prepare_kernel,
        out_shape=(head_major, head_major, head_major, half, half, shape((TOK, 768), BF)),
        in_specs=[scalars()] + [in_hbm()] * 5,
        out_specs=(whole(),) * 6,
        scratch_shapes=[
            buffer,
            buffer,
            buffer,
            pltpu.VMEM((1, TOK), jnp.int32),
            pltpu.VMEM((2, ROWS, DIM), F32),
            pltpu.SemaphoreType.DMA((3, steps)),
            pltpu.SemaphoreType.DMA,
            pltpu.SemaphoreType.DMA,
        ],
        compiler_params=params(12),
        cost_estimate=cost(2 * HEADS * TOK * DIM * DIM, 6 * MIB),
        name="prepare",
    )(place, *[pltpu.with_memory_space_constraint(a, pltpu.HBM) for a in (queries, keys, values, docs, cotangent)])


def chip_kernel(forward, place, keep_ref, got_ref, *rest):
    far_ref, chip_ref = rest[-2:]
    c = place[2]
    far_is_mine = (c == 0) if forward else (c == 1)

    def write(far, near):
        same = (far[ROWS : ROWS + 1] == near[ROWS : ROWS + 1]).astype(F32)
        far_ref[...] = far[...]
        chip_ref[:ROWS] = (near[:ROWS] + same * far[:ROWS]).astype(BF)
        chip_ref[ROWS:] = jnp.broadcast_to(near[ROWS : ROWS + 1], (16, DIM)).astype(BF)

    @pl.when(far_is_mine)
    def _():
        write(keep_ref, got_ref)

    @pl.when(jnp.logical_not(far_is_mine))
    def _():
        write(got_ref, keep_ref)


def chip_state(place, keep, got, forward, *earlier):
    def kernel(*refs):
        chip_kernel(forward, *refs)

    return pl.pallas_call(
        kernel,
        out_shape=(shape((ROWS + 8, DIM), F32), shape((ROWS + 16, DIM), BF)),
        in_specs=[scalars(), whole(), whole()] + [anywhere()] * len(earlier),
        out_specs=(whole(), whole()),
        compiler_params=params(4),
        cost_estimate=cost(ROWS * DIM * 3, MIB),
        name="chip_state",
    )(place, keep, got, *earlier)


def spot_of(place, forward, step):
    chip = place[0] * 4 + place[1]
    spot = lax.rem(chip // step, 2)
    return spot if forward else 1 - spot


def join_kernel(forward, step, place, own_ref, other_ref, *rest):
    out_ref = rest[-1]
    first = spot_of(place, forward, step) == 0

    def write(early, late):
        doc = late[ROWS : ROWS + 1]
        same = (early[ROWS : ROWS + 1] == doc).astype(F32)
        total = late[:ROWS].astype(F32) + same * early[:ROWS].astype(F32)
        out_ref[:ROWS] = total.astype(BF)
        out_ref[ROWS:] = jnp.broadcast_to(doc, (16, DIM))

    @pl.when(first)
    def _():
        write(own_ref, other_ref)

    @pl.when(jnp.logical_not(first))
    def _():
        write(other_ref, own_ref)


def join(place, own, other, forward, step, *earlier):
    def kernel(*refs):
        join_kernel(forward, step, *refs)

    return pl.pallas_call(
        kernel,
        out_shape=shape((ROWS + 16, DIM), BF),
        in_specs=[scalars()] + [whole()] * 2 + [anywhere()] * len(earlier),
        out_specs=whole(),
        compiler_params=params(4),
        cost_estimate=cost(ROWS * DIM * 3, MIB),
        name="join",
    )(place, own, other, *earlier)


def entry_kernel(forward, steps, place, far_ref, *refs):
    parts, (keep_ref, give_ref, doc_ref) = refs[: len(steps)], refs[-3:]
    y, c = place[0], place[2]
    level = y if forward else 3 - y
    far_is_mine = (c == 0) if forward else (c == 1)
    inside = [spot_of(place, forward, step) == 1 if step > 0 else level >= -step for step in steps]
    docs = [p[ROWS : ROWS + 1].astype(F32) for p in parts]
    before_doc = jnp.full((1, DIM), -1.0, F32)
    for k in reversed(range(len(steps))):
        before_doc = jnp.where(inside[k], docs[k], before_doc)
    before = jnp.zeros((ROWS, DIM), F32)
    for k in range(len(steps)):
        use = jnp.where(inside[k], (docs[k] == before_doc).astype(F32), 0.0)
        before = before + use * parts[k][:ROWS].astype(F32)
    far_doc = far_ref[ROWS : ROWS + 1]
    after = far_ref[:ROWS] + (before_doc == far_doc).astype(F32) * before

    @pl.when(far_is_mine)
    def _():
        keep_ref[...] = before.astype(BF)
        give_ref[...] = after.astype(BF)
        doc_ref[...] = jnp.broadcast_to(before_doc, (8, DIM))

    @pl.when(jnp.logical_not(far_is_mine))
    def _():
        keep_ref[...] = after.astype(BF)
        give_ref[...] = before.astype(BF)
        doc_ref[...] = jnp.broadcast_to(far_doc, (8, DIM))


def entry_state(place, far, parts, steps, forward, *earlier):
    def kernel(*refs):
        entry_kernel(forward, steps, *refs)

    half = shape((ROWS, DIM), BF)
    return pl.pallas_call(
        kernel,
        out_shape=(half, half, shape((8, DIM), F32)),
        in_specs=[scalars()] + [whole()] * (1 + len(parts)) + [anywhere()] * len(earlier),
        out_specs=(whole(),) * 3,
        compiler_params=params(4),
        cost_estimate=cost(ROWS * DIM * 10, MIB),
        name="entry_state",
    )(place, far, *parts, *earlier)


def causal(docs_ref):
    row = jnp.broadcast_to(docs_ref[...].astype(F32), (TOK, TOK))
    t = lax.broadcasted_iota(jnp.int32, (TOK, TOK), 0)
    s = lax.broadcasted_iota(jnp.int32, (TOK, TOK), 1)
    same = row.T == row
    return (t >= s) & same, (s >= t) & same


def intra_kernel(q_ref, k_ref, v_ref, docs_ref, *rest):
    attn_ref, mask = rest[-2:]
    mask[...] = causal(docs_ref)[0].astype(BF)
    mid = TOK // 2
    for h in range(q_ref.shape[0]):
        for rows, width in ((slice(0, mid), mid), (slice(mid, TOK), TOK)):
            scores = dot(q_ref[h, rows], k_ref[h, :width], 1, 1).astype(BF) * mask[rows, :width]
            attn_ref[h, rows] = dot(scores, v_ref[h, :width], 1, 0)


def intra(qh, kh, vh, docs, group, *earlier):
    part = pl.BlockSpec((HALF, TOK, DIM), lambda n: (group, 0, 0))
    return pl.pallas_call(
        intra_kernel,
        grid=(1,),
        out_shape=shape((HALF, TOK, DIM), F32),
        in_specs=[part, part, part, fixed(1, TOK)] + [anywhere()] * len(earlier),
        out_specs=fixed(HALF, TOK, DIM),
        scratch_shapes=[pltpu.VMEM((TOK, TOK), BF)],
        compiler_params=params(14),
        cost_estimate=cost(2 * HEADS * TOK * TOK * DIM, 3 * MIB),
        name="intra",
    )(qh, kh, vh, docs, *earlier)


def upper_kernel(q_ref, k_ref, docs_ref, *rest):
    out_ref, mask = rest[-2:]
    mask[...] = causal(docs_ref)[1].astype(BF)
    mid = TOK // 2
    for h in range(HEADS):
        for rows, start in ((slice(0, mid), 0), (slice(mid, TOK), mid)):
            scores = dot(k_ref[h, rows], q_ref[h, start:], 1, 1)
            out_ref[h, rows, start:] = scores.astype(BF) * mask[rows, start:]


def upper_scores(qh, kh, docs, *earlier):
    return pl.pallas_call(
        upper_kernel,
        out_shape=shape((HEADS, TOK, TOK), BF),
        in_specs=[whole()] * 3 + [anywhere()] * len(earlier),
        out_specs=whole(),
        scratch_shapes=[pltpu.VMEM((TOK, TOK), BF)],
        compiler_params=params(10),
        cost_estimate=cost(2 * HEADS * TOK * TOK * DIM, 6 * MIB),
        name="upper_scores",
    )(qh, kh, docs, *earlier)


def pick_state(c, keep_ref, take_ref, h):
    rows = slice((h % HALF) * DIM, (h % HALF + 1) * DIM)
    mine = c == h // HALF
    return jnp.where(mine, keep_ref[rows], take_ref[rows])


def attend_kernel(place, q_ref, intra0, intra1, keep_ref, take_ref, doc_ref, docs_ref, *rest):
    attn_ref, normed_ref = rest[-2:]
    c = place[2]
    reads = (upright(docs_ref[...], DIM) == doc_ref[:1]).astype(F32)
    for h in range(HEADS):
        state = pick_state(c, keep_ref, take_ref, h)
        attn = (intra0, intra1)[h // HALF][h % HALF] + reads * dot(q_ref[h], state, 1, 0)
        attn_ref[h] = attn
        scale = lax.rsqrt(jnp.mean(attn * attn, axis=-1, keepdims=True) + 1e-05)
        normed_ref[:, h * DIM : (h + 1) * DIM] = (attn * scale).astype(BF)


def attend(place, qh, intra0, intra1, keep, take, doc, docs, *earlier):
    return pl.pallas_call(
        attend_kernel,
        out_shape=(shape((HEADS, TOK, DIM), F32), shape((TOK, FEAT), BF)),
        in_specs=[scalars()] + [whole()] * 7 + [anywhere()] * len(earlier),
        out_specs=(whole(), whole()),
        compiler_params=params(8),
        cost_estimate=cost(2 * HEADS * TOK * DIM * DIM, 6 * MIB),
        name="attend",
    )(place, qh, intra0, intra1, keep, take, doc, docs, *earlier)


def project_kernel(places, place, normed_ref, w_hbm, *rest):
    outs, (w_buf, sems) = rest[-3 - len(places) : -2], rest[-2:]
    x = place[3]
    copies = []
    for n, r in enumerate(places):
        spot = pl.multiple_of(lax.rem(x + r, 4) * 768, 768)
        copies.append(pltpu.make_async_copy(w_hbm.at[:, pl.ds(spot, 768)], w_buf.at[n], sems.at[n]))
        copies[n].start()
    for n, r in enumerate(places):
        copies[n].wait()
        part = jnp.dot(normed_ref[...], w_buf[n], preferred_element_type=F32)
        if r == 2:
            mid = TOK // 2
            outs[0][...] = part[:mid].astype(BF)
            outs[1][...] = part[mid:].astype(BF)
        else:
            outs[n + 1][...] = part.astype(outs[n + 1].dtype)


def project(place, places, normed, weight, *earlier):
    outs = []
    for r in places:
        if r == 2:
            outs += [shape((TOK // 2, 768), BF)] * 2
        else:
            outs.append(shape((TOK, 768), BF if r else F32))
    shift = 0 if 2 in places else 1

    def kernel(*refs):
        ahead = 3 + len(earlier)
        project_kernel(places, *refs[:ahead], *([None] * shift), *refs[ahead:])

    return pl.pallas_call(
        kernel,
        out_shape=tuple(outs),
        in_specs=[scalars(), whole(), in_hbm()] + [anywhere()] * len(earlier),
        out_specs=(whole(),) * len(outs),
        scratch_shapes=[pltpu.VMEM((len(places), FEAT, 768), BF), pltpu.SemaphoreType.DMA((len(places),))],
        compiler_params=params(4 + 3 * len(places)),
        cost_estimate=cost(TOK * FEAT * COLS * len(places) // 2, 3 * MIB * len(places)),
        name="project",
    )(place, normed, weight, *earlier)


def halves_kernel(left_ref, right_ref, *rest):
    top_ref, bottom_ref = rest[-2:]
    mid = TOK // 2
    top_ref[...] = left_ref[:mid]
    bottom_ref[...] = right_ref[mid:]


def halves(left, right, *earlier):
    out = shape((TOK // 2, 768), BF)
    return pl.pallas_call(
        halves_kernel,
        out_shape=(out, out),
        in_specs=[whole()] * 2 + [anywhere()] * len(earlier),
        out_specs=(whole(),) * 2,
        compiler_params=params(6),
        cost_estimate=cost(TOK * 768, 2 * MIB),
        name="halves",
    )(left, right, *earlier)


def out_pass_kernel(right_ref, left_ref, top_ref, bottom_ref, *rest):
    out_right, out_left = rest[-2:]
    mid = TOK // 2
    out_right[:mid] = (right_ref[:mid].astype(F32) + top_ref[...].astype(F32)).astype(BF)
    out_right[mid:] = right_ref[mid:]
    out_left[:mid] = left_ref[:mid]
    out_left[mid:] = (left_ref[mid:].astype(F32) + bottom_ref[...].astype(F32)).astype(BF)


def out_pass(right, left, top, bottom, *earlier):
    part = shape((TOK, 768), BF)
    return pl.pallas_call(
        out_pass_kernel,
        out_shape=(part, part),
        in_specs=[whole()] * 4 + [anywhere()] * len(earlier),
        out_specs=(whole(), whole()),
        compiler_params=params(6),
        cost_estimate=cost(TOK * 768, 4 * MIB),
        name="out_pass",
    )(right, left, top, bottom, *earlier)


def out_end_kernel(own_ref, left_ref, right_ref, *rest):
    total = own_ref[...] + left_ref[...].astype(F32) + right_ref[...].astype(F32)
    rest[-1][...] = total.astype(BF)


def out_end(own, from_left, from_right, *earlier):
    return pl.pallas_call(
        out_end_kernel,
        out_shape=shape((TOK, 768), BF),
        in_specs=[whole()] * 3 + [anywhere()] * len(earlier),
        out_specs=whole(),
        compiler_params=params(6),
        cost_estimate=cost(2 * TOK * 768, 4 * MIB),
        name="out_end",
    )(own, from_left, from_right, *earlier)


def turn_kernel(place, own_ref, right_ref, top_ref, bottom_ref, left_ref, *rest):
    joined_ref, keep_ref, give_ref = rest[-3:]
    c, x = place[2], place[3]
    mid = TOK // 2
    for r, ref, tokens in (
        (0, own_ref, slice(0, TOK)),
        (1, right_ref, slice(0, TOK)),
        (3, left_ref, slice(0, TOK)),
        (2, top_ref, slice(0, mid)),
        (2, bottom_ref, slice(mid, TOK)),
    ):
        block = ref[...]
        spot = pl.multiple_of(lax.rem(x + r, 4) * 768, 768)
        joined_ref[tokens, pl.ds(spot, 768)] = block
        turned = block.T.reshape(4, 2, 96, block.shape[0])
        low, high = turned[:, 0], turned[:, 1]
        keep_ref[r, :, :, tokens] = jnp.where(c == 0, low, high)
        give_ref[r, :, :, tokens] = jnp.where(c == 0, high, low)


def turn(place, own, right, top, bottom, left, *earlier):
    out = shape((4, 4, 96, TOK), BF)
    return pl.pallas_call(
        turn_kernel,
        out_shape=(shape((TOK, COLS), BF), out, out),
        in_specs=[scalars()] + [whole()] * 5 + [anywhere()] * len(earlier),
        out_specs=(whole(),) * 3,
        compiler_params=params(8),
        cost_estimate=cost(TOK * COLS, 6 * MIB),
        name="turn",
    )(place, own, right, top, bottom, left, *earlier)


def back_kernel(place, cot_ref, w_ref, attn_ref, q_ref, docs_ref, *rest):
    grad_ref, keep_ref, give_ref, own = rest[-4:]
    c = place[2]
    pairs = HEADS // 2
    docs = docs_ref[...].astype(F32)
    first = docs[:, :1]
    lead = (upright(docs, DIM) == first).astype(BF)
    for n in range(pairs):
        grad_normed = dot(cot_ref[...], w_ref[n * 2 * DIM : (n + 1) * 2 * DIM], 1, 1)
        for j in range(2):
            h = 2 * n + j
            attn = attn_ref[h]
            scale = lax.rsqrt(jnp.mean(attn * attn, axis=-1, keepdims=True) + 1e-05)
            normed = attn * scale
            grad = grad_normed[:, j * DIM : (j + 1) * DIM]
            grad = scale * (grad - normed * jnp.mean(grad * normed, axis=-1, keepdims=True))
            grad = grad.astype(BF)
            grad_ref[h] = grad
            spot = slice((h % HALF) * DIM, (h % HALF + 1) * DIM)
            own[h // HALF, spot] = dot(q_ref[h] * lead, grad, 0, 0)
    keep_ref[:ROWS] = own[c]
    give_ref[:ROWS] = own[1 - c]
    doc_rows = jnp.broadcast_to(first, (8, DIM))
    keep_ref[ROWS:] = doc_rows
    give_ref[ROWS:] = doc_rows


def back(place, cotangent, weight, attn, qh, docs, *earlier):
    half = shape((ROWS + 8, DIM), F32)
    return pl.pallas_call(
        back_kernel,
        out_shape=(shape((HEADS, TOK, DIM), BF), half, half),
        in_specs=[scalars()] + [whole()] * 5 + [anywhere()] * len(earlier),
        out_specs=(whole(),) * 3,
        scratch_shapes=[pltpu.VMEM((2, ROWS, DIM), F32)],
        compiler_params=params(8),
        cost_estimate=cost(2 * TOK * FEAT * COLS + 2 * HEADS * TOK * DIM * DIM, 15 * MIB),
        name="back",
    )(place, cotangent, weight, attn, qh, docs, *earlier)


def block_rows(place, keep_ref, got_ref, a):
    y, z, c, x = place[0], place[1], place[2], place[3]
    rows = []
    for b in range(4):
        to_y = lax.rem(y + jnp.where(c == 0, a, b), 4)
        to_z = lax.rem(z + jnp.where(c == 0, b, a), 4)
        r = lax.rem(to_y + 4 - x, 4)
        rows.append(jnp.concatenate([keep_ref[r, to_z], got_ref[r, to_z]], 1))
    return jnp.concatenate(rows, 0)


def far_terms_kernel(place, keep_ref, got_ref, normed_ref, normed2_ref, *rest):
    up_ref, down_ref = rest[-2:]
    rows = block_rows(place, keep_ref, got_ref, 2)
    total = dot(rows[:, :TOK], normed_ref[...], 1, 0) + dot(rows[:, TOK:], normed2_ref[...], 1, 0)
    up_ref[...] = total[:192].astype(BF)
    down_ref[...] = total[192:].astype(BF)


def far_terms(place, keep, got, normed, normed2, *earlier):
    out = shape((192, FEAT), BF)
    return pl.pallas_call(
        far_terms_kernel,
        out_shape=(out, out),
        in_specs=[scalars()] + [whole()] * 4 + [anywhere()] * len(earlier),
        out_specs=(whole(), whole()),
        compiler_params=params(10),
        cost_estimate=cost(TOK * FEAT * COLS // 2, 6 * MIB),
        name="far_terms",
    )(place, keep, got, normed, normed2, *earlier)


def near_terms_kernel(place, keep_ref, got_ref, normed_ref, normed2_ref, *rest):
    out_ref = rest[-1]
    for slot, a in ((0, 1), (1, 3), (2, 0)):
        rows = block_rows(place, keep_ref, got_ref, a)
        part = dot(rows[:, :TOK], normed_ref[...], 1, 0)
        out_ref[slot] = part + dot(rows[:, TOK:], normed2_ref[...], 1, 0)


def near_terms(place, keep, got, normed, normed2, *earlier):
    return pl.pallas_call(
        near_terms_kernel,
        out_shape=shape((3, 384, FEAT), F32),
        in_specs=[scalars()] + [whole()] * 4 + [anywhere()] * len(earlier),
        out_specs=whole(),
        compiler_params=params(12),
        cost_estimate=cost(3 * TOK * FEAT * COLS // 2, 10 * MIB),
        name="near_terms",
    )(place, keep, got, normed, normed2, *earlier)


def inner_kernel(group, place, scores_ref, q_ref, k_ref, v_ref, grad_ref, keep_ref, take_ref, doc_ref, docs_ref, *rest):
    gq_ref, gk_ref, gv_ref, mask, turned = rest[-5:]
    n = pl.program_id(0)

    @pl.when(n == 0)
    def _():
        before, after = causal(docs_ref)
        mask[...] = before.astype(BF)
        turned[...] = after.astype(BF)

    c = place[2]
    reads = (upright(docs_ref[...], DIM) == doc_ref[:1]).astype(F32)
    mid = TOK // 2
    for j in range(2):
        q, k, v, grad = q_ref[j], k_ref[j], v_ref[j], grad_ref[j]
        spot = pl.multiple_of((n * 2 + j) * DIM, DIM)
        state = jnp.where(c == group, keep_ref[pl.ds(spot, DIM)], take_ref[pl.ds(spot, DIM)])
        across = reads * dot(grad, state, 1, 1)
        for rows, width in ((slice(0, mid), mid), (slice(mid, TOK), TOK)):
            scores = dot(grad[rows], v[:width], 1, 1).astype(BF) * mask[rows, :width]
            gq_ref[j, rows] = (dot(scores, k[:width], 1, 0) + across[rows]).astype(BF)
        for rows, start in ((slice(0, mid), 0), (slice(mid, TOK), mid)):
            scores = dot(v[rows], grad[start:], 1, 1).astype(BF) * turned[rows, start:]
            gk_ref[j, rows] = dot(scores, q[start:], 1, 0)
            gv_ref[j, rows] = dot(scores_ref[j, rows, start:], grad[start:], 1, 0)


def inner(group, place, scores, qh, kh, vh, grad, keep, take, doc, docs, *earlier):
    def kernel(*refs):
        inner_kernel(group, *refs)

    head = pl.BlockSpec((2, TOK, DIM), lambda n: (n + group * HALF // 2, 0, 0))
    out = pl.BlockSpec((2, TOK, DIM), lambda n: (n, 0, 0))
    return pl.pallas_call(
        kernel,
        grid=(HALF // 2,),
        out_shape=(shape((HALF, TOK, DIM), BF),) + (shape((HALF, TOK, DIM), F32),) * 2,
        in_specs=[scalars(), pl.BlockSpec((2, TOK, TOK), lambda n: (n + group * HALF // 2, 0, 0))]
        + [head] * 4
        + [fixed(ROWS, DIM)] * 2
        + [fixed(8, DIM), fixed(1, TOK)]
        + [anywhere()] * len(earlier),
        out_specs=(out, out, out),
        scratch_shapes=[pltpu.VMEM((TOK, TOK), BF), pltpu.VMEM((TOK, TOK), BF)],
        compiler_params=params(14),
        cost_estimate=cost(5 * HEADS * TOK * TOK * DIM, 5 * MIB),
        name="inner",
    )(place, scores, qh, kh, vh, grad, keep, take, doc, docs, *earlier)


def last_kernel(place, k_ref, v_ref, gq0, gk0, gv0, gq1, gk1, gv1, keep_ref, take_ref, doc_ref, docs_ref, *rest):
    out_q, out_k, out_v, held_k, held_v = rest[-5:]
    c = place[2]
    writes = (upright(docs_ref[...], DIM) == doc_ref[:1]).astype(F32)
    for h in range(HEADS):
        state = pick_state(c, keep_ref, take_ref, h)
        gk, gv = ((gk0, gv0), (gk1, gv1))[h // HALF]
        held_k[h] = (gk[h % HALF] + writes * dot(v_ref[h], state, 1, 1)).astype(BF)
        held_v[h] = (gv[h % HALF] + writes * dot(k_ref[h], state, 1, 0)).astype(BF)
    out_q[...] = jnp.swapaxes(jnp.concatenate([gq0[...], gq1[...]], 0), 0, 1)
    out_k[...] = jnp.swapaxes(held_k[...], 0, 1)
    out_v[...] = jnp.swapaxes(held_v[...], 0, 1)


def last(place, kh, vh, lower, upper, keep, take, doc, docs, *earlier):
    out = shape((TOK, HEADS, DIM), BF)
    return pl.pallas_call(
        last_kernel,
        out_shape=(out, out, out),
        in_specs=[scalars()] + [whole()] * 12 + [anywhere()] * len(earlier),
        out_specs=(whole(),) * 3,
        scratch_shapes=[pltpu.VMEM((HEADS, TOK, DIM), BF)] * 2,
        compiler_params=params(12),
        cost_estimate=cost(4 * HEADS * TOK * DIM * DIM, 9 * MIB),
        name="last",
    )(place, kh, vh, *lower, *upper, keep, take, doc, docs, *earlier)


def pass_kernel(terms_ref, up_ref, down_ref, out_right, out_left):
    rows = up_ref.shape[0]
    out_right[:rows] = (terms_ref[0, :rows] + up_ref[...].astype(F32)).astype(BF)
    out_right[rows:] = terms_ref[0, rows:].astype(BF)
    out_left[:rows] = terms_ref[1, :rows].astype(BF)
    out_left[rows:] = (terms_ref[1, rows:] + down_ref[...].astype(F32)).astype(BF)


def pass_on(terms, up, down):
    out = shape((384, FEAT), BF)
    return pl.pallas_call(
        pass_kernel,
        grid=(1,),
        out_shape=(out, out),
        in_specs=[pl.BlockSpec((2, 384, FEAT), lambda n: (0, 0, 0)), fixed(192, FEAT), fixed(192, FEAT)],
        out_specs=(fixed(384, FEAT), fixed(384, FEAT)),
        compiler_params=params(16),
        cost_estimate=cost(384 * FEAT * 2, 5 * MIB),
        name="pass_on",
    )(terms, up, down)


def middle_kernel(own_ref, left_ref, right_ref, own_out, *outs):
    total = own_ref[...] + left_ref[...].astype(F32) + right_ref[...].astype(F32)
    own_out[...] = total[:96]
    for b in (1, 2, 3):
        outs[b - 1][...] = total[96 * b : 96 * (b + 1)].astype(BF)


def middle(terms, from_left, from_right):
    small = shape((96, FEAT), BF)
    return pl.pallas_call(
        middle_kernel,
        grid=(1,),
        out_shape=(shape((96, FEAT), F32), small, small, small),
        in_specs=[
            pl.BlockSpec((pl.squeezed, 384, FEAT), lambda n: (2, 0, 0)),
            fixed(384, FEAT),
            fixed(384, FEAT),
        ],
        out_specs=(fixed(96, FEAT),) * 4,
        compiler_params=params(16),
        cost_estimate=cost(384 * FEAT * 2, 4 * MIB),
        name="middle",
    )(terms, from_left, from_right)


def end_kernel(own_ref, p1, p2, p3, out_ref):
    out_ref[...] = own_ref[...] + p1[...].astype(F32) + p2[...].astype(F32) + p3[...].astype(F32)


def end(own, parts):
    return pl.pallas_call(
        end_kernel,
        grid=(1,),
        out_shape=shape((96, FEAT), F32),
        in_specs=[fixed(96, FEAT)] * 4,
        out_specs=fixed(96, FEAT),
        compiler_params=params(8),
        cost_estimate=cost(96 * FEAT * 3, MIB),
        name="end",
    )(own, *parts)


def route(move):
    pairs = []
    for i in range(32):
        target = move(i // 8, (i // 2) % 4, i % 2)
        if target is not None:
            y, z, c = target
            pairs.append((i, ((y % 4) * 4 + z % 4) * 2 + c))
    return pairs


SWAP = route(lambda y, z, c: (y, z, 1 - c))


def across_z(step):
    return route(lambda y, z, c: (y, z ^ step, c))


def across_y(step):
    return route(lambda y, z, c: (y ^ step, z, c))


def along_y_open(step):
    return route(lambda y, z, c: (y + step, z, c) if 0 <= y + step < 4 else None)


def along_first(step):
    return route(lambda y, z, c: (y + step, z, c) if c == 0 else (y, z + step, c))


def along_second(step):
    return route(lambda y, z, c: (y, z + step, c) if c == 0 else (y + step, z, c))


def send(array, pairs):
    return lax.ppermute(array, "seq", pairs)


def along_head(array, step):
    return lax.ppermute(array, "head", [(i, (i + step) % 4) for i in range(4)])


def shards(queries, key_vectors, value_vectors, doc_ids, out_weight, grad_out):
    i = lax.axis_index("seq")
    place = jnp.stack([i // 8, (i // 2) % 4, i % 2, lax.axis_index("head")]).astype(jnp.int32)
    docs = doc_ids.reshape(1, TOK)
    qh, kh, vh, keep, give, cot = prepare(place, queries, key_vectors, value_vectors, docs, grad_out)
    on_left, on_right = along_head(cot, 1), along_head(cot, -1)
    far, chip = chip_state(place, keep, send(give, SWAP), True)
    beside = send(chip, across_z(1))
    intra0 = intra(qh, kh, vh, docs, 0, far)
    pair = join(place, chip, beside, True, 1, intra0)
    beyond = send(pair, across_z(2))
    scores = upper_scores(qh, kh, docs, pair)
    total = join(place, pair, beyond, True, 2, scores)
    aboves = [send(total, along_y_open(k)) for k in (1, 2)]
    intra1 = intra(qh, kh, vh, docs, 1, total)
    top, bottom = halves(on_left, on_right, intra1)
    mine, theirs, doc = entry_state(place, far, [beside, beyond] + aboves, (1, 2, -1, -2), True, top)
    far_top, far_bottom = along_head(top, 1), along_head(bottom, -1)
    taken = send(theirs, SWAP)
    attn, normed = attend(place, qh, intra0, intra1, mine, taken, doc, docs)
    normed2 = send(normed, SWAP)
    cotangent, blocks, others = turn(place, cot, on_right, far_top, far_bottom, on_left, normed)
    blocks2 = send(others, SWAP)
    grad, keep, give = back(place, cotangent, out_weight, attn, qh, docs, others)
    got = send(give, SWAP)
    far_up, far_down = far_terms(place, blocks, blocks2, normed, normed2, keep)
    up, down = send(far_up, along_first(1)), send(far_down, along_first(-1))
    far, chip = chip_state(place, keep, got, False, far_up)
    steps = [send(chip, across_z(1))]
    top, bottom = project(place, (2,), normed, out_weight, far)
    top, bottom = along_head(top, 1), along_head(bottom, -1)
    terms = near_terms(place, blocks, blocks2, normed, normed2, far)
    joined = join(place, chip, steps[0], False, 1, terms)
    steps.append(send(joined, across_z(2)))
    on, back_on = pass_on(terms, up, down)
    on, back_on = send(on, along_first(1)), send(back_on, along_first(-1))
    right, left, out_own = project(place, (1, 3, 0), normed, out_weight, joined)
    joined = join(place, joined, steps[1], False, 2, right)
    steps.append(send(joined, across_y(1)))
    right, left = out_pass(right, left, top, bottom, joined)
    right, left = along_head(right, 1), along_head(left, -1)
    lower = inner(0, place, scores, qh, kh, vh, grad, mine, taken, doc, docs, joined)
    joined = join(place, joined, steps[2], False, 4, lower[0])
    steps.append(send(joined, across_y(2)))
    upper = inner(1, place, scores, qh, kh, vh, grad, mine, taken, doc, docs, joined)
    back_mine, theirs, back_doc = entry_state(place, far, steps, (1, 2, 4, 8), False, upper[0])
    back_taken = send(theirs, SWAP)
    own, *shares = middle(terms, on, back_on)
    shares = [send(share, along_second(k)) for k, share in zip((1, 2, 3), shares)]
    grad_queries, grad_keys, grad_values = last(
        place, kh, vh, lower, upper, back_mine, back_taken, back_doc, docs, own
    )
    layer_out = out_end(out_own, right, left, own)
    grad_weight = end(own, shares).T
    return layer_out, grad_queries, grad_keys, grad_values, grad_weight


def solution(mesh):
    placed = (
        P("seq", "head", None),
        P("seq", "head", None),
        P("seq", "head", None),
        P("seq"),
        P("head", None),
        P("seq", "head"),
    )
    return jax.shard_map(
        shards,
        mesh=mesh,
        in_specs=placed,
        out_specs=(
            P("seq", "head"),
            P("seq", "head", None),
            P("seq", "head", None),
            P("seq", "head", None),
            P("head", "seq"),
        ),
        check_vma=False,
    )
```

```python
import jax
import jax.numpy as jnp
from jax import lax
from jax.experimental import pallas as pl
from jax.experimental.pallas import tpu as pltpu
from jax.sharding import PartitionSpec as P

BF = jnp.bfloat16
F32 = jnp.float32
TOK, HEADS, DIM, FEAT, COLS = 512, 8, 128, 1024, 3072
HALF = HEADS // 2
ROWS = HALF * DIM
MIB = 2**20


def shape(dims, dtype):
    return jax.ShapeDtypeStruct(dims, dtype)


def whole():
    return pl.BlockSpec(memory_space=pltpu.VMEM)


def scalars():
    return pl.BlockSpec(memory_space=pltpu.SMEM)


def params(mib):
    return pltpu.CompilerParams(vmem_limit_bytes=mib * MIB)


def cost(flops, moved):
    return pl.CostEstimate(flops=flops, bytes_accessed=moved, transcendentals=0)


def dot(a, b, ca, cb):
    return lax.dot_general(a, b, (((ca,), (cb,)), ((), ())), preferred_element_type=F32)


def fixed(*dims):
    return pl.BlockSpec(dims, lambda n: (0,) * len(dims))


def in_hbm():
    return pl.BlockSpec(memory_space=pltpu.HBM)


def anywhere():
    return pl.BlockSpec(memory_space=pl.ANY)


def upright(docs_row, width):
    docs_row = docs_row.astype(F32)
    return jnp.broadcast_to(docs_row, (width, docs_row.shape[1])).T


def prepare_kernel(place, q_hbm, k_hbm, v_hbm, docs_hbm, cot_hbm, qh_ref, kh_ref, vh_ref, keep_ref, give_ref, cot_ref, q_buf, k_buf, v_buf, docs_buf, own, sems, docs_sem, cot_sem):
    steps = k_buf.shape[0]
    rows = TOK // steps

    def fetch(n, source, target, sem):
        copy = pltpu.make_async_copy(source.at[n * rows : (n + 1) * rows], target.at[n], sem)
        copy.start()
        return copy

    docs_copy = pltpu.make_async_copy(docs_hbm, docs_buf, docs_sem)
    docs_copy.start()
    copies = []
    for n in range(steps):
        copies.append(fetch(n, k_hbm, k_buf, sems.at[0, n]))
        copies.append(fetch(n, v_hbm, v_buf, sems.at[1, n]))
    q_copies = [fetch(n, q_hbm, q_buf, sems.at[2, n]) for n in range(steps)]
    cot_copy = pltpu.make_async_copy(cot_hbm, cot_ref, cot_sem)
    cot_copy.start()
    c = place[2]
    docs_copy.wait()
    docs = docs_buf[...].astype(F32)
    last = docs[:, TOK - 1 :]
    tail = (upright(docs, DIM) == last).astype(BF)
    for n in range(steps):
        span = slice(n * rows, (n + 1) * rows)
        copies[2 * n].wait()
        copies[2 * n + 1].wait()
        kh = jnp.swapaxes(k_buf[n], 0, 1)
        vh = jnp.swapaxes(v_buf[n], 0, 1)
        kh_ref[:, span] = kh
        vh_ref[:, span] = vh
        for h in range(HEADS):
            part = dot(kh[h] * tail[span], vh[h], 0, 0)
            spot = slice((h % HALF) * DIM, (h % HALF + 1) * DIM)
            if n == 0:
                own[h // HALF, spot] = part
            else:
                own[h // HALF, spot] += part
    keep_ref[:ROWS] = own[c]
    give_ref[:ROWS] = own[1 - c]
    doc_rows = jnp.broadcast_to(last, (8, DIM))
    keep_ref[ROWS:] = doc_rows
    give_ref[ROWS:] = doc_rows
    for n in range(steps):
        q_copies[n].wait()
        qh_ref[:, n * rows : (n + 1) * rows] = jnp.swapaxes(q_buf[n], 0, 1)
    cot_copy.wait()


def prepare(place, queries, keys, values, docs, cotangent):
    steps = 2
    head_major = shape((HEADS, TOK, DIM), BF)
    half = shape((ROWS + 8, DIM), F32)
    buffer = pltpu.VMEM((steps, TOK // steps, HEADS, DIM), BF)
    return pl.pallas_call(
        prepare_kernel,
        out_shape=(head_major, head_major, head_major, half, half, shape((TOK, 768), BF)),
        in_specs=[scalars()] + [in_hbm()] * 5,
        out_specs=(whole(),) * 6,
        scratch_shapes=[
            buffer,
            buffer,
            buffer,
            pltpu.VMEM((1, TOK), jnp.int32),
            pltpu.VMEM((2, ROWS, DIM), F32),
            pltpu.SemaphoreType.DMA((3, steps)),
            pltpu.SemaphoreType.DMA,
            pltpu.SemaphoreType.DMA,
        ],
        compiler_params=params(12),
        cost_estimate=cost(2 * HEADS * TOK * DIM * DIM, 6 * MIB),
        name="prepare",
    )(place, *[pltpu.with_memory_space_constraint(a, pltpu.HBM) for a in (queries, keys, values, docs, cotangent)])


def chip_kernel(forward, place, keep_ref, got_ref, *rest):
    far_ref, chip_ref = rest[-2:]
    c = place[2]
    far_is_mine = (c == 0) if forward else (c == 1)

    def write(far, near):
        same = (far[ROWS : ROWS + 1] == near[ROWS : ROWS + 1]).astype(F32)
        far_ref[...] = far[...]
        chip_ref[:ROWS] = (near[:ROWS] + same * far[:ROWS]).astype(BF)
        chip_ref[ROWS:] = jnp.broadcast_to(near[ROWS : ROWS + 1], (16, DIM)).astype(BF)

    @pl.when(far_is_mine)
    def _():
        write(keep_ref, got_ref)

    @pl.when(jnp.logical_not(far_is_mine))
    def _():
        write(got_ref, keep_ref)


def chip_state(place, keep, got, forward, *earlier):
    def kernel(*refs):
        chip_kernel(forward, *refs)

    return pl.pallas_call(
        kernel,
        out_shape=(shape((ROWS + 8, DIM), F32), shape((ROWS + 16, DIM), BF)),
        in_specs=[scalars(), whole(), whole()] + [anywhere()] * len(earlier),
        out_specs=(whole(), whole()),
        compiler_params=params(4),
        cost_estimate=cost(ROWS * DIM * 3, MIB),
        name="chip_state",
    )(place, keep, got, *earlier)


def spot_of(place, forward, step):
    chip = place[0] * 4 + place[1]
    spot = lax.rem(chip // step, 2)
    return spot if forward else 1 - spot


def join_kernel(forward, step, place, own_ref, other_ref, *rest):
    out_ref = rest[-1]
    first = spot_of(place, forward, step) == 0

    def write(early, late):
        doc = late[ROWS : ROWS + 1]
        same = (early[ROWS : ROWS + 1] == doc).astype(F32)
        total = late[:ROWS].astype(F32) + same * early[:ROWS].astype(F32)
        out_ref[:ROWS] = total.astype(BF)
        out_ref[ROWS:] = jnp.broadcast_to(doc, (16, DIM))

    @pl.when(first)
    def _():
        write(own_ref, other_ref)

    @pl.when(jnp.logical_not(first))
    def _():
        write(other_ref, own_ref)


def join(place, own, other, forward, step, *earlier):
    def kernel(*refs):
        join_kernel(forward, step, *refs)

    return pl.pallas_call(
        kernel,
        out_shape=shape((ROWS + 16, DIM), BF),
        in_specs=[scalars()] + [whole()] * 2 + [anywhere()] * len(earlier),
        out_specs=whole(),
        compiler_params=params(4),
        cost_estimate=cost(ROWS * DIM * 3, MIB),
        name="join",
    )(place, own, other, *earlier)


def entry_kernel(forward, steps, place, far_ref, *refs):
    parts, (keep_ref, give_ref, doc_ref) = refs[: len(steps)], refs[-3:]
    y, c = place[0], place[2]
    level = y if forward else 3 - y
    far_is_mine = (c == 0) if forward else (c == 1)
    inside = [spot_of(place, forward, step) == 1 if step > 0 else level >= -step for step in steps]
    docs = [p[ROWS : ROWS + 1].astype(F32) for p in parts]
    before_doc = jnp.full((1, DIM), -1.0, F32)
    for k in reversed(range(len(steps))):
        before_doc = jnp.where(inside[k], docs[k], before_doc)
    before = jnp.zeros((ROWS, DIM), F32)
    for k in range(len(steps)):
        use = jnp.where(inside[k], (docs[k] == before_doc).astype(F32), 0.0)
        before = before + use * parts[k][:ROWS].astype(F32)
    far_doc = far_ref[ROWS : ROWS + 1]
    after = far_ref[:ROWS] + (before_doc == far_doc).astype(F32) * before

    @pl.when(far_is_mine)
    def _():
        keep_ref[...] = before.astype(BF)
        give_ref[...] = after.astype(BF)
        doc_ref[...] = jnp.broadcast_to(before_doc, (8, DIM))

    @pl.when(jnp.logical_not(far_is_mine))
    def _():
        keep_ref[...] = after.astype(BF)
        give_ref[...] = before.astype(BF)
        doc_ref[...] = jnp.broadcast_to(far_doc, (8, DIM))


def entry_state(place, far, parts, steps, forward, *earlier):
    def kernel(*refs):
        entry_kernel(forward, steps, *refs)

    half = shape((ROWS, DIM), BF)
    return pl.pallas_call(
        kernel,
        out_shape=(half, half, shape((8, DIM), F32)),
        in_specs=[scalars()] + [whole()] * (1 + len(parts)) + [anywhere()] * len(earlier),
        out_specs=(whole(),) * 3,
        compiler_params=params(4),
        cost_estimate=cost(ROWS * DIM * 10, MIB),
        name="entry_state",
    )(place, far, *parts, *earlier)


def causal(docs_ref):
    row = jnp.broadcast_to(docs_ref[...].astype(F32), (TOK, TOK))
    t = lax.broadcasted_iota(jnp.int32, (TOK, TOK), 0)
    s = lax.broadcasted_iota(jnp.int32, (TOK, TOK), 1)
    same = row.T == row
    return (t >= s) & same, (s >= t) & same


def intra_kernel(q_ref, k_ref, v_ref, docs_ref, *rest):
    attn_ref, mask = rest[-2:]
    mask[...] = causal(docs_ref)[0].astype(BF)
    mid = TOK // 2
    for h in range(q_ref.shape[0]):
        for rows, width in ((slice(0, mid), mid), (slice(mid, TOK), TOK)):
            scores = dot(q_ref[h, rows], k_ref[h, :width], 1, 1).astype(BF) * mask[rows, :width]
            attn_ref[h, rows] = dot(scores, v_ref[h, :width], 1, 0)


def intra(qh, kh, vh, docs, group, *earlier):
    part = pl.BlockSpec((HALF, TOK, DIM), lambda n: (group, 0, 0))
    return pl.pallas_call(
        intra_kernel,
        grid=(1,),
        out_shape=shape((HALF, TOK, DIM), F32),
        in_specs=[part, part, part, fixed(1, TOK)] + [anywhere()] * len(earlier),
        out_specs=fixed(HALF, TOK, DIM),
        scratch_shapes=[pltpu.VMEM((TOK, TOK), BF)],
        compiler_params=params(14),
        cost_estimate=cost(2 * HEADS * TOK * TOK * DIM, 3 * MIB),
        name="intra",
    )(qh, kh, vh, docs, *earlier)


def upper_kernel(q_ref, k_ref, docs_ref, *rest):
    out_ref, mask = rest[-2:]
    mask[...] = causal(docs_ref)[1].astype(BF)
    mid = TOK // 2
    for h in range(HEADS):
        for rows, start in ((slice(0, mid), 0), (slice(mid, TOK), mid)):
            scores = dot(k_ref[h, rows], q_ref[h, start:], 1, 1)
            out_ref[h, rows, start:] = scores.astype(BF) * mask[rows, start:]


def upper_scores(qh, kh, docs, *earlier):
    return pl.pallas_call(
        upper_kernel,
        out_shape=shape((HEADS, TOK, TOK), BF),
        in_specs=[whole()] * 3 + [anywhere()] * len(earlier),
        out_specs=whole(),
        scratch_shapes=[pltpu.VMEM((TOK, TOK), BF)],
        compiler_params=params(10),
        cost_estimate=cost(2 * HEADS * TOK * TOK * DIM, 6 * MIB),
        name="upper_scores",
    )(qh, kh, docs, *earlier)


def pick_state(c, keep_ref, take_ref, h):
    rows = slice((h % HALF) * DIM, (h % HALF + 1) * DIM)
    mine = c == h // HALF
    return jnp.where(mine, keep_ref[rows], take_ref[rows])


def attend_kernel(place, q_ref, intra0, intra1, keep_ref, take_ref, doc_ref, docs_ref, *rest):
    attn_ref, normed_ref = rest[-2:]
    c = place[2]
    reads = (upright(docs_ref[...], DIM) == doc_ref[:1]).astype(F32)
    for h in range(HEADS):
        state = pick_state(c, keep_ref, take_ref, h)
        attn = (intra0, intra1)[h // HALF][h % HALF] + reads * dot(q_ref[h], state, 1, 0)
        attn_ref[h] = attn
        scale = lax.rsqrt(jnp.mean(attn * attn, axis=-1, keepdims=True) + 1e-05)
        normed_ref[:, h * DIM : (h + 1) * DIM] = (attn * scale).astype(BF)


def attend(place, qh, intra0, intra1, keep, take, doc, docs, *earlier):
    return pl.pallas_call(
        attend_kernel,
        out_shape=(shape((HEADS, TOK, DIM), F32), shape((TOK, FEAT), BF)),
        in_specs=[scalars()] + [whole()] * 7 + [anywhere()] * len(earlier),
        out_specs=(whole(), whole()),
        compiler_params=params(8),
        cost_estimate=cost(2 * HEADS * TOK * DIM * DIM, 6 * MIB),
        name="attend",
    )(place, qh, intra0, intra1, keep, take, doc, docs, *earlier)


def project_kernel(places, place, normed_ref, w_hbm, *rest):
    outs, (w_buf, sems) = rest[-3 - len(places) : -2], rest[-2:]
    x = place[3]
    copies = []
    for n, r in enumerate(places):
        spot = pl.multiple_of(lax.rem(x + r, 4) * 768, 768)
        copies.append(pltpu.make_async_copy(w_hbm.at[:, pl.ds(spot, 768)], w_buf.at[n], sems.at[n]))
        copies[n].start()
    for n, r in enumerate(places):
        copies[n].wait()
        part = jnp.dot(normed_ref[...], w_buf[n], preferred_element_type=F32)
        if r == 2:
            mid = TOK // 2
            outs[0][...] = part[:mid].astype(BF)
            outs[1][...] = part[mid:].astype(BF)
        else:
            outs[n + 1][...] = part.astype(outs[n + 1].dtype)


def project(place, places, normed, weight, *earlier):
    outs = []
    for r in places:
        if r == 2:
            outs += [shape((TOK // 2, 768), BF)] * 2
        else:
            outs.append(shape((TOK, 768), BF if r else F32))
    shift = 0 if 2 in places else 1

    def kernel(*refs):
        ahead = 3 + len(earlier)
        project_kernel(places, *refs[:ahead], *([None] * shift), *refs[ahead:])

    return pl.pallas_call(
        kernel,
        out_shape=tuple(outs),
        in_specs=[scalars(), whole(), in_hbm()] + [anywhere()] * len(earlier),
        out_specs=(whole(),) * len(outs),
        scratch_shapes=[pltpu.VMEM((len(places), FEAT, 768), BF), pltpu.SemaphoreType.DMA((len(places),))],
        compiler_params=params(4 + 3 * len(places)),
        cost_estimate=cost(TOK * FEAT * COLS * len(places) // 2, 3 * MIB * len(places)),
        name="project",
    )(place, normed, weight, *earlier)


def halves_kernel(left_ref, right_ref, *rest):
    top_ref, bottom_ref = rest[-2:]
    mid = TOK // 2
    top_ref[...] = left_ref[:mid]
    bottom_ref[...] = right_ref[mid:]


def halves(left, right, *earlier):
    out = shape((TOK // 2, 768), BF)
    return pl.pallas_call(
        halves_kernel,
        out_shape=(out, out),
        in_specs=[whole()] * 2 + [anywhere()] * len(earlier),
        out_specs=(whole(),) * 2,
        compiler_params=params(6),
        cost_estimate=cost(TOK * 768, 2 * MIB),
        name="halves",
    )(left, right, *earlier)


def out_pass_kernel(right_ref, left_ref, top_ref, bottom_ref, *rest):
    out_right, out_left = rest[-2:]
    mid = TOK // 2
    out_right[:mid] = (right_ref[:mid].astype(F32) + top_ref[...].astype(F32)).astype(BF)
    out_right[mid:] = right_ref[mid:]
    out_left[:mid] = left_ref[:mid]
    out_left[mid:] = (left_ref[mid:].astype(F32) + bottom_ref[...].astype(F32)).astype(BF)


def out_pass(right, left, top, bottom, *earlier):
    part = shape((TOK, 768), BF)
    return pl.pallas_call(
        out_pass_kernel,
        out_shape=(part, part),
        in_specs=[whole()] * 4 + [anywhere()] * len(earlier),
        out_specs=(whole(), whole()),
        compiler_params=params(6),
        cost_estimate=cost(TOK * 768, 4 * MIB),
        name="out_pass",
    )(right, left, top, bottom, *earlier)


def out_end_kernel(own_ref, left_ref, right_ref, *rest):
    total = own_ref[...] + left_ref[...].astype(F32) + right_ref[...].astype(F32)
    rest[-1][...] = total.astype(BF)


def out_end(own, from_left, from_right, *earlier):
    return pl.pallas_call(
        out_end_kernel,
        out_shape=shape((TOK, 768), BF),
        in_specs=[whole()] * 3 + [anywhere()] * len(earlier),
        out_specs=whole(),
        compiler_params=params(6),
        cost_estimate=cost(2 * TOK * 768, 4 * MIB),
        name="out_end",
    )(own, from_left, from_right, *earlier)


def turn_kernel(place, own_ref, right_ref, top_ref, bottom_ref, left_ref, *rest):
    joined_ref, keep_ref, give_ref = rest[-3:]
    c, x = place[2], place[3]
    mid = TOK // 2
    for r, ref, tokens in (
        (0, own_ref, slice(0, TOK)),
        (1, right_ref, slice(0, TOK)),
        (3, left_ref, slice(0, TOK)),
        (2, top_ref, slice(0, mid)),
        (2, bottom_ref, slice(mid, TOK)),
    ):
        block = ref[...]
        spot = pl.multiple_of(lax.rem(x + r, 4) * 768, 768)
        joined_ref[tokens, pl.ds(spot, 768)] = block
        turned = block.T.reshape(4, 2, 96, block.shape[0])
        low, high = turned[:, 0], turned[:, 1]
        keep_ref[r, :, :, tokens] = jnp.where(c == 0, low, high)
        give_ref[r, :, :, tokens] = jnp.where(c == 0, high, low)


def turn(place, own, right, top, bottom, left, *earlier):
    out = shape((4, 4, 96, TOK), BF)
    return pl.pallas_call(
        turn_kernel,
        out_shape=(shape((TOK, COLS), BF), out, out),
        in_specs=[scalars()] + [whole()] * 5 + [anywhere()] * len(earlier),
        out_specs=(whole(),) * 3,
        compiler_params=params(8),
        cost_estimate=cost(TOK * COLS, 6 * MIB),
        name="turn",
    )(place, own, right, top, bottom, left, *earlier)


def back_kernel(place, cot_ref, w_ref, attn_ref, q_ref, docs_ref, *rest):
    grad_ref, keep_ref, give_ref, own = rest[-4:]
    c = place[2]
    pairs = HEADS // 2
    docs = docs_ref[...].astype(F32)
    first = docs[:, :1]
    lead = (upright(docs, DIM) == first).astype(BF)
    for n in range(pairs):
        grad_normed = dot(cot_ref[...], w_ref[n * 2 * DIM : (n + 1) * 2 * DIM], 1, 1)
        for j in range(2):
            h = 2 * n + j
            attn = attn_ref[h]
            scale = lax.rsqrt(jnp.mean(attn * attn, axis=-1, keepdims=True) + 1e-05)
            normed = attn * scale
            grad = grad_normed[:, j * DIM : (j + 1) * DIM]
            grad = scale * (grad - normed * jnp.mean(grad * normed, axis=-1, keepdims=True))
            grad = grad.astype(BF)
            grad_ref[h] = grad
            spot = slice((h % HALF) * DIM, (h % HALF + 1) * DIM)
            own[h // HALF, spot] = dot(q_ref[h] * lead, grad, 0, 0)
    keep_ref[:ROWS] = own[c]
    give_ref[:ROWS] = own[1 - c]
    doc_rows = jnp.broadcast_to(first, (8, DIM))
    keep_ref[ROWS:] = doc_rows
    give_ref[ROWS:] = doc_rows


def back(place, cotangent, weight, attn, qh, docs, *earlier):
    half = shape((ROWS + 8, DIM), F32)
    return pl.pallas_call(
        back_kernel,
        out_shape=(shape((HEADS, TOK, DIM), BF), half, half),
        in_specs=[scalars()] + [whole()] * 5 + [anywhere()] * len(earlier),
        out_specs=(whole(),) * 3,
        scratch_shapes=[pltpu.VMEM((2, ROWS, DIM), F32)],
        compiler_params=params(8),
        cost_estimate=cost(2 * TOK * FEAT * COLS + 2 * HEADS * TOK * DIM * DIM, 15 * MIB),
        name="back",
    )(place, cotangent, weight, attn, qh, docs, *earlier)


def block_rows(place, keep_ref, got_ref, a):
    y, z, c, x = place[0], place[1], place[2], place[3]
    rows = []
    for b in range(4):
        to_y = lax.rem(y + jnp.where(c == 0, a, b), 4)
        to_z = lax.rem(z + jnp.where(c == 0, b, a), 4)
        r = lax.rem(to_y + 4 - x, 4)
        rows.append(jnp.concatenate([keep_ref[r, to_z], got_ref[r, to_z]], 1))
    return jnp.concatenate(rows, 0)


def far_terms_kernel(place, keep_ref, got_ref, normed_ref, normed2_ref, *rest):
    up_ref, down_ref = rest[-2:]
    rows = block_rows(place, keep_ref, got_ref, 2)
    total = dot(rows[:, :TOK], normed_ref[...], 1, 0) + dot(rows[:, TOK:], normed2_ref[...], 1, 0)
    up_ref[...] = total[:192].astype(BF)
    down_ref[...] = total[192:].astype(BF)


def far_terms(place, keep, got, normed, normed2, *earlier):
    out = shape((192, FEAT), BF)
    return pl.pallas_call(
        far_terms_kernel,
        out_shape=(out, out),
        in_specs=[scalars()] + [whole()] * 4 + [anywhere()] * len(earlier),
        out_specs=(whole(), whole()),
        compiler_params=params(10),
        cost_estimate=cost(TOK * FEAT * COLS // 2, 6 * MIB),
        name="far_terms",
    )(place, keep, got, normed, normed2, *earlier)


def near_terms_kernel(place, keep_ref, got_ref, normed_ref, normed2_ref, *rest):
    out_ref = rest[-1]
    for slot, a in ((0, 1), (1, 3), (2, 0)):
        rows = block_rows(place, keep_ref, got_ref, a)
        part = dot(rows[:, :TOK], normed_ref[...], 1, 0)
        out_ref[slot] = part + dot(rows[:, TOK:], normed2_ref[...], 1, 0)


def near_terms(place, keep, got, normed, normed2, *earlier):
    return pl.pallas_call(
        near_terms_kernel,
        out_shape=shape((3, 384, FEAT), F32),
        in_specs=[scalars()] + [whole()] * 4 + [anywhere()] * len(earlier),
        out_specs=whole(),
        compiler_params=params(12),
        cost_estimate=cost(3 * TOK * FEAT * COLS // 2, 10 * MIB),
        name="near_terms",
    )(place, keep, got, normed, normed2, *earlier)


def inner_kernel(group, place, scores_ref, q_ref, k_ref, v_ref, grad_ref, keep_ref, take_ref, doc_ref, docs_ref, *rest):
    gq_ref, gk_ref, gv_ref, mask, turned = rest[-5:]
    n = pl.program_id(0)

    @pl.when(n == 0)
    def _():
        before, after = causal(docs_ref)
        mask[...] = before.astype(BF)
        turned[...] = after.astype(BF)

    c = place[2]
    reads = (upright(docs_ref[...], DIM) == doc_ref[:1]).astype(F32)
    mid = TOK // 2
    for j in range(2):
        q, k, v, grad = q_ref[j], k_ref[j], v_ref[j], grad_ref[j]
        spot = pl.multiple_of((n * 2 + j) * DIM, DIM)
        state = jnp.where(c == group, keep_ref[pl.ds(spot, DIM)], take_ref[pl.ds(spot, DIM)])
        across = reads * dot(grad, state, 1, 1)
        for rows, width in ((slice(0, mid), mid), (slice(mid, TOK), TOK)):
            scores = dot(grad[rows], v[:width], 1, 1).astype(BF) * mask[rows, :width]
            gq_ref[j, rows] = (dot(scores, k[:width], 1, 0) + across[rows]).astype(BF)
        for rows, start in ((slice(0, mid), 0), (slice(mid, TOK), mid)):
            scores = dot(v[rows], grad[start:], 1, 1).astype(BF) * turned[rows, start:]
            gk_ref[j, rows] = dot(scores, q[start:], 1, 0)
            gv_ref[j, rows] = dot(scores_ref[j, rows, start:], grad[start:], 1, 0)


def inner(group, place, scores, qh, kh, vh, grad, keep, take, doc, docs, *earlier):
    def kernel(*refs):
        inner_kernel(group, *refs)

    head = pl.BlockSpec((2, TOK, DIM), lambda n: (n + group * HALF // 2, 0, 0))
    out = pl.BlockSpec((2, TOK, DIM), lambda n: (n, 0, 0))
    return pl.pallas_call(
        kernel,
        grid=(HALF // 2,),
        out_shape=(shape((HALF, TOK, DIM), BF),) + (shape((HALF, TOK, DIM), F32),) * 2,
        in_specs=[scalars(), pl.BlockSpec((2, TOK, TOK), lambda n: (n + group * HALF // 2, 0, 0))]
        + [head] * 4
        + [fixed(ROWS, DIM)] * 2
        + [fixed(8, DIM), fixed(1, TOK)]
        + [anywhere()] * len(earlier),
        out_specs=(out, out, out),
        scratch_shapes=[pltpu.VMEM((TOK, TOK), BF), pltpu.VMEM((TOK, TOK), BF)],
        compiler_params=params(14),
        cost_estimate=cost(5 * HEADS * TOK * TOK * DIM, 5 * MIB),
        name="inner",
    )(place, scores, qh, kh, vh, grad, keep, take, doc, docs, *earlier)


def last_kernel(place, k_ref, v_ref, gq0, gk0, gv0, gq1, gk1, gv1, keep_ref, take_ref, doc_ref, docs_ref, *rest):
    out_q, out_k, out_v, held_k, held_v = rest[-5:]
    c = place[2]
    writes = (upright(docs_ref[...], DIM) == doc_ref[:1]).astype(F32)
    for h in range(HEADS):
        state = pick_state(c, keep_ref, take_ref, h)
        gk, gv = ((gk0, gv0), (gk1, gv1))[h // HALF]
        held_k[h] = (gk[h % HALF] + writes * dot(v_ref[h], state, 1, 1)).astype(BF)
        held_v[h] = (gv[h % HALF] + writes * dot(k_ref[h], state, 1, 0)).astype(BF)
    out_q[...] = jnp.swapaxes(jnp.concatenate([gq0[...], gq1[...]], 0), 0, 1)
    out_k[...] = jnp.swapaxes(held_k[...], 0, 1)
    out_v[...] = jnp.swapaxes(held_v[...], 0, 1)


def last(place, kh, vh, lower, upper, keep, take, doc, docs, *earlier):
    out = shape((TOK, HEADS, DIM), BF)
    return pl.pallas_call(
        last_kernel,
        out_shape=(out, out, out),
        in_specs=[scalars()] + [whole()] * 12 + [anywhere()] * len(earlier),
        out_specs=(whole(),) * 3,
        scratch_shapes=[pltpu.VMEM((HEADS, TOK, DIM), BF)] * 2,
        compiler_params=params(12),
        cost_estimate=cost(4 * HEADS * TOK * DIM * DIM, 9 * MIB),
        name="last",
    )(place, kh, vh, *lower, *upper, keep, take, doc, docs, *earlier)


def pass_kernel(terms_ref, up_ref, down_ref, out_right, out_left):
    rows = up_ref.shape[0]
    out_right[:rows] = (terms_ref[0, :rows] + up_ref[...].astype(F32)).astype(BF)
    out_right[rows:] = terms_ref[0, rows:].astype(BF)
    out_left[:rows] = terms_ref[1, :rows].astype(BF)
    out_left[rows:] = (terms_ref[1, rows:] + down_ref[...].astype(F32)).astype(BF)


def pass_on(terms, up, down):
    out = shape((384, FEAT), BF)
    return pl.pallas_call(
        pass_kernel,
        grid=(1,),
        out_shape=(out, out),
        in_specs=[pl.BlockSpec((2, 384, FEAT), lambda n: (0, 0, 0)), fixed(192, FEAT), fixed(192, FEAT)],
        out_specs=(fixed(384, FEAT), fixed(384, FEAT)),
        compiler_params=params(16),
        cost_estimate=cost(384 * FEAT * 2, 5 * MIB),
        name="pass_on",
    )(terms, up, down)


def middle_kernel(own_ref, left_ref, right_ref, own_out, *outs):
    total = own_ref[...] + left_ref[...].astype(F32) + right_ref[...].astype(F32)
    own_out[...] = total[:96]
    for b in (1, 2, 3):
        outs[b - 1][...] = total[96 * b : 96 * (b + 1)].astype(BF)


def middle(terms, from_left, from_right):
    small = shape((96, FEAT), BF)
    return pl.pallas_call(
        middle_kernel,
        grid=(1,),
        out_shape=(shape((96, FEAT), F32), small, small, small),
        in_specs=[
            pl.BlockSpec((pl.squeezed, 384, FEAT), lambda n: (2, 0, 0)),
            fixed(384, FEAT),
            fixed(384, FEAT),
        ],
        out_specs=(fixed(96, FEAT),) * 4,
        compiler_params=params(16),
        cost_estimate=cost(384 * FEAT * 2, 4 * MIB),
        name="middle",
    )(terms, from_left, from_right)


def hold_kernel(share_ref, *rest):
    rest[-1][...] = share_ref[...]


def hold(share, *earlier):
    return pl.pallas_call(
        hold_kernel,
        out_shape=shape(share.shape, BF),
        in_specs=[whole()] + [anywhere()] * len(earlier),
        out_specs=whole(),
        compiler_params=params(4),
        cost_estimate=cost(96 * FEAT, MIB),
        name="hold",
    )(share, *earlier)


def end_kernel(own_ref, p1, p2, p3, out_ref):
    out_ref[...] = own_ref[...] + p1[...].astype(F32) + p2[...].astype(F32) + p3[...].astype(F32)


def end(own, parts):
    return pl.pallas_call(
        end_kernel,
        grid=(1,),
        out_shape=shape((96, FEAT), F32),
        in_specs=[fixed(96, FEAT)] * 4,
        out_specs=fixed(96, FEAT),
        compiler_params=params(8),
        cost_estimate=cost(96 * FEAT * 3, MIB),
        name="end",
    )(own, *parts)


def route(move):
    pairs = []
    for i in range(32):
        target = move(i // 8, (i // 2) % 4, i % 2)
        if target is not None:
            y, z, c = target
            pairs.append((i, ((y % 4) * 4 + z % 4) * 2 + c))
    return pairs


SWAP = route(lambda y, z, c: (y, z, 1 - c))


def across_z(step):
    return route(lambda y, z, c: (y, z ^ step, c))


def across_y(step):
    return route(lambda y, z, c: (y ^ step, z, c))


def along_y_open(step):
    return route(lambda y, z, c: (y + step, z, c) if 0 <= y + step < 4 else None)


def along_first(step):
    return route(lambda y, z, c: (y + step, z, c) if c == 0 else (y, z + step, c))


def along_second(step):
    return route(lambda y, z, c: (y, z + step, c) if c == 0 else (y + step, z, c))


def send(array, pairs):
    return lax.ppermute(array, "seq", pairs)


def along_head(array, step):
    return lax.ppermute(array, "head", [(i, (i + step) % 4) for i in range(4)])


def shards(queries, key_vectors, value_vectors, doc_ids, out_weight, grad_out):
    i = lax.axis_index("seq")
    place = jnp.stack([i // 8, (i // 2) % 4, i % 2, lax.axis_index("head")]).astype(jnp.int32)
    docs = doc_ids.reshape(1, TOK)
    qh, kh, vh, keep, give, cot = prepare(place, queries, key_vectors, value_vectors, docs, grad_out)
    on_left, on_right = along_head(cot, 1), along_head(cot, -1)
    far, chip = chip_state(place, keep, send(give, SWAP), True)
    beside = send(chip, across_z(1))
    intra0 = intra(qh, kh, vh, docs, 0, far)
    pair = join(place, chip, beside, True, 1, intra0)
    beyond = send(pair, across_z(2))
    scores = upper_scores(qh, kh, docs, pair)
    total = join(place, pair, beyond, True, 2, scores)
    aboves = [send(total, along_y_open(k)) for k in (1, 2)]
    intra1 = intra(qh, kh, vh, docs, 1, total)
    top, bottom = halves(on_left, on_right, intra1)
    mine, theirs, doc = entry_state(place, far, [beside, beyond] + aboves, (1, 2, -1, -2), True, top)
    far_top, far_bottom = along_head(top, 1), along_head(bottom, -1)
    taken = send(theirs, SWAP)
    attn, normed = attend(place, qh, intra0, intra1, mine, taken, doc, docs)
    normed2 = send(normed, SWAP)
    cotangent, blocks, others = turn(place, cot, on_right, far_top, far_bottom, on_left, normed)
    blocks2 = send(others, SWAP)
    grad, keep, give = back(place, cotangent, out_weight, attn, qh, docs, others)
    got = send(give, SWAP)
    far_up, far_down = far_terms(place, blocks, blocks2, normed, normed2, keep)
    up, down = send(far_up, along_first(1)), send(far_down, along_first(-1))
    far, chip = chip_state(place, keep, got, False, far_up)
    steps = [send(chip, across_z(1))]
    top, bottom = project(place, (2,), normed, out_weight, far)
    top, bottom = along_head(top, 1), along_head(bottom, -1)
    terms = near_terms(place, blocks, blocks2, normed, normed2, far)
    joined = join(place, chip, steps[0], False, 1, terms)
    steps.append(send(joined, across_z(2)))
    on, back_on = pass_on(terms, up, down)
    on, back_on = send(on, along_first(1)), send(back_on, along_first(-1))
    right, left, out_own = project(place, (1, 3, 0), normed, out_weight, joined)
    joined = join(place, joined, steps[1], False, 2, right)
    steps.append(send(joined, across_y(1)))
    right, left = out_pass(right, left, top, bottom, joined)
    right, left = along_head(right, 1), along_head(left, -1)
    lower = inner(0, place, scores, qh, kh, vh, grad, mine, taken, doc, docs, joined)
    joined = join(place, joined, steps[2], False, 4, lower[0])
    steps.append(send(joined, across_y(2)))
    upper = inner(1, place, scores, qh, kh, vh, grad, mine, taken, doc, docs, joined)
    back_mine, theirs, back_doc = entry_state(place, far, steps, (1, 2, 4, 8), False, upper[0])
    back_taken = send(theirs, SWAP)
    own, *shares = middle(terms, on, back_on)
    shares[1] = hold(shares[1], theirs)
    shares = [send(share, along_second(k)) for k, share in zip((1, 2, 3), shares)]
    grad_queries, grad_keys, grad_values = last(
        place, kh, vh, lower, upper, back_mine, back_taken, back_doc, docs, own
    )
    layer_out = out_end(out_own, right, left, own)
    grad_weight = end(own, shares).T
    return layer_out, grad_queries, grad_keys, grad_values, grad_weight


def solution(mesh):
    placed = (
        P("seq", "head", None),
        P("seq", "head", None),
        P("seq", "head", None),
        P("seq"),
        P("head", None),
        P("seq", "head"),
    )
    return jax.shard_map(
        shards,
        mesh=mesh,
        in_specs=placed,
        out_specs=(
            P("seq", "head"),
            P("seq", "head", None),
            P("seq", "head", None),
            P("seq", "head", None),
            P("head", "seq"),
        ),
        check_vma=False,
    )
```

```python
import jax
import jax.numpy as jnp
from jax import lax
from jax.experimental import pallas as pl
from jax.experimental.pallas import tpu as pltpu
from jax.sharding import PartitionSpec as P

BF = jnp.bfloat16
F32 = jnp.float32
TOK, HEADS, DIM, FEAT, COLS = 512, 8, 128, 1024, 3072
HALF = HEADS // 2
ROWS = HALF * DIM
MIB = 2**20


def shape(dims, dtype):
    return jax.ShapeDtypeStruct(dims, dtype)


def whole():
    return pl.BlockSpec(memory_space=pltpu.VMEM)


def scalars():
    return pl.BlockSpec(memory_space=pltpu.SMEM)


def params(mib):
    return pltpu.CompilerParams(vmem_limit_bytes=mib * MIB)


def cost(flops, moved):
    return pl.CostEstimate(flops=flops, bytes_accessed=moved, transcendentals=0)


def dot(a, b, ca, cb):
    return lax.dot_general(a, b, (((ca,), (cb,)), ((), ())), preferred_element_type=F32)


def fixed(*dims):
    return pl.BlockSpec(dims, lambda n: (0,) * len(dims))


def in_hbm():
    return pl.BlockSpec(memory_space=pltpu.HBM)


def anywhere():
    return pl.BlockSpec(memory_space=pl.ANY)


def upright(docs_row, width):
    docs_row = docs_row.astype(F32)
    return jnp.broadcast_to(docs_row, (width, docs_row.shape[1])).T


def prepare_kernel(place, q_hbm, k_hbm, v_hbm, docs_hbm, cot_hbm, qh_ref, kh_ref, vh_ref, keep_ref, give_ref, cot_ref, q_buf, k_buf, v_buf, docs_buf, own, sems, docs_sem, cot_sem):
    steps = k_buf.shape[0]
    rows = TOK // steps

    def fetch(n, source, target, sem):
        copy = pltpu.make_async_copy(source.at[n * rows : (n + 1) * rows], target.at[n], sem)
        copy.start()
        return copy

    docs_copy = pltpu.make_async_copy(docs_hbm, docs_buf, docs_sem)
    docs_copy.start()
    copies = []
    for n in range(steps):
        copies.append(fetch(n, k_hbm, k_buf, sems.at[0, n]))
        copies.append(fetch(n, v_hbm, v_buf, sems.at[1, n]))
    q_copies = [fetch(n, q_hbm, q_buf, sems.at[2, n]) for n in range(steps)]
    cot_copy = pltpu.make_async_copy(cot_hbm, cot_ref, cot_sem)
    cot_copy.start()
    c = place[2]
    docs_copy.wait()
    docs = docs_buf[...].astype(F32)
    last = docs[:, TOK - 1 :]
    tail = (upright(docs, DIM) == last).astype(BF)
    for n in range(steps):
        span = slice(n * rows, (n + 1) * rows)
        copies[2 * n].wait()
        copies[2 * n + 1].wait()
        kh = jnp.swapaxes(k_buf[n], 0, 1)
        vh = jnp.swapaxes(v_buf[n], 0, 1)
        kh_ref[:, span] = kh
        vh_ref[:, span] = vh
        for h in range(HEADS):
            part = dot(kh[h] * tail[span], vh[h], 0, 0)
            spot = slice((h % HALF) * DIM, (h % HALF + 1) * DIM)
            if n == 0:
                own[h // HALF, spot] = part
            else:
                own[h // HALF, spot] += part
    keep_ref[:ROWS] = own[c]
    give_ref[:ROWS] = own[1 - c]
    doc_rows = jnp.broadcast_to(last, (8, DIM))
    keep_ref[ROWS:] = doc_rows
    give_ref[ROWS:] = doc_rows
    for n in range(steps):
        q_copies[n].wait()
        qh_ref[:, n * rows : (n + 1) * rows] = jnp.swapaxes(q_buf[n], 0, 1)
    cot_copy.wait()


def prepare(place, queries, keys, values, docs, cotangent):
    steps = 2
    head_major = shape((HEADS, TOK, DIM), BF)
    half = shape((ROWS + 8, DIM), F32)
    buffer = pltpu.VMEM((steps, TOK // steps, HEADS, DIM), BF)
    return pl.pallas_call(
        prepare_kernel,
        out_shape=(head_major, head_major, head_major, half, half, shape((TOK, 768), BF)),
        in_specs=[scalars()] + [in_hbm()] * 5,
        out_specs=(whole(),) * 6,
        scratch_shapes=[
            buffer,
            buffer,
            buffer,
            pltpu.VMEM((1, TOK), jnp.int32),
            pltpu.VMEM((2, ROWS, DIM), F32),
            pltpu.SemaphoreType.DMA((3, steps)),
            pltpu.SemaphoreType.DMA,
            pltpu.SemaphoreType.DMA,
        ],
        compiler_params=params(12),
        cost_estimate=cost(2 * HEADS * TOK * DIM * DIM, 6 * MIB),
        name="prepare",
    )(place, *[pltpu.with_memory_space_constraint(a, pltpu.HBM) for a in (queries, keys, values, docs, cotangent)])


def chip_kernel(forward, place, keep_ref, got_ref, *rest):
    far_ref, chip_ref = rest[-2:]
    c = place[2]
    far_is_mine = (c == 0) if forward else (c == 1)

    def write(far, near):
        same = (far[ROWS : ROWS + 1] == near[ROWS : ROWS + 1]).astype(F32)
        far_ref[...] = far[...]
        chip_ref[:ROWS] = (near[:ROWS] + same * far[:ROWS]).astype(BF)
        chip_ref[ROWS:] = jnp.broadcast_to(near[ROWS : ROWS + 1], (16, DIM)).astype(BF)

    @pl.when(far_is_mine)
    def _():
        write(keep_ref, got_ref)

    @pl.when(jnp.logical_not(far_is_mine))
    def _():
        write(got_ref, keep_ref)


def chip_state(place, keep, got, forward, *earlier):
    def kernel(*refs):
        chip_kernel(forward, *refs)

    return pl.pallas_call(
        kernel,
        out_shape=(shape((ROWS + 8, DIM), F32), shape((ROWS + 16, DIM), BF)),
        in_specs=[scalars(), whole(), whole()] + [anywhere()] * len(earlier),
        out_specs=(whole(), whole()),
        compiler_params=params(4),
        cost_estimate=cost(ROWS * DIM * 3, MIB),
        name="chip_state",
    )(place, keep, got, *earlier)


def spot_of(place, forward, step):
    chip = place[0] * 4 + place[1]
    spot = lax.rem(chip // step, 2)
    return spot if forward else 1 - spot


def join_kernel(forward, step, place, own_ref, other_ref, *rest):
    out_ref = rest[-1]
    first = spot_of(place, forward, step) == 0

    def write(early, late):
        doc = late[ROWS : ROWS + 1]
        same = (early[ROWS : ROWS + 1] == doc).astype(F32)
        total = late[:ROWS].astype(F32) + same * early[:ROWS].astype(F32)
        out_ref[:ROWS] = total.astype(BF)
        out_ref[ROWS:] = jnp.broadcast_to(doc, (16, DIM))

    @pl.when(first)
    def _():
        write(own_ref, other_ref)

    @pl.when(jnp.logical_not(first))
    def _():
        write(other_ref, own_ref)


def join(place, own, other, forward, step, *earlier):
    def kernel(*refs):
        join_kernel(forward, step, *refs)

    return pl.pallas_call(
        kernel,
        out_shape=shape((ROWS + 16, DIM), BF),
        in_specs=[scalars()] + [whole()] * 2 + [anywhere()] * len(earlier),
        out_specs=whole(),
        compiler_params=params(4),
        cost_estimate=cost(ROWS * DIM * 3, MIB),
        name="join",
    )(place, own, other, *earlier)


def entry_kernel(forward, steps, place, far_ref, *refs):
    parts, (keep_ref, give_ref, doc_ref) = refs[: len(steps)], refs[-3:]
    y, c = place[0], place[2]
    level = y if forward else 3 - y
    far_is_mine = (c == 0) if forward else (c == 1)
    inside = [spot_of(place, forward, step) == 1 if step > 0 else level >= -step for step in steps]
    docs = [p[ROWS : ROWS + 1].astype(F32) for p in parts]
    before_doc = jnp.full((1, DIM), -1.0, F32)
    for k in reversed(range(len(steps))):
        before_doc = jnp.where(inside[k], docs[k], before_doc)
    before = jnp.zeros((ROWS, DIM), F32)
    for k in range(len(steps)):
        use = jnp.where(inside[k], (docs[k] == before_doc).astype(F32), 0.0)
        before = before + use * parts[k][:ROWS].astype(F32)
    far_doc = far_ref[ROWS : ROWS + 1]
    after = far_ref[:ROWS] + (before_doc == far_doc).astype(F32) * before

    @pl.when(far_is_mine)
    def _():
        keep_ref[...] = before.astype(BF)
        give_ref[...] = after.astype(BF)
        doc_ref[...] = jnp.broadcast_to(before_doc, (8, DIM))

    @pl.when(jnp.logical_not(far_is_mine))
    def _():
        keep_ref[...] = after.astype(BF)
        give_ref[...] = before.astype(BF)
        doc_ref[...] = jnp.broadcast_to(far_doc, (8, DIM))


def entry_state(place, far, parts, steps, forward, *earlier):
    def kernel(*refs):
        entry_kernel(forward, steps, *refs)

    half = shape((ROWS, DIM), BF)
    return pl.pallas_call(
        kernel,
        out_shape=(half, half, shape((8, DIM), F32)),
        in_specs=[scalars()] + [whole()] * (1 + len(parts)) + [anywhere()] * len(earlier),
        out_specs=(whole(),) * 3,
        compiler_params=params(4),
        cost_estimate=cost(ROWS * DIM * 10, MIB),
        name="entry_state",
    )(place, far, *parts, *earlier)


def causal(docs_ref):
    row = jnp.broadcast_to(docs_ref[...].astype(F32), (TOK, TOK))
    t = lax.broadcasted_iota(jnp.int32, (TOK, TOK), 0)
    s = lax.broadcasted_iota(jnp.int32, (TOK, TOK), 1)
    same = row.T == row
    return (t >= s) & same, (s >= t) & same


def intra_kernel(q_ref, k_ref, v_ref, docs_ref, *rest):
    attn_ref, mask = rest[-2:]
    mask[...] = causal(docs_ref)[0].astype(BF)
    mid = TOK // 2
    for h in range(q_ref.shape[0]):
        for rows, width in ((slice(0, mid), mid), (slice(mid, TOK), TOK)):
            scores = dot(q_ref[h, rows], k_ref[h, :width], 1, 1).astype(BF) * mask[rows, :width]
            attn_ref[h, rows] = dot(scores, v_ref[h, :width], 1, 0)


def intra(qh, kh, vh, docs, group, *earlier):
    part = pl.BlockSpec((HALF, TOK, DIM), lambda n: (group, 0, 0))
    return pl.pallas_call(
        intra_kernel,
        grid=(1,),
        out_shape=shape((HALF, TOK, DIM), F32),
        in_specs=[part, part, part, fixed(1, TOK)] + [anywhere()] * len(earlier),
        out_specs=fixed(HALF, TOK, DIM),
        scratch_shapes=[pltpu.VMEM((TOK, TOK), BF)],
        compiler_params=params(14),
        cost_estimate=cost(2 * HEADS * TOK * TOK * DIM, 3 * MIB),
        name="intra",
    )(qh, kh, vh, docs, *earlier)


def upper_kernel(q_ref, k_ref, docs_ref, *rest):
    out_ref, mask = rest[-2:]
    mask[...] = causal(docs_ref)[1].astype(BF)
    mid = TOK // 2
    for h in range(HEADS):
        for rows, start in ((slice(0, mid), 0), (slice(mid, TOK), mid)):
            scores = dot(k_ref[h, rows], q_ref[h, start:], 1, 1)
            out_ref[h, rows, start:] = scores.astype(BF) * mask[rows, start:]


def upper_scores(qh, kh, docs, *earlier):
    return pl.pallas_call(
        upper_kernel,
        out_shape=shape((HEADS, TOK, TOK), BF),
        in_specs=[whole()] * 3 + [anywhere()] * len(earlier),
        out_specs=whole(),
        scratch_shapes=[pltpu.VMEM((TOK, TOK), BF)],
        compiler_params=params(10),
        cost_estimate=cost(2 * HEADS * TOK * TOK * DIM, 6 * MIB),
        name="upper_scores",
    )(qh, kh, docs, *earlier)


def pick_state(c, keep_ref, take_ref, h):
    rows = slice((h % HALF) * DIM, (h % HALF + 1) * DIM)
    mine = c == h // HALF
    return jnp.where(mine, keep_ref[rows], take_ref[rows])


def attend_kernel(place, q_ref, intra0, intra1, keep_ref, take_ref, doc_ref, docs_ref, *rest):
    attn_ref, normed_ref = rest[-2:]
    c = place[2]
    reads = (upright(docs_ref[...], DIM) == doc_ref[:1]).astype(F32)
    for h in range(HEADS):
        state = pick_state(c, keep_ref, take_ref, h)
        attn = (intra0, intra1)[h // HALF][h % HALF] + reads * dot(q_ref[h], state, 1, 0)
        attn_ref[h] = attn
        scale = lax.rsqrt(jnp.mean(attn * attn, axis=-1, keepdims=True) + 1e-05)
        normed_ref[:, h * DIM : (h + 1) * DIM] = (attn * scale).astype(BF)


def attend(place, qh, intra0, intra1, keep, take, doc, docs, *earlier):
    return pl.pallas_call(
        attend_kernel,
        out_shape=(shape((HEADS, TOK, DIM), F32), shape((TOK, FEAT), BF)),
        in_specs=[scalars()] + [whole()] * 7 + [anywhere()] * len(earlier),
        out_specs=(whole(), whole()),
        compiler_params=params(8),
        cost_estimate=cost(2 * HEADS * TOK * DIM * DIM, 6 * MIB),
        name="attend",
    )(place, qh, intra0, intra1, keep, take, doc, docs, *earlier)


def project_kernel(places, place, normed_ref, w_hbm, *rest):
    outs, (w_buf, sems) = rest[-3 - len(places) : -2], rest[-2:]
    x = place[3]
    copies = []
    for n, r in enumerate(places):
        spot = pl.multiple_of(lax.rem(x + r, 4) * 768, 768)
        copies.append(pltpu.make_async_copy(w_hbm.at[:, pl.ds(spot, 768)], w_buf.at[n], sems.at[n]))
        copies[n].start()
    for n, r in enumerate(places):
        copies[n].wait()
        part = jnp.dot(normed_ref[...], w_buf[n], preferred_element_type=F32)
        if r == 2:
            mid = TOK // 2
            outs[0][...] = part[:mid].astype(BF)
            outs[1][...] = part[mid:].astype(BF)
        else:
            outs[n + 1][...] = part.astype(outs[n + 1].dtype)


def project(place, places, normed, weight, *earlier):
    outs = []
    for r in places:
        if r == 2:
            outs += [shape((TOK // 2, 768), BF)] * 2
        else:
            outs.append(shape((TOK, 768), BF if r else F32))
    shift = 0 if 2 in places else 1

    def kernel(*refs):
        ahead = 3 + len(earlier)
        project_kernel(places, *refs[:ahead], *([None] * shift), *refs[ahead:])

    return pl.pallas_call(
        kernel,
        out_shape=tuple(outs),
        in_specs=[scalars(), whole(), in_hbm()] + [anywhere()] * len(earlier),
        out_specs=(whole(),) * len(outs),
        scratch_shapes=[pltpu.VMEM((len(places), FEAT, 768), BF), pltpu.SemaphoreType.DMA((len(places),))],
        compiler_params=params(4 + 3 * len(places)),
        cost_estimate=cost(TOK * FEAT * COLS * len(places) // 2, 3 * MIB * len(places)),
        name="project",
    )(place, normed, weight, *earlier)


def halves_kernel(left_ref, right_ref, *rest):
    top_ref, bottom_ref = rest[-2:]
    mid = TOK // 2
    top_ref[...] = left_ref[:mid]
    bottom_ref[...] = right_ref[mid:]


def halves(left, right, *earlier):
    out = shape((TOK // 2, 768), BF)
    return pl.pallas_call(
        halves_kernel,
        out_shape=(out, out),
        in_specs=[whole()] * 2 + [anywhere()] * len(earlier),
        out_specs=(whole(),) * 2,
        compiler_params=params(6),
        cost_estimate=cost(TOK * 768, 2 * MIB),
        name="halves",
    )(left, right, *earlier)


def out_pass_kernel(right_ref, left_ref, top_ref, bottom_ref, *rest):
    out_right, out_left = rest[-2:]
    mid = TOK // 2
    out_right[:mid] = (right_ref[:mid].astype(F32) + top_ref[...].astype(F32)).astype(BF)
    out_right[mid:] = right_ref[mid:]
    out_left[:mid] = left_ref[:mid]
    out_left[mid:] = (left_ref[mid:].astype(F32) + bottom_ref[...].astype(F32)).astype(BF)


def out_pass(right, left, top, bottom, *earlier):
    part = shape((TOK, 768), BF)
    return pl.pallas_call(
        out_pass_kernel,
        out_shape=(part, part),
        in_specs=[whole()] * 4 + [anywhere()] * len(earlier),
        out_specs=(whole(), whole()),
        compiler_params=params(6),
        cost_estimate=cost(TOK * 768, 4 * MIB),
        name="out_pass",
    )(right, left, top, bottom, *earlier)


def out_end_kernel(own_ref, left_ref, right_ref, *rest):
    total = own_ref[...] + left_ref[...].astype(F32) + right_ref[...].astype(F32)
    rest[-1][...] = total.astype(BF)


def out_end(own, from_left, from_right, *earlier):
    return pl.pallas_call(
        out_end_kernel,
        out_shape=shape((TOK, 768), BF),
        in_specs=[whole()] * 3 + [anywhere()] * len(earlier),
        out_specs=whole(),
        compiler_params=params(6),
        cost_estimate=cost(2 * TOK * 768, 4 * MIB),
        name="out_end",
    )(own, from_left, from_right, *earlier)


def turn_kernel(place, own_ref, right_ref, top_ref, bottom_ref, left_ref, *rest):
    joined_ref, keep_ref, give_ref = rest[-3:]
    c, x = place[2], place[3]
    mid = TOK // 2
    for r, ref, tokens in (
        (0, own_ref, slice(0, TOK)),
        (1, right_ref, slice(0, TOK)),
        (3, left_ref, slice(0, TOK)),
        (2, top_ref, slice(0, mid)),
        (2, bottom_ref, slice(mid, TOK)),
    ):
        block = ref[...]
        spot = pl.multiple_of(lax.rem(x + r, 4) * 768, 768)
        joined_ref[tokens, pl.ds(spot, 768)] = block
        turned = block.T.reshape(4, 2, 96, block.shape[0])
        low, high = turned[:, 0], turned[:, 1]
        keep_ref[r, :, :, tokens] = jnp.where(c == 0, low, high)
        give_ref[r, :, :, tokens] = jnp.where(c == 0, high, low)


def turn(place, own, right, top, bottom, left, *earlier):
    out = shape((4, 4, 96, TOK), BF)
    return pl.pallas_call(
        turn_kernel,
        out_shape=(shape((TOK, COLS), BF), out, out),
        in_specs=[scalars()] + [whole()] * 5 + [anywhere()] * len(earlier),
        out_specs=(whole(),) * 3,
        compiler_params=params(8),
        cost_estimate=cost(TOK * COLS, 6 * MIB),
        name="turn",
    )(place, own, right, top, bottom, left, *earlier)


def back_kernel(place, cot_ref, w_ref, attn_ref, q_ref, docs_ref, *rest):
    grad_ref, keep_ref, give_ref, own = rest[-4:]
    c = place[2]
    pairs = HEADS // 2
    docs = docs_ref[...].astype(F32)
    first = docs[:, :1]
    lead = (upright(docs, DIM) == first).astype(BF)
    for n in range(pairs):
        grad_normed = dot(cot_ref[...], w_ref[n * 2 * DIM : (n + 1) * 2 * DIM], 1, 1)
        for j in range(2):
            h = 2 * n + j
            attn = attn_ref[h]
            scale = lax.rsqrt(jnp.mean(attn * attn, axis=-1, keepdims=True) + 1e-05)
            normed = attn * scale
            grad = grad_normed[:, j * DIM : (j + 1) * DIM]
            grad = scale * (grad - normed * jnp.mean(grad * normed, axis=-1, keepdims=True))
            grad = grad.astype(BF)
            grad_ref[h] = grad
            spot = slice((h % HALF) * DIM, (h % HALF + 1) * DIM)
            own[h // HALF, spot] = dot(q_ref[h] * lead, grad, 0, 0)
    keep_ref[:ROWS] = own[c]
    give_ref[:ROWS] = own[1 - c]
    doc_rows = jnp.broadcast_to(first, (8, DIM))
    keep_ref[ROWS:] = doc_rows
    give_ref[ROWS:] = doc_rows


def back(place, cotangent, weight, attn, qh, docs, *earlier):
    half = shape((ROWS + 8, DIM), F32)
    return pl.pallas_call(
        back_kernel,
        out_shape=(shape((HEADS, TOK, DIM), BF), half, half),
        in_specs=[scalars()] + [whole()] * 5 + [anywhere()] * len(earlier),
        out_specs=(whole(),) * 3,
        scratch_shapes=[pltpu.VMEM((2, ROWS, DIM), F32)],
        compiler_params=params(8),
        cost_estimate=cost(2 * TOK * FEAT * COLS + 2 * HEADS * TOK * DIM * DIM, 15 * MIB),
        name="back",
    )(place, cotangent, weight, attn, qh, docs, *earlier)


def block_rows(place, keep_ref, got_ref, a):
    y, z, c, x = place[0], place[1], place[2], place[3]
    rows = []
    for b in range(4):
        to_y = lax.rem(y + jnp.where(c == 0, a, b), 4)
        to_z = lax.rem(z + jnp.where(c == 0, b, a), 4)
        r = lax.rem(to_y + 4 - x, 4)
        rows.append(jnp.concatenate([keep_ref[r, to_z], got_ref[r, to_z]], 1))
    return jnp.concatenate(rows, 0)


def far_terms_kernel(place, keep_ref, got_ref, normed_ref, normed2_ref, *rest):
    up_ref, down_ref = rest[-2:]
    rows = block_rows(place, keep_ref, got_ref, 2)
    total = dot(rows[:, :TOK], normed_ref[...], 1, 0) + dot(rows[:, TOK:], normed2_ref[...], 1, 0)
    up_ref[...] = total[:192].astype(BF)
    down_ref[...] = total[192:].astype(BF)


def far_terms(place, keep, got, normed, normed2, *earlier):
    out = shape((192, FEAT), BF)
    return pl.pallas_call(
        far_terms_kernel,
        out_shape=(out, out),
        in_specs=[scalars()] + [whole()] * 4 + [anywhere()] * len(earlier),
        out_specs=(whole(), whole()),
        compiler_params=params(10),
        cost_estimate=cost(TOK * FEAT * COLS // 2, 6 * MIB),
        name="far_terms",
    )(place, keep, got, normed, normed2, *earlier)


def near_terms_kernel(place, keep_ref, got_ref, normed_ref, normed2_ref, *rest):
    out_ref = rest[-1]
    for slot, a in ((0, 1), (1, 3), (2, 0)):
        rows = block_rows(place, keep_ref, got_ref, a)
        part = dot(rows[:, :TOK], normed_ref[...], 1, 0)
        out_ref[slot] = part + dot(rows[:, TOK:], normed2_ref[...], 1, 0)


def near_terms(place, keep, got, normed, normed2, *earlier):
    return pl.pallas_call(
        near_terms_kernel,
        out_shape=shape((3, 384, FEAT), F32),
        in_specs=[scalars()] + [whole()] * 4 + [anywhere()] * len(earlier),
        out_specs=whole(),
        compiler_params=params(12),
        cost_estimate=cost(3 * TOK * FEAT * COLS // 2, 10 * MIB),
        name="near_terms",
    )(place, keep, got, normed, normed2, *earlier)


def inner_kernel(group, place, scores_ref, q_ref, k_ref, v_ref, grad_ref, keep_ref, take_ref, doc_ref, docs_ref, *rest):
    gq_ref, gk_ref, gv_ref, mask, turned = rest[-5:]
    n = pl.program_id(0)

    @pl.when(n == 0)
    def _():
        before, after = causal(docs_ref)
        mask[...] = before.astype(BF)
        turned[...] = after.astype(BF)

    c = place[2]
    reads = (upright(docs_ref[...], DIM) == doc_ref[:1]).astype(F32)
    mid = TOK // 2
    for j in range(2):
        q, k, v, grad = q_ref[j], k_ref[j], v_ref[j], grad_ref[j]
        spot = pl.multiple_of((n * 2 + j) * DIM, DIM)
        state = jnp.where(c == group, keep_ref[pl.ds(spot, DIM)], take_ref[pl.ds(spot, DIM)])
        across = reads * dot(grad, state, 1, 1)
        for rows, width in ((slice(0, mid), mid), (slice(mid, TOK), TOK)):
            scores = dot(grad[rows], v[:width], 1, 1).astype(BF) * mask[rows, :width]
            gq_ref[j, rows] = (dot(scores, k[:width], 1, 0) + across[rows]).astype(BF)
        for rows, start in ((slice(0, mid), 0), (slice(mid, TOK), mid)):
            scores = dot(v[rows], grad[start:], 1, 1).astype(BF) * turned[rows, start:]
            gk_ref[j, rows] = dot(scores, q[start:], 1, 0)
            gv_ref[j, rows] = dot(scores_ref[j, rows, start:], grad[start:], 1, 0)


def inner(group, place, scores, qh, kh, vh, grad, keep, take, doc, docs, *earlier):
    def kernel(*refs):
        inner_kernel(group, *refs)

    head = pl.BlockSpec((2, TOK, DIM), lambda n: (n + group * HALF // 2, 0, 0))
    out = pl.BlockSpec((2, TOK, DIM), lambda n: (n, 0, 0))
    return pl.pallas_call(
        kernel,
        grid=(HALF // 2,),
        out_shape=(shape((HALF, TOK, DIM), BF),) + (shape((HALF, TOK, DIM), F32),) * 2,
        in_specs=[scalars(), pl.BlockSpec((2, TOK, TOK), lambda n: (n + group * HALF // 2, 0, 0))]
        + [head] * 4
        + [fixed(ROWS, DIM)] * 2
        + [fixed(8, DIM), fixed(1, TOK)]
        + [anywhere()] * len(earlier),
        out_specs=(out, out, out),
        scratch_shapes=[pltpu.VMEM((TOK, TOK), BF), pltpu.VMEM((TOK, TOK), BF)],
        compiler_params=params(14),
        cost_estimate=cost(5 * HEADS * TOK * TOK * DIM, 5 * MIB),
        name="inner",
    )(place, scores, qh, kh, vh, grad, keep, take, doc, docs, *earlier)


def queries_kernel(low_ref, high_ref, *rest):
    rest[-1][...] = jnp.swapaxes(jnp.concatenate([low_ref[...], high_ref[...]], 0), 0, 1)


def queries_out(low, high, *earlier):
    return pl.pallas_call(
        queries_kernel,
        out_shape=shape((TOK, HEADS, DIM), BF),
        in_specs=[whole()] * 2 + [anywhere()] * len(earlier),
        out_specs=whole(),
        compiler_params=params(8),
        cost_estimate=cost(TOK * FEAT, 2 * MIB),
        name="queries_out",
    )(low, high, *earlier)


def last_kernel(place, k_ref, v_ref, gk0, gv0, gk1, gv1, keep_ref, take_ref, doc_ref, docs_ref, *rest):
    out_k, out_v, held_k, held_v = rest[-4:]
    c = place[2]
    writes = (upright(docs_ref[...], DIM) == doc_ref[:1]).astype(F32)
    for h in range(HEADS):
        state = pick_state(c, keep_ref, take_ref, h)
        gk, gv = ((gk0, gv0), (gk1, gv1))[h // HALF]
        held_k[h] = (gk[h % HALF] + writes * dot(v_ref[h], state, 1, 1)).astype(BF)
        held_v[h] = (gv[h % HALF] + writes * dot(k_ref[h], state, 1, 0)).astype(BF)
    out_k[...] = jnp.swapaxes(held_k[...], 0, 1)
    out_v[...] = jnp.swapaxes(held_v[...], 0, 1)


def last(place, kh, vh, lower, upper, keep, take, doc, docs, *earlier):
    out = shape((TOK, HEADS, DIM), BF)
    return pl.pallas_call(
        last_kernel,
        out_shape=(out, out),
        in_specs=[scalars()] + [whole()] * 10 + [anywhere()] * len(earlier),
        out_specs=(whole(),) * 2,
        scratch_shapes=[pltpu.VMEM((HEADS, TOK, DIM), BF)] * 2,
        compiler_params=params(12),
        cost_estimate=cost(4 * HEADS * TOK * DIM * DIM, 9 * MIB),
        name="last",
    )(place, kh, vh, *lower[1:], *upper[1:], keep, take, doc, docs, *earlier)


def pass_kernel(terms_ref, up_ref, down_ref, out_right, out_left):
    rows = up_ref.shape[0]
    out_right[:rows] = (terms_ref[0, :rows] + up_ref[...].astype(F32)).astype(BF)
    out_right[rows:] = terms_ref[0, rows:].astype(BF)
    out_left[:rows] = terms_ref[1, :rows].astype(BF)
    out_left[rows:] = (terms_ref[1, rows:] + down_ref[...].astype(F32)).astype(BF)


def pass_on(terms, up, down):
    out = shape((384, FEAT), BF)
    return pl.pallas_call(
        pass_kernel,
        grid=(1,),
        out_shape=(out, out),
        in_specs=[pl.BlockSpec((2, 384, FEAT), lambda n: (0, 0, 0)), fixed(192, FEAT), fixed(192, FEAT)],
        out_specs=(fixed(384, FEAT), fixed(384, FEAT)),
        compiler_params=params(16),
        cost_estimate=cost(384 * FEAT * 2, 5 * MIB),
        name="pass_on",
    )(terms, up, down)


def middle_kernel(own_ref, left_ref, right_ref, own_out, *outs):
    total = own_ref[...] + left_ref[...].astype(F32) + right_ref[...].astype(F32)
    own_out[...] = total[:96]
    for b in (1, 2, 3):
        outs[b - 1][...] = total[96 * b : 96 * (b + 1)].astype(BF)


def middle(terms, from_left, from_right):
    small = shape((96, FEAT), BF)
    return pl.pallas_call(
        middle_kernel,
        grid=(1,),
        out_shape=(shape((96, FEAT), F32), small, small, small),
        in_specs=[
            pl.BlockSpec((pl.squeezed, 384, FEAT), lambda n: (2, 0, 0)),
            fixed(384, FEAT),
            fixed(384, FEAT),
        ],
        out_specs=(fixed(96, FEAT),) * 4,
        compiler_params=params(16),
        cost_estimate=cost(384 * FEAT * 2, 4 * MIB),
        name="middle",
    )(terms, from_left, from_right)


def hold_kernel(share_ref, *rest):
    rest[-1][...] = share_ref[...]


def hold(share, *earlier):
    return pl.pallas_call(
        hold_kernel,
        out_shape=shape(share.shape, BF),
        in_specs=[whole()] + [anywhere()] * len(earlier),
        out_specs=whole(),
        compiler_params=params(4),
        cost_estimate=cost(96 * FEAT, MIB),
        name="hold",
    )(share, *earlier)


def end_kernel(own_ref, p1, p2, p3, out_ref):
    out_ref[...] = own_ref[...] + p1[...].astype(F32) + p2[...].astype(F32) + p3[...].astype(F32)


def end(own, parts):
    return pl.pallas_call(
        end_kernel,
        grid=(1,),
        out_shape=shape((96, FEAT), F32),
        in_specs=[fixed(96, FEAT)] * 4,
        out_specs=fixed(96, FEAT),
        compiler_params=params(8),
        cost_estimate=cost(96 * FEAT * 3, MIB),
        name="end",
    )(own, *parts)


def route(move):
    pairs = []
    for i in range(32):
        target = move(i // 8, (i // 2) % 4, i % 2)
        if target is not None:
            y, z, c = target
            pairs.append((i, ((y % 4) * 4 + z % 4) * 2 + c))
    return pairs


SWAP = route(lambda y, z, c: (y, z, 1 - c))


def across_z(step):
    return route(lambda y, z, c: (y, z ^ step, c))


def across_y(step):
    return route(lambda y, z, c: (y ^ step, z, c))


def along_y_open(step):
    return route(lambda y, z, c: (y + step, z, c) if 0 <= y + step < 4 else None)


def along_first(step):
    return route(lambda y, z, c: (y + step, z, c) if c == 0 else (y, z + step, c))


def along_second(step):
    return route(lambda y, z, c: (y, z + step, c) if c == 0 else (y + step, z, c))


def send(array, pairs):
    return lax.ppermute(array, "seq", pairs)


def along_head(array, step):
    return lax.ppermute(array, "head", [(i, (i + step) % 4) for i in range(4)])


def shards(queries, key_vectors, value_vectors, doc_ids, out_weight, grad_out):
    i = lax.axis_index("seq")
    place = jnp.stack([i // 8, (i // 2) % 4, i % 2, lax.axis_index("head")]).astype(jnp.int32)
    docs = doc_ids.reshape(1, TOK)
    qh, kh, vh, keep, give, cot = prepare(place, queries, key_vectors, value_vectors, docs, grad_out)
    on_left, on_right = along_head(cot, 1), along_head(cot, -1)
    far, chip = chip_state(place, keep, send(give, SWAP), True)
    beside = send(chip, across_z(1))
    intra0 = intra(qh, kh, vh, docs, 0, far)
    pair = join(place, chip, beside, True, 1, intra0)
    beyond = send(pair, across_z(2))
    scores = upper_scores(qh, kh, docs, pair)
    total = join(place, pair, beyond, True, 2, scores)
    aboves = [send(total, along_y_open(k)) for k in (1, 2)]
    intra1 = intra(qh, kh, vh, docs, 1, total)
    top, bottom = halves(on_left, on_right, intra1)
    mine, theirs, doc = entry_state(place, far, [beside, beyond] + aboves, (1, 2, -1, -2), True, top)
    far_top, far_bottom = along_head(top, 1), along_head(bottom, -1)
    taken = send(theirs, SWAP)
    attn, normed = attend(place, qh, intra0, intra1, mine, taken, doc, docs)
    normed2 = send(normed, SWAP)
    cotangent, blocks, others = turn(place, cot, on_right, far_top, far_bottom, on_left, normed)
    blocks2 = send(others, SWAP)
    grad, keep, give = back(place, cotangent, out_weight, attn, qh, docs, others)
    got = send(give, SWAP)
    far_up, far_down = far_terms(place, blocks, blocks2, normed, normed2, keep)
    up, down = send(far_up, along_first(1)), send(far_down, along_first(-1))
    far, chip = chip_state(place, keep, got, False, far_up)
    steps = [send(chip, across_z(1))]
    top, bottom = project(place, (2,), normed, out_weight, far)
    top, bottom = along_head(top, 1), along_head(bottom, -1)
    terms = near_terms(place, blocks, blocks2, normed, normed2, far)
    joined = join(place, chip, steps[0], False, 1, terms)
    steps.append(send(joined, across_z(2)))
    on, back_on = pass_on(terms, up, down)
    on, back_on = send(on, along_first(1)), send(back_on, along_first(-1))
    right, left, out_own = project(place, (1, 3, 0), normed, out_weight, joined)
    joined = join(place, joined, steps[1], False, 2, right)
    steps.append(send(joined, across_y(1)))
    right, left = out_pass(right, left, top, bottom, joined)
    right, left = along_head(right, 1), along_head(left, -1)
    lower = inner(0, place, scores, qh, kh, vh, grad, mine, taken, doc, docs, joined)
    joined = join(place, joined, steps[2], False, 4, lower[0])
    steps.append(send(joined, across_y(2)))
    upper = inner(1, place, scores, qh, kh, vh, grad, mine, taken, doc, docs, joined)
    back_mine, theirs, back_doc = entry_state(place, far, steps, (1, 2, 4, 8), False, upper[0])
    back_taken = send(theirs, SWAP)
    own, *shares = middle(terms, on, back_on)
    shares[1] = hold(shares[1], theirs)
    shares = [send(share, along_second(k)) for k, share in zip((1, 2, 3), shares)]
    grad_queries = queries_out(lower[0], upper[0], theirs)
    grad_keys, grad_values = last(
        place, kh, vh, lower, upper, back_mine, back_taken, back_doc, docs, own
    )
    layer_out = out_end(out_own, right, left, own)
    grad_weight = end(own, shares).T
    return layer_out, grad_queries, grad_keys, grad_values, grad_weight


def solution(mesh):
    placed = (
        P("seq", "head", None),
        P("seq", "head", None),
        P("seq", "head", None),
        P("seq"),
        P("head", None),
        P("seq", "head"),
    )
    return jax.shard_map(
        shards,
        mesh=mesh,
        in_specs=placed,
        out_specs=(
            P("seq", "head"),
            P("seq", "head", None),
            P("seq", "head", None),
            P("seq", "head", None),
            P("head", "seq"),
        ),
        check_vma=False,
    )
```
